32 devices in a mesh: dp: 16 (over z, x, core), tensor: 2 (over y).
Axes of the slice: x: 2, y: 2, z: 4, core: 2. Of those that a mesh axis runs over, the one named last changes fastest.
Arguments:
- tokens: bfloat16 [16384, 768], P(('dp', 'tensor')), may hold values from -6 to 6
- segment_ids: int32 [16, 1024], P('dp'), may hold values from 0 to 4, as said below
- pad_mask: int32 [16, 1024], P('dp'), may hold values from 0 to 1, as said below
- norm1_gain: float32 [768], replicated, may hold values from 0.5 to 1.5
- norm1_shift: float32 [768], replicated, may hold values from -1 to 1
- w_query: bfloat16 [768, 768], P(None, 'tensor'), may hold values from -2 to 2
- w_key: bfloat16 [768, 768], P(None, 'tensor'), may hold values from -2 to 2
- w_value: bfloat16 [768, 768], P(None, 'tensor'), may hold values from -0.21875 to 0.21875
- w_out: bfloat16 [768, 768], P('tensor'), may hold values from -0.4375 to 0.4375
- norm2_gain: float32 [768], replicated, may hold values from 0.5 to 1.5
- norm2_shift: float32 [768], replicated, may hold values from -1 to 1
- w_up: bfloat16 [768, 3072], P(None, 'tensor'), may hold values from -0.21875 to 0.21875
- w_down: bfloat16 [3072, 768], P('tensor'), may hold values from -0.109375 to 0.109375
- cotangent: bfloat16 [16384, 768], P(('dp', 'tensor')), may hold values from -6 to 6
Outputs:
- mixed: bfloat16 [16384, 768], P(('dp', 'tensor'))
- tokens_grad: bfloat16 [16384, 768], P(('dp', 'tensor'))
- norm1_gain_grad: float32 [768], replicated
- norm1_shift_grad: float32 [768], replicated
- w_query_grad: float32 [768, 768], P(None, 'tensor')
- w_key_grad: float32 [768, 768], P(None, 'tensor')
- w_value_grad: float32 [768, 768], P(None, 'tensor')
- w_out_grad: float32 [768, 768], P('tensor')
- norm2_gain_grad: float32 [768], replicated
- norm2_shift_grad: float32 [768], replicated
- w_up_grad: float32 [768, 3072], P(None, 'tensor')
- w_down_grad: float32 [3072, 768], P('tensor')
The draws below stay inside these ranges and needn't reach their ends.
Inputs may be any that keep to these rules, and one draw needn't show every extreme that they name: `segment_ids`: in each row the numbers never fall from one position to the next, and positions 256 to 767 lie in one document. `pad_mask`: in each row the pad slots form one nonempty run at the end, inside the row's last document.
All inputs are finite; a program needn't handle non-finite values.
Results may differ from the reference program's by a relative error of at most 0.014.
Values may be sent and summed in bfloat16 or wider, within the bound.
No kernel may reach another device: no remote copies, remote signals or barrier semaphores. Data moves between devices by JAX's collectives and lax.ppermute only.
A program may use at most 192 MiB of HBM per device.

```python
import math
import jax
import jax.numpy as jnp
from jax import lax

D = 768
HEADS = 12
HEAD_DIM = 64
FF = 3072
SEQ = 1024
ROWS = 16
TOKENS = 16384


def row_bounds(key):
    keys_list = jax.random.split(key, 5)
    cut_one = jax.random.randint(keys_list[0], (ROWS,), 2, SEQ // 4)
    cut_zero = jax.random.randint(keys_list[1], (ROWS,), 1, cut_one)
    cut_two = jax.random.randint(keys_list[2], (ROWS,), 3 * SEQ // 4, SEQ - 1)
    cut_three = jax.random.randint(keys_list[3], (ROWS,), cut_two + 1, SEQ)
    pad_start = jax.random.randint(keys_list[4], (ROWS,), cut_three, SEQ)
    return (cut_zero, cut_one, cut_two, cut_three, pad_start)


def draw_segment_ids(key, part):
    cut_zero, cut_one, cut_two, cut_three, pad_start = row_bounds(key)
    positions = jnp.arange(SEQ)[None, :]
    doc_ids = (positions >= cut_zero[:, None]).astype(jnp.int32)
    doc_ids = doc_ids + (positions >= cut_one[:, None]).astype(jnp.int32)
    doc_ids = doc_ids + (positions >= cut_two[:, None]).astype(jnp.int32)
    doc_ids = doc_ids + (positions >= cut_three[:, None]).astype(jnp.int32)
    return doc_ids


def draw_pad_mask(key, part):
    cut_zero, cut_one, cut_two, cut_three, pad_start = row_bounds(key)
    positions = jnp.arange(SEQ)[None, :]
    return (positions < pad_start[:, None]).astype(jnp.int32)


def shared_offset(key):
    direction = jax.random.truncated_normal(jax.random.fold_in(key, 101), -4.0, 4.0, (D,), jnp.float32)
    sign_bits = jax.random.randint(jax.random.fold_in(key, 102), (HEAD_DIM,), 0, 2)
    column_signs = sign_bits.astype(jnp.float32) * 2.0 - 1.0
    return (direction, column_signs)


def with_offset(noise, direction, column_signs, strength):
    leading = noise[:, :HEAD_DIM] + strength * direction[:, None] * column_signs[None, :]
    return jnp.concatenate([leading, noise[:, HEAD_DIM:]], axis=1)


def draw_norm1_shift(key, part):
    direction, column_signs = shared_offset(key)
    return 0.25 * direction


def draw_w_query(key, part):
    direction, column_signs = shared_offset(key)
    key = jax.random.fold_in(key, 3)
    noise = jax.random.truncated_normal(key, -5.0, 5.0, (D, D), jnp.float32) / math.sqrt(D)
    return with_offset(noise, direction, column_signs, math.sqrt(64.0 / HEAD_DIM) / (0.25 * D)).astype(jnp.bfloat16)


def draw_w_key(key, part):
    direction, column_signs = shared_offset(key)
    key = jax.random.fold_in(key, 4)
    noise = jax.random.truncated_normal(key, -5.0, 5.0, (D, D), jnp.float32) / math.sqrt(D)
    return with_offset(noise, direction, column_signs, -math.sqrt(64.0 / HEAD_DIM) / (0.25 * D)).astype(jnp.bfloat16)


def level_of(own_key, extent, shards, low, high):
    factor_of, own = 1.0, jax.random.fold_in(own_key, 6)
    for axis_at, parts in shards:
        heights = jnp.exp(jax.random.uniform(jax.random.fold_in(own, axis_at), (parts,), jnp.float32, low / len(shards), high / len(shards)))
        factor_of = factor_of * jnp.repeat(heights, extent[axis_at] // parts).reshape([-1 if axis == axis_at else 1 for axis in range(len(extent))])
    return factor_of


def bell_draw(key, shape, deviation, most, cuts=(), kind=jnp.bfloat16):
    array = deviation * jax.random.normal(key, shape, jnp.float32)
    if cuts:
        array = array * level_of(key, shape, cuts, -0.22, 0.18)
    return jnp.clip(array, -most, most).astype(kind)


def setup_inputs(seed: int = 0) -> dict:
    key_of = jax.random.split(jax.random.key(seed), 15)
    return {
        "tokens": bell_draw(key_of[0], (TOKENS, D), 1.0, 6.0, ((0, 32),)),
        "segment_ids": draw_segment_ids(jax.random.fold_in(key_of[14], 71), 0),
        "pad_mask": draw_pad_mask(jax.random.fold_in(key_of[14], 71), 0),
        "norm1_gain": jnp.clip(1.0 + 0.1 * jax.random.normal(key_of[3], (D,), jnp.float32), 0.5, 1.5),
        "norm1_shift": draw_norm1_shift(jax.random.fold_in(key_of[14], 71), 0),
        "w_query": draw_w_query(jax.random.fold_in(key_of[14], 71), 0),
        "w_key": draw_w_key(jax.random.fold_in(key_of[14], 71), 0),
        "w_value": bell_draw(key_of[7], (D, D), D ** -0.5, 0.21875, ((1, 2),)),
        "w_out": bell_draw(key_of[8], (D, D), (D // 4) ** -0.5, 0.4375, ((0, 2),)),
        "norm2_gain": jnp.clip(1.0 + 0.1 * jax.random.normal(key_of[9], (D,), jnp.float32), 0.5, 1.5),
        "norm2_shift": bell_draw(key_of[10], (D,), 0.2, 1.0, (), jnp.float32),
        "w_up": bell_draw(key_of[11], (D, FF), D ** -0.5, 0.21875, ((1, 2),)),
        "w_down": bell_draw(key_of[12], (FF, D), FF ** -0.5, 0.109375, ((0, 2),)),
        "cotangent": bell_draw(key_of[13], (TOKENS, D), 1.0, 6.0, ((0, 32),)),
    }


@jax.custom_vjp
def low(v):
    return lax.optimization_barrier(v.astype(jnp.bfloat16)).astype(jnp.float32)

@jax.custom_vjp
def low_back(v):
    return v

def low_keep(v):
    return (low(v), None)

def low_pass(kept, grad):
    return (grad,)

def back_keep(v):
    return (v, None)

def back_low(kept, grad):
    return (low(grad),)
low.defvjp(low_keep, low_pass)
low_back.defvjp(back_keep, back_low)
highest = lax.Precision.HIGHEST
eps_norm = 1e-05

def high_dot(first_op, second_op):
    return jnp.dot(first_op, second_op, precision=highest, preferred_element_type=jnp.float32)

def norm_rows(values, norm_gain, norm_shift):
    center = values - lax.optimization_barrier(jnp.mean(values, axis=-1, keepdims=True))
    inverse = lax.rsqrt(lax.optimization_barrier(jnp.mean(center * center, axis=-1, keepdims=True)) + eps_norm)
    return center * inverse * norm_gain + norm_shift

def row_masks(seg_row, pad_row):
    length = seg_row.shape[0]
    row_ids = jnp.arange(length)[:, None]
    col_ids = jnp.arange(length)[None, :]
    same_doc = seg_row[:, None] == seg_row[None, :]
    real_key = pad_row[None, :] > 0
    allowed = same_doc & (col_ids <= row_ids) & real_key | (col_ids == row_ids)
    picked = same_doc & (col_ids < row_ids) & real_key & (pad_row[:, None] > 0)
    return (allowed, picked)

def reference(tokens, segment_ids, pad_mask, norm1_gain, norm1_shift, w_query, w_key, w_value, w_out, norm2_gain, norm2_shift, w_up, w_down, cotangent):

    def as_float(array_in):
        return array_in.astype(jnp.float32)
    row_block = as_float(tokens).reshape(-1, SEQ, D)
    params = [as_float(p_item) for p_item in (norm1_gain, norm1_shift, w_query, w_key, w_value, w_out, norm2_gain, norm2_shift, w_up, w_down)]

    def forward(all_rows, gain_one, shift_one, query_w, key_w, value_w, out_w, gain_two, shift_two, up_w, down_w):

        def one_sequence(inputs):
            seq_rows, seg_row, pad_row = inputs
            allowed, picked = row_masks(seg_row, pad_row)
            length = seq_rows.shape[0]
            normed = low(norm_rows(seq_rows, gain_one, shift_one))

            def project(weight):
                return low(low_back(high_dot(normed, weight))).reshape(length, HEADS, HEAD_DIM)
            queries = project(query_w)
            keys_all = project(key_w)
            values_all = project(value_w)
            raw_scores = jnp.einsum('ihd,jhd->hij', queries, keys_all, precision=highest) * 0.125
            scores = low_back(raw_scores)
            select = low(jnp.where(picked, jax.nn.softplus(raw_scores[0]), 0.0))
            positions = jnp.arange(length)
            lower_ones = (positions[None, :] < positions[:, None]).astype(jnp.float32)
            penalty = high_dot(lower_ones, select)
            logits = jnp.where(allowed[None], scores - penalty[None], -1e+30)
            probs_all = jax.nn.softmax(logits, axis=-1)
            heads_out = jnp.einsum('hij,jhd->ihd', low(probs_all), values_all, precision=highest).reshape(length, HEADS * HEAD_DIM)
            attended = low_back(high_dot(low(low_back(heads_out)), out_w))
            hidden = seq_rows + attended
            normed_two = low(norm_rows(hidden, gain_two, shift_two))
            up_values = low_back(high_dot(normed_two, up_w))
            active = low(jax.nn.gelu(up_values, approximate=False))
            return hidden + high_dot(active, down_w)
        return lax.map(jax.checkpoint(one_sequence), (all_rows, segment_ids, pad_mask))
    outputs, pullback = jax.vjp(forward, row_block, *params)
    gradients = pullback(as_float(cotangent).reshape(outputs.shape))
    return (outputs.reshape(-1, D).astype(jnp.bfloat16), gradients[0].reshape(-1, D).astype(jnp.bfloat16), gradients[1], gradients[2], gradients[3], gradients[4], gradients[5], gradients[6], gradients[7], gradients[8], gradients[9], gradients[10])
```

```python
import functools

import jax
import jax.numpy as jnp
from jax import lax
from jax.experimental import pallas as pl
from jax.experimental.pallas import tpu as pltpu
from jax.sharding import PartitionSpec as P

HEAD_DIM = 64
EPS = 1e-05
FAR = 1e30
FORWARD_BLOCK = 512
BF16 = jnp.bfloat16
F32 = jnp.float32
TN = (((0,), (0,)), ((), ()))
NT = (((1,), (1,)), ((), ()))
NN = (((1,), (0,)), ((), ()))
TT = (((0,), (1,)), ((), ()))
ERF_P = 0.39
ERF_C = (
    0.23532589847272212,
    0.09138415344709826,
    0.6495700167142381,
    -0.6354134214178592,
    0.8866724519682867,
    -0.22753910091022167,
)


def dot(left, right, dims):
    return lax.dot_general(left, right, dims, preferred_element_type=F32)


def cost(flops, nbytes):
    return pl.CostEstimate(flops=int(flops), bytes_accessed=int(nbytes), transcendentals=0)


def params():
    return pltpu.CompilerParams(vmem_limit_bytes=58 << 20)


def sds(shape, dtype):
    return jax.ShapeDtypeStruct(shape, dtype)


SMEM = pl.BlockSpec(memory_space=pltpu.SMEM)


def whole(shape):
    return pl.BlockSpec(shape, lambda *_: (0,) * len(shape))


def normalize(values):
    center = values - jnp.mean(values, axis=-1, keepdims=True)
    inverse = lax.rsqrt(jnp.mean(center * center, axis=-1, keepdims=True) + EPS)
    return center * inverse, inverse


def norm_back(grad_normed, scaled, inverse, gain):
    grad_scaled = grad_normed * gain
    return inverse * (
        grad_scaled
        - jnp.mean(grad_scaled, axis=-1, keepdims=True)
        - scaled * jnp.mean(grad_scaled * scaled, axis=-1, keepdims=True)
    )


def gelu_pair(x):
    z = jnp.abs(x) * 0.7071067811865476
    t = 1.0 / (1.0 + ERF_P * z)
    poly = ERF_C[5]
    for coefficient in ERF_C[4::-1]:
        poly = poly * t + coefficient
    bell = jnp.exp(-0.5 * x * x)
    tail = 0.5 * poly * t * bell
    phi = jnp.where(x >= 0, 1.0 - tail, tail)
    return x * phi, phi + x * bell * 0.3989422804014327


def norm1_kernel(tokens, gain, shift, out):
    scaled, _ = normalize(tokens[...].astype(F32))
    out[...] = (scaled * gain[...] + shift[...]).astype(BF16)


def norm1(tokens, gain, shift):
    return pl.pallas_call(
        norm1_kernel,
        out_shape=sds(tokens.shape, BF16),
        compiler_params=params(),
        cost_estimate=cost(0, 4 * tokens.size),
    )(tokens, gain, shift)


def masks(seg_pad, cols, low, high):
    width = high - low
    seg_row = seg_pad[0:1, low:high]
    pad_row = seg_pad[1:2, low:high]
    row_key = jnp.where(pad_row > 0, seg_row, -2.0)
    col_seg = cols[:high, 0:1]
    col_pad = cols[:high, 1:2]
    col_key = jnp.where(col_pad > 0, col_seg, -1.0)
    key_at = lax.broadcasted_iota(jnp.int32, (high, width), 0)
    query_at = lax.broadcasted_iota(jnp.int32, (high, width), 1) + low
    allowed = ((col_key == seg_row) & (key_at <= query_at)) | (key_at == query_at)
    picked = (col_key == row_key) & (key_at < query_at)
    return allowed, picked


def penalty_kernel(block, core, n1_own, n1_other, wqk0, seg_pad, n1_out, penalty, qk0):
    seq = n1_out.shape[0]
    half = seq // 2
    here = core[0]
    n1_out[pl.ds(pl.multiple_of(here * half, half), half), :] = n1_own[...]
    n1_out[pl.ds(pl.multiple_of((1 - here) * half, half), half), :] = n1_other[...]
    qk = dot(wqk0[...], n1_out[...], TT)
    q0 = (qk[:HEAD_DIM].astype(BF16) * 0.125).astype(BF16)
    k0 = qk[HEAD_DIM:].astype(BF16)
    qk0[:HEAD_DIM, :] = q0
    qk0[HEAD_DIM:, :] = k0
    seg_value = seg_pad[...]
    cols = seg_value.T
    earlier = lax.broadcasted_iota(jnp.int32, (block, block + 128), 0)
    later = lax.broadcasted_iota(jnp.int32, (block, block + 128), 1)
    sums = ((earlier < later) | (later >= block)).astype(F32).astype(BF16)
    carry = jnp.zeros((seq, 128), F32)
    for low in range(0, seq, block):
        high = low + block
        allowed, picked = masks(seg_value, cols, low, high)
        score = dot(k0[:, :high], q0[:, low:high], TN)
        small = jnp.exp(-jnp.abs(score))
        log1p = jnp.where(small < 1e-3, small - 0.5 * small * small, jnp.log(1.0 + small))
        select = jnp.where(picked, jnp.maximum(score, 0.0) + log1p, 0.0).astype(BF16)
        total = dot(select, sums, NN)
        before = jnp.concatenate([carry[:high]] * (block // 128), axis=1)
        penalty[:high, low:high] = jnp.where(allowed, total[:, :block] + before, FAR)
        if high % FORWARD_BLOCK:
            edge = high + FORWARD_BLOCK - high % FORWARD_BLOCK
            penalty[high:edge, low:high] = jnp.full((edge - high, block), FAR, F32)
        carry = jnp.concatenate([carry[:high] + total[:, block:], carry[high:]], axis=0)


def penalty_call(core, n1_own, n1_other, wqk0, seg_pad):
    half, dim = n1_own.shape
    seq = 2 * half
    return pl.pallas_call(
        functools.partial(penalty_kernel, 256),
        in_specs=[SMEM] + [pl.BlockSpec(memory_space=pltpu.VMEM)] * 4,
        out_shape=[sds((seq, dim), BF16), sds((seq, seq), F32), sds((2 * HEAD_DIM, seq), BF16)],
        compiler_params=params(),
        cost_estimate=cost(3e9, 8e6),
    )(core, n1_own, n1_other, wqk0, seg_pad)


def forward_kernel(block, n1, weights, penalty, qkv, out, lse):
    head = pl.program_id(0)
    third = qkv.shape[0] // 3
    seq = qkv.shape[1]

    @pl.when(head == 0)
    def _():
        product = dot(weights[...], n1[...], TT).astype(BF16)
        qkv[:third, :] = (product[:third] * 0.125).astype(BF16)
        qkv[third:, :] = product[third:]

    at = pl.multiple_of(head * HEAD_DIM, HEAD_DIM)
    query = qkv[pl.ds(at, HEAD_DIM), :]
    key = qkv[pl.ds(third + at, HEAD_DIM), :]
    value = qkv[pl.ds(2 * third + at, HEAD_DIM), :]
    value = jnp.concatenate([value, jnp.ones((16, seq), BF16)], axis=0)
    for low in range(0, seq, block):
        high = low + block
        logits = dot(key[:, :high], query[:, low:high], TN) - penalty[:high, low:high]
        largest = jnp.max(logits, axis=0, keepdims=True)
        weight = jnp.exp(logits - largest).astype(BF16)
        result = dot(value[:, :high], weight, NN)
        total = result[HEAD_DIM : HEAD_DIM + 1, :]
        out[:, low:high] = (result[:HEAD_DIM] / total).astype(BF16)
        lse[:, low:high] = largest + jnp.log(total)


def forward_call(n1, weights, penalty):
    seq, dim = n1.shape
    width = weights.shape[1]
    heads = width // (3 * HEAD_DIM)
    return pl.pallas_call(
        functools.partial(forward_kernel, FORWARD_BLOCK),
        grid=(heads,),
        in_specs=[whole((seq, dim)), whole((dim, width)), whole((seq, seq))],
        out_specs=[
            whole((width, seq)),
            pl.BlockSpec((HEAD_DIM, seq), lambda h: (h, 0)),
            pl.BlockSpec((None, 1, seq), lambda h: (h, 0, 0)),
        ],
        out_shape=[
            sds((width, seq), BF16),
            sds((heads * HEAD_DIM, seq), BF16),
            sds((heads, 1, seq), F32),
        ],
        compiler_params=params(),
        cost_estimate=cost(5e9, 8e6),
    )(n1, weights, penalty)


def project_kernel(core, out_l, out_r, w_l, w_r, own, send):
    half = own.shape[0]
    here = core[0]
    mixed = jnp.concatenate([w_l[...], w_r[...]], axis=0)

    def part(which):
        at = pl.ds(pl.multiple_of(which * half, half), half)
        heads = jnp.concatenate([out_l[:, at], out_r[:, at]], axis=0)
        return dot(heads, mixed, TN)

    send[...] = part(1 - here).astype(BF16)
    own[...] = part(here)


def project_call(core, out_l, out_r, w_l, w_r):
    half, dim = out_l.shape[1] // 2, w_l.shape[1]
    return pl.pallas_call(
        project_kernel,
        in_specs=[SMEM] + [pl.BlockSpec(memory_space=pltpu.VMEM)] * 4,
        out_shape=[sds((half, dim), F32), sds((half, dim), BF16)],
        compiler_params=params(),
        cost_estimate=cost(6e8, 5e6),
    )(core, out_l, out_r, w_l, w_r)


def norm2_kernel(tokens, own, received, gain, shift, hidden, out):
    total = tokens[...].astype(F32) + (own[...] + received[...].astype(F32))
    hidden[...] = total
    scaled, _ = normalize(total)
    out[...] = (scaled * gain[...] + shift[...]).astype(BF16)


def norm2_call(tokens, own, received, gain, shift):
    return pl.pallas_call(
        norm2_kernel,
        out_shape=[sds(tokens.shape, F32), sds(tokens.shape, BF16)],
        compiler_params=params(),
        cost_estimate=cost(0, 14 * tokens.size),
    )(tokens, own, received, gain, shift)


def mlp_kernel(first, steps, *refs):
    if first:
        n2_other, n2_own, g_other, g_own, w_up, w_down = refs[:6]
        rest = refs[6:]
        before = None
    else:
        n2_other, n2_own, g_other, g_own, w_up, w_down = refs[:6]
        before = refs[6:10]
        rest = refs[10:]
    mixed_send, mixed_own, back_send, back_own, w_grads, sums = rest
    step = pl.program_id(0)
    dim = w_up.shape[0]

    def work(n2, grad, mixed_out, back_out, mixed_in, back_in):
        rows = n2[...]
        grad_rows = grad[...]
        up_values = dot(rows, w_up[...], NN)
        active, slope = gelu_pair(up_values)
        active = active.astype(BF16)
        grad_up = (dot(grad_rows, w_down[...], NT) * slope).astype(BF16)
        back = dot(grad_up, w_up[...], NT)
        mixed = dot(active, w_down[...], NN)
        if mixed_in is not None:
            back = back + back_in[...]
            mixed = mixed + mixed_in[...]
        back_out[...] = back.astype(back_out.dtype)
        mixed_out[...] = mixed.astype(mixed_out.dtype)
        up_grad = dot(rows, grad_up, TN)
        down_grad = dot(active, grad_rows, TN)

        @pl.when(step == 0)
        def _():
            sums[:dim, :] = up_grad
            sums[dim:, :] = down_grad

        @pl.when(step > 0)
        def _():
            sums[:dim, :] += up_grad
            sums[dim:, :] += down_grad

    @pl.when(step < steps // 2)
    def _():
        ins = (None, None) if first else (before[0], before[2])
        work(n2_other, g_other, mixed_send, back_send, *ins)

    @pl.when(step >= steps // 2)
    def _():
        ins = (None, None) if first else (before[1], before[3])
        work(n2_own, g_own, mixed_own, back_own, *ins)

    @pl.when(step == steps - 1)
    def _():
        w_grads[...] = sums[...].astype(w_grads.dtype)


def mlp_call(n2_other, n2_own, g_other, g_own, w_up, w_down, before=None):
    half, dim = n2_own.shape
    units = w_up.shape[1]
    block = 256
    steps = 2 * half // block
    last = steps // 2 - 1
    sent = pl.BlockSpec((block, dim), lambda i: (jnp.minimum(i, last), 0))
    kept = pl.BlockSpec((block, dim), lambda i: (jnp.maximum(i - last - 1, 0), 0))
    first = before is None
    operands = (n2_other, n2_own, g_other, g_own, w_up, w_down) + (() if first else tuple(before))
    in_specs = [sent, kept, sent, kept, whole((dim, units)), whole((units, dim))]
    in_specs += [] if first else [sent, kept, sent, kept]
    sent_type = F32 if first else BF16
    return pl.pallas_call(
        functools.partial(mlp_kernel, first, steps),
        grid=(steps,),
        in_specs=in_specs,
        out_specs=[sent, kept, sent, kept, whole((dim + units, dim))],
        out_shape=[
            sds((half, dim), sent_type),
            sds((half, dim), F32),
            sds((half, dim), sent_type),
            sds((half, dim), F32),
            sds((dim + units, dim), F32 if first else BF16),
        ],
        scratch_shapes=[pltpu.VMEM((dim + units, dim), F32)],
        compiler_params=params(),
        cost_estimate=cost(7.2e9, 18e6),
    )(*operands)


def norm2_back_kernel(hidden, own, received, grad, gain, grad_hidden, low, sums):
    normed_grad = own[...] + received[...].astype(F32)
    scaled, inverse = normalize(hidden[...])
    total = grad[...].astype(F32) + norm_back(normed_grad, scaled, inverse, gain[...])
    grad_hidden[...] = total
    low[...] = total.astype(BF16)
    sums[...] = jnp.zeros(sums.shape, F32)
    sums[0:1, :] = jnp.sum(normed_grad * scaled, axis=0, keepdims=True)
    sums[1:2, :] = jnp.sum(normed_grad, axis=0, keepdims=True)


def norm2_back_call(hidden, own, received, grad, gain):
    return pl.pallas_call(
        norm2_back_kernel,
        out_shape=[
            sds(hidden.shape, F32),
            sds(hidden.shape, BF16),
            sds((8, hidden.shape[1]), F32),
        ],
        compiler_params=params(),
        cost_estimate=cost(0, 18 * hidden.size),
    )(hidden, own, received, grad, gain)


def backward_kernel(first, block, *refs):
    core, g_own, g_other, w_out, heads_out, qkv, lse, penalty = refs[:8]
    if first:
        before = None
        grads, w_grad, logit_sum, grad_full, grad_heads, key_sum, value_sum = refs[8:]
        low_sum = None
    else:
        before = refs[8]
        grads, w_grad, logit_sum, low_sum, grad_full, grad_heads, key_sum, value_sum = refs[9:]
    head = pl.program_id(0)
    third = qkv.shape[0] // 3
    seq = qkv.shape[1]
    half = seq // 2

    @pl.when(head == 0)
    def _():
        here = core[0]
        grad_full[pl.ds(pl.multiple_of(here * half, half), half), :] = g_own[...]
        grad_full[pl.ds(pl.multiple_of((1 - here) * half, half), half), :] = g_other[...]
        whole_grad = grad_full[...]
        grad_heads[...] = dot(w_out[...], whole_grad, NT).astype(BF16)
        w_grad[...] = dot(heads_out[...], whole_grad, NN).astype(w_grad.dtype)

    at = pl.multiple_of(head * HEAD_DIM, HEAD_DIM)
    query = qkv[pl.ds(at, HEAD_DIM), :]
    key = qkv[pl.ds(third + at, HEAD_DIM), :]
    value = qkv[pl.ds(2 * third + at, HEAD_DIM), :]
    grad = grad_heads[pl.ds(at, HEAD_DIM), :]
    for low in range(0, seq, block):
        high = low + block
        cols = slice(low, high)
        score = dot(key[:, :high], query[:, cols], TN)
        probs = jnp.exp(score - penalty[:high, cols] - lse[:, cols])
        grad_probs = dot(value[:, :high], grad[:, cols], TN)
        row_dot = jnp.sum(probs * grad_probs, axis=0, keepdims=True)
        grad_logits = probs * (grad_probs - row_dot)
        if first:

            @pl.when(head == 0)
            def _():
                logit_sum[:high, cols] = grad_logits

            @pl.when(head > 0)
            def _():
                logit_sum[:high, cols] += grad_logits

        else:

            @pl.when(head == 0)
            def _():
                logit_sum[:high, cols] = before[:high, cols] + grad_logits

            @pl.when(head > 0)
            def _():
                logit_sum[:high, cols] += grad_logits

        low_logits = grad_logits.astype(BF16)
        low_probs = probs.astype(BF16)
        grads[pl.ds(at, HEAD_DIM), cols] = (
            dot(key[:, :high], low_logits, NN) * 0.125
        ).astype(BF16)
        value_new = dot(grad[:, cols], low_probs, NT)
        key_new = dot(query[:, cols], low_logits, NT)
        if low:
            key_sum[:, :low] += key_new[:, :low]
            value_sum[:, :low] += value_new[:, :low]
        key_sum[:, cols] = key_new[:, low:]
        value_sum[:, cols] = value_new[:, low:]
    grads[pl.ds(third + at, HEAD_DIM), :] = key_sum[...].astype(BF16)
    grads[pl.ds(2 * third + at, HEAD_DIM), :] = value_sum[...].astype(BF16)
    if low_sum is not None:

        @pl.when(head == pl.num_programs(0) - 1)
        def _():
            for low in range(0, seq, block):
                high = low + block
                low_sum[:high, low:high] = logit_sum[:high, low:high].astype(BF16)


def backward_call(core, g_own, g_other, w_out, heads_out, qkv, lse, penalty, before=None):
    width, seq = qkv.shape
    heads = width // (3 * HEAD_DIM)
    half, dim = g_own.shape
    first = before is None
    square = whole((seq, seq))
    operands = (core, g_own, g_other, w_out, heads_out, qkv, lse, penalty)
    in_specs = [
        SMEM,
        whole((half, dim)),
        whole((half, dim)),
        whole(w_out.shape),
        whole(heads_out.shape),
        whole((width, seq)),
        pl.BlockSpec((None, 1, seq), lambda h: (h, 0, 0)),
        square,
    ]
    out_specs = [whole((width, seq)), whole(w_out.shape), square]
    out_shape = [sds((width, seq), BF16), sds(w_out.shape, F32), sds((seq, seq), F32)]
    if not first:
        operands += (before,)
        in_specs.append(square)
        out_specs.append(square)
        out_shape.append(sds((seq, seq), BF16))
    return pl.pallas_call(
        functools.partial(backward_kernel, first, 256),
        grid=(heads,),
        in_specs=in_specs,
        out_specs=out_specs,
        out_shape=out_shape,
        scratch_shapes=[
            pltpu.VMEM((seq, dim), BF16),
            pltpu.VMEM((width // 3, seq), BF16),
            pltpu.VMEM((HEAD_DIM, seq), F32),
            pltpu.VMEM((HEAD_DIM, seq), F32),
        ],
        compiler_params=params(),
        cost_estimate=cost(1e10, 16e6),
    )(*operands)


def halves(value):
    high = value.astype(BF16)
    return high, (value - high.astype(F32)).astype(BF16)


def select_back_kernel(block, own, received, qk0, seg_pad, out):
    seq = own.shape[0]
    q0 = qk0[:HEAD_DIM, :]
    k0 = qk0[HEAD_DIM:, :]
    seg_value = seg_pad[...]
    cols = seg_value.T
    later = lax.broadcasted_iota(jnp.int32, (block, block + 128), 0)
    earlier = lax.broadcasted_iota(jnp.int32, (block, block + 128), 1)
    sums = ((later > earlier) | (earlier >= block)).astype(F32).astype(BF16)
    carry = jnp.zeros((seq, 128), F32)
    out[...] = jnp.zeros(out.shape, F32)
    for low in range(seq - block, -1, -block):
        high = low + block
        logit_sum = own[:high, low:high] + received[:high, low:high].astype(F32)
        top, bottom = halves(logit_sum)
        total = dot(top, sums, NN) + dot(bottom, sums, NN)
        after = jnp.concatenate([carry[:high]] * (block // 128), axis=1)
        select_grad = -(total[:, :block] + after)
        carry = carry[:high] + total[:, block:]
        _, picked = masks(seg_value, cols, low, high)
        score = dot(k0[:, :high], q0[:, low:high], TN)
        through = jnp.where(picked, select_grad / (1.0 + jnp.exp(-score)), 0.0)
        top, bottom = halves(through)
        out[:HEAD_DIM, low:high] = 0.125 * (
            dot(k0[:, :high], top, NN) + dot(k0[:, :high], bottom, NN)
        )
        out[HEAD_DIM:, :high] += dot(q0[:, low:high], top, NT) + dot(q0[:, low:high], bottom, NT)


def select_back_call(own, received, qk0, seg_pad):
    return pl.pallas_call(
        functools.partial(select_back_kernel, 256),
        out_shape=sds(qk0.shape, F32),
        compiler_params=params(),
        cost_estimate=cost(4e9, 8e6),
    )(own, received, qk0, seg_pad)


def weights_kernel(core, flags, n1, grads_l, grads_r, extra, w_l, w_r, out_l, out_r, *rest):
    sum_l, sum_r, own, send, all_grads = rest
    width = grads_l.shape[0]
    third = width // 3
    half = own.shape[0]
    all_grads[:width, :] = grads_l[...]
    all_grads[width:, :] = grads_r[...]
    for place, flag in ((0, flags[0]), (width, flags[1])):

        @pl.when(flag > 0)
        def _():
            for at, source in ((place, 0), (place + third, HEAD_DIM)):
                rows = slice(at, at + HEAD_DIM)
                all_grads[rows, :] = (
                    all_grads[rows, :].astype(F32) + extra[source : source + HEAD_DIM, :]
                ).astype(BF16)

    here = core[0]
    both = jnp.concatenate([w_l[...], w_r[...]], axis=1)

    def part(which):
        at = pl.ds(pl.multiple_of(which * half, half), half)
        return dot(all_grads[:, at], both, TT)

    send[...] = part(1 - here).astype(BF16)
    own[...] = part(here)
    product = dot(all_grads[...], n1[...], NN)
    sum_l[:width, :] = product[:width]
    sum_l[width:, :] = out_l[...]
    sum_r[:width, :] = product[width:].astype(BF16)
    sum_r[width:, :] = out_r[...].astype(BF16)


def weights_call(core, flags, n1, grads_l, grads_r, extra, w_l, w_r, out_l, out_r):
    seq, dim = n1.shape
    width = grads_l.shape[0]
    rows = width + out_l.shape[0]
    return pl.pallas_call(
        weights_kernel,
        in_specs=[SMEM, SMEM] + [pl.BlockSpec(memory_space=pltpu.VMEM)] * 8,
        out_shape=[
            sds((rows, dim), F32),
            sds((rows, dim), BF16),
            sds((seq // 2, dim), F32),
            sds((seq // 2, dim), BF16),
        ],
        scratch_shapes=[pltpu.VMEM((2 * width, seq), BF16)],
        compiler_params=params(),
        cost_estimate=cost(4e9, 16e6),
    )(core, flags, n1, grads_l, grads_r, extra, w_l, w_r, out_l, out_r)


def norm1_back_kernel(tokens, own, received, grad_hidden, gain, out, sums):
    normed_grad = own[...] + received[...].astype(F32)
    scaled, inverse = normalize(tokens[...].astype(F32))
    total = grad_hidden[...] + norm_back(normed_grad, scaled, inverse, gain[...])
    out[...] = total.astype(BF16)
    sums[...] = jnp.zeros(sums.shape, F32)
    sums[0:1, :] = jnp.sum(normed_grad * scaled, axis=0, keepdims=True)
    sums[1:2, :] = jnp.sum(normed_grad, axis=0, keepdims=True)


def norm1_back_call(tokens, own, received, grad_hidden, gain):
    return pl.pallas_call(
        norm1_back_kernel,
        out_shape=[sds(tokens.shape, BF16), sds((8, tokens.shape[1]), F32)],
        compiler_params=params(),
        cost_estimate=cost(0, 14 * tokens.size),
    )(tokens, own, received, grad_hidden, gain)


def make_body(devices, parts):
    axes = ("dp", "tensor")
    chips = devices // 2
    masks_in_order = [1 << bit for bit in range(chips.bit_length() - 1)]
    turned = masks_in_order[1:] + masks_in_order[:1]

    def pairs(move):
        found = []
        for device in range(devices):
            for part in range(parts):
                to_chip, to_core, to_part = move(device // 2, device % 2, part)
                source = device * parts + part
                found.append((source, (to_chip * 2 + to_core) * parts + to_part))
        return found

    by_role = pairs(lambda chip, core, part: (chip, part, core))
    by_core = pairs(lambda chip, core, part: (chip, 1 - core, part))
    by_part = pairs(lambda chip, core, part: (chip, core, 1 - part))
    first_part = [pair for pair in by_part if pair[0] % parts == 0]
    first_core = [pair for pair in by_core if (pair[0] // parts) % 2 == 1]
    by_chip = [
        pairs(lambda chip, core, part: (chip ^ (turned[i] if core else masks_in_order[i]), core, part))
        for i in range(len(masks_in_order))
    ]

    def move(value, how):
        return lax.ppermute(value, axes, how)

    def body(
        tokens,
        segment_ids,
        pad_mask,
        norm1_gain,
        norm1_shift,
        w_query,
        w_key,
        w_value,
        w_out,
        norm2_gain,
        norm2_shift,
        w_up,
        w_down,
        cotangent,
    ):
        device = lax.axis_index("dp")
        part = lax.axis_index("tensor")
        core = device % 2
        chip = device // 2
        core_ref = jnp.reshape(core, (1,)).astype(jnp.int32)
        bits = [
            jnp.where(core == 1, (chip & turned[i]) != 0, (chip & masks_in_order[i]) != 0)
            for i in range(len(masks_in_order))
        ]
        gain1, shift1, gain2, shift2 = (
            vector[None, :] for vector in (norm1_gain, norm1_shift, norm2_gain, norm2_shift)
        )
        dim = tokens.shape[1]
        width = w_query.shape[1] // 2
        units = w_up.shape[1] // 2

        mine = move(tokens, by_role)
        first_heads = jnp.concatenate([w_query[:, :HEAD_DIM], w_key[:, :HEAD_DIM]], axis=1)
        first_moved = move(first_heads, first_part)
        wqk0 = jnp.where(part == 0, first_heads, first_moved)
        ints = jnp.concatenate([segment_ids, pad_mask], axis=0)
        ints = jnp.where(core == part, ints, move(ints, by_core)).astype(F32)
        seg_pad = jnp.concatenate([ints, jnp.zeros((6, ints.shape[1]), F32)], axis=0)

        def columns(weight, size):
            return lax.dynamic_slice_in_dim(weight, core * size, size, axis=1)

        def rows(weight, size):
            return lax.dynamic_slice_in_dim(weight, core * size, size, axis=0)

        qkv_l = jnp.concatenate(
            [columns(weight, width) for weight in (w_query, w_key, w_value)], axis=1
        )
        out_l = rows(w_out, width)
        up_l = columns(w_up, units)
        down_l = rows(w_down, units)
        qkv_r = move(qkv_l, by_part)
        out_r = move(out_l, by_part)
        grad_own = move(cotangent, by_role)
        up_r = move(up_l, by_part)
        down_r = move(down_l, by_part)

        n1_own = norm1(mine, gain1, shift1)
        n1_other = move(n1_own, by_core)
        grad_other = move(grad_own, by_core)
        n1, penalty, qk0 = penalty_call(core_ref, n1_own, n1_other, wqk0, seg_pad)
        qkvt_l, heads_l, lse_l = forward_call(n1, qkv_l, penalty)
        qkvt_r, heads_r, lse_r = forward_call(n1, qkv_r, penalty)
        own, send = project_call(core_ref, heads_l, heads_r, out_l, out_r)
        hidden, n2_own = norm2_call(mine, own, move(send, by_core), gain2, shift2)
        n2_other = move(n2_own, by_core)
        *before, ff_l = mlp_call(n2_other, n2_own, grad_other, grad_own, up_l, down_l)
        mixed_send, mixed_own, back_send, back_own, ff_r = mlp_call(
            n2_other, n2_own, grad_other, grad_own, up_r, down_r, before
        )
        grad_hidden, low_own, sums2 = norm2_back_call(
            hidden, back_own, move(back_send, by_core), grad_own, gain2
        )
        low_other = move(low_own, by_core)
        mixed = hidden + (mixed_own + move(mixed_send, by_core).astype(F32))
        mixed = move(mixed.astype(BF16), by_role)

        grads_r, wo_r, sum_r = backward_call(
            core_ref, low_own, low_other, out_r, heads_r, qkvt_r, lse_r, penalty
        )
        grads_l, wo_l, logit_sum, logit_low = backward_call(
            core_ref, low_own, low_other, out_l, heads_l, qkvt_l, lse_l, penalty, sum_r
        )
        extra = select_back_call(logit_sum, move(logit_low, first_core), qk0, seg_pad)
        flags = jnp.stack([(core == 0) & (part == 0), (core == 0) & (part == 1)])
        sum_l, sum_r, own, send = weights_call(
            core_ref, flags.astype(jnp.int32), n1, grads_l, grads_r, extra, qkv_l, qkv_r, wo_l, wo_r
        )
        tokens_grad, sums1 = norm1_back_call(
            mine, own, move(send, by_core), grad_hidden, gain1
        )
        tokens_grad = move(tokens_grad, by_role)

        def all_sum(mine_l, mine_r):
            value = mine_l + move(mine_r, by_part).astype(F32)
            for how, bit in zip(by_chip, bits):
                size = value.shape[0] // 2
                at = jnp.where(bit, size, 0)
                sent = lax.dynamic_slice_in_dim(value, size - at, size, axis=0).astype(BF16)
                kept = lax.dynamic_slice_in_dim(value, at, size, axis=0)
                value = kept + move(sent, how).astype(F32)
            value = value.astype(BF16)
            for how, bit in zip(by_chip[::-1], bits[::-1]):
                got = move(value, how)
                value = jnp.concatenate(
                    [jnp.where(bit, got, value), jnp.where(bit, value, got)], axis=0
                )
            other = move(value, by_core)
            return (
                jnp.where(core == 0, value, other).astype(F32),
                jnp.where(core == 0, other, value).astype(F32),
            )

        ff_0, ff_1 = all_sum(ff_l, ff_r)
        at_0, at_1 = all_sum(sum_l, sum_r)
        up_grad = jnp.concatenate([ff_0[:dim], ff_1[:dim]], axis=1)
        down_grad = jnp.concatenate([ff_0[dim:], ff_1[dim:]], axis=0)
        w_grads = []
        for i in range(3):
            piece = slice(i * width, (i + 1) * width)
            w_grads.append(jnp.concatenate([at_0[piece], at_1[piece]], axis=0).T)
        out_grad = jnp.concatenate([at_0[3 * width :], at_1[3 * width :]], axis=0)

        norms = jnp.concatenate([sums1[:2], sums2[:2], jnp.zeros((4, dim), F32)], axis=0)
        norms = norms + move(norms, by_core)
        norms = norms + move(norms, by_part)
        for how in by_chip:
            norms = norms + move(norms, how)
        return (
            mixed,
            tokens_grad,
            norms[0],
            norms[1],
            w_grads[0],
            w_grads[1],
            w_grads[2],
            out_grad,
            norms[2],
            norms[3],
            up_grad,
            down_grad,
        )

    return body


def solution(mesh):
    in_specs = (
        P(("dp", "tensor"), None),
        P("dp", None),
        P("dp", None),
        P(),
        P(),
        P(None, "tensor"),
        P(None, "tensor"),
        P(None, "tensor"),
        P("tensor", None),
        P(),
        P(),
        P(None, "tensor"),
        P("tensor", None),
        P(("dp", "tensor"), None),
    )
    out_specs = (
        P(("dp", "tensor"), None),
        P(("dp", "tensor"), None),
        P(),
        P(),
        P(None, "tensor"),
        P(None, "tensor"),
        P(None, "tensor"),
        P("tensor", None),
        P(),
        P(),
        P(None, "tensor"),
        P("tensor", None),
    )
    body = make_body(mesh.shape["dp"], mesh.shape["tensor"])
    return jax.shard_map(body, mesh=mesh, in_specs=in_specs, out_specs=out_specs, check_vma=False)
```

```python
import functools

import jax
import jax.numpy as jnp
from jax import lax
from jax.experimental import pallas as pl
from jax.experimental.pallas import tpu as pltpu
from jax.sharding import PartitionSpec as P

HEAD_DIM = 64
EPS = 1e-05
FAR = 1e30
FORWARD_BLOCK = 512
BF16 = jnp.bfloat16
F32 = jnp.float32
TN = (((0,), (0,)), ((), ()))
NT = (((1,), (1,)), ((), ()))
NN = (((1,), (0,)), ((), ()))
TT = (((0,), (1,)), ((), ()))
ERF_C = (
    1.5897294934128858e-07,
    -5.985900079472216e-06,
    8.971378204617447e-05,
    -0.0006257225011275588,
    -0.0001843806018428344,
    0.10276548023357895,
    1.1283797055884355,
)
ERF_X = tuple(c * 0.5 ** (6 - i) * 0.7071067811865476 for i, c in enumerate(ERF_C))


def dot(left, right, dims):
    return lax.dot_general(left, right, dims, preferred_element_type=F32)


def sds(shape, dtype):
    return jax.ShapeDtypeStruct(shape, dtype)


SMEM = pl.BlockSpec(memory_space=pltpu.SMEM)
VMEM = pl.BlockSpec(memory_space=pltpu.VMEM)
ANY = pl.BlockSpec(memory_space=pl.ANY)


WEIGHT = 20.0


class Order:
    def __init__(self):
        self.last = None

    def run(self, us, kernel, operands, out_shape, in_specs=None, after=(), **rest):
        after = tuple(after) + (() if self.last is None else (self.last,))
        count, extra = len(operands), len(after)
        in_specs = list(in_specs or [VMEM] * count) + [ANY] * extra

        def body(*refs):
            kernel(*refs[:count], *refs[count + extra :])

        out = pl.pallas_call(
            body,
            out_shape=out_shape,
            in_specs=in_specs,
            compiler_params=pltpu.CompilerParams(vmem_limit_bytes=58 << 20),
            cost_estimate=pl.CostEstimate(
                flops=int(us * WEIGHT * 1.15e9), bytes_accessed=0, transcendentals=0
            ),
            **rest,
        )(*operands, *after)
        self.last = out[-1] if isinstance(out, (list, tuple)) else out
        return out


def hold(value, after):
    def kernel(*refs):
        pass

    return pl.pallas_call(
        kernel,
        out_shape=sds(value.shape, value.dtype),
        in_specs=[ANY] * (1 + len(after)),
        out_specs=ANY,
        input_output_aliases={0: 0},
        compiler_params=pltpu.CompilerParams(has_side_effects=True),
        cost_estimate=pl.CostEstimate(flops=0, bytes_accessed=0, transcendentals=0),
    )(value, *after)


def whole(shape):
    return pl.BlockSpec(shape, lambda *_: (0,) * len(shape))


def normalize(values):
    center = values - jnp.mean(values, axis=-1, keepdims=True)
    inverse = lax.rsqrt(jnp.mean(center * center, axis=-1, keepdims=True) + EPS)
    return center * inverse, inverse


def norm_back(grad_normed, scaled, inverse, gain):
    grad_scaled = grad_normed * gain
    return inverse * (
        grad_scaled
        - jnp.mean(grad_scaled, axis=-1, keepdims=True)
        - scaled * jnp.mean(grad_scaled * scaled, axis=-1, keepdims=True)
    )


def gelu_pair(x):
    square = x * x
    near = jnp.minimum(square, 64.0)
    poly = ERF_X[0]
    for coefficient in ERF_X[1:]:
        poly = poly * near + coefficient
    phi = 0.5 * jnp.tanh(x * poly) + 0.5
    bell = jnp.exp(square * -0.5)
    return x * phi, phi + x * (bell * 0.3989422804014327)


def pack_first_kernel(place, w_query, w_key, w_value, qkv, qkv_send, first):
    width = qkv.shape[1] // 3
    half = qkv_send.shape[0]
    first[:, :HEAD_DIM] = w_query[:, :HEAD_DIM]
    first[:, HEAD_DIM:] = w_key[:, :HEAD_DIM]
    for core in range(2):

        @pl.when(place[0] == core)
        def _():
            narrow = slice(core * width, (core + 1) * width)
            for i, weight in enumerate((w_query, w_key, w_value)):
                qkv[:, i * width : (i + 1) * width] = weight[:, narrow]

    qkv_send[...] = qkv[pl.ds(pl.multiple_of(place[2] * half, half), half), :]


def pack_first_call(order, place, w_query, w_key, w_value):
    dim, width = w_query.shape[0], w_query.shape[1] // 2
    return order.run(
        4,
        pack_first_kernel,
        (place, w_query, w_key, w_value),
        [
            sds((dim, 3 * width), BF16),
            sds((dim // 2, 3 * width), BF16),
            sds((dim, 2 * HEAD_DIM), BF16),
        ],
        [SMEM] + [VMEM] * 3,
    )


def pack_last_kernel(place, w_out, w_up, w_down, grad, out, up, up_send, down, down_send, grad_out):
    width = out.shape[0]
    units = down.shape[0]
    half = units // 2
    grad_out[...] = grad[...]
    for core in range(2):

        @pl.when(place[0] == core)
        def _():
            wide = slice(core * units, (core + 1) * units)
            out[...] = w_out[core * width : (core + 1) * width, :]
            up[...] = w_up[:, wide]
            down[...] = w_down[wide, :]

    rows = pl.ds(pl.multiple_of(place[2] * half, half), half)
    up_send[...] = up[rows, :]
    down_send[...] = down[rows, :]


def pack_last_call(order, place, w_out, w_up, w_down, grad):
    width, dim = w_out.shape[0] // 2, w_out.shape[1]
    units = w_up.shape[1] // 2
    return order.run(
        5,
        pack_last_kernel,
        (place, w_out, w_up, w_down, grad),
        [
            sds((width, dim), BF16),
            sds((dim, units), BF16),
            sds((dim // 2, units), BF16),
            sds((units, dim), BF16),
            sds((units // 2, dim), BF16),
            sds(grad.shape, BF16),
        ],
        [SMEM] + [VMEM] * 4,
    )


def norm1_kernel(tokens, gain, shift, out):
    scaled, _ = normalize(tokens[...].astype(F32))
    out[...] = (scaled * gain[...] + shift[...]).astype(BF16)


def rows_spec(block, dim):
    return pl.BlockSpec((block, dim), lambda i: (i, 0))


def norm1_call(order, tokens, gain, shift):
    return order.run(2.5, norm1_kernel, (tokens, gain, shift), sds(tokens.shape, BF16))


def masks(seg_pad, cols, low, high):
    width = high - low
    seg_row = seg_pad[0:1, low:high]
    pad_row = seg_pad[1:2, low:high]
    row_key = jnp.where(pad_row > 0, seg_row, -2.0)
    col_seg = cols[:high, 0:1]
    col_pad = cols[:high, 1:2]
    col_key = jnp.where(col_pad > 0, col_seg, -1.0)
    key_at = lax.broadcasted_iota(jnp.int32, (high, width), 0)
    query_at = lax.broadcasted_iota(jnp.int32, (high, width), 1) + low
    allowed = ((col_key == seg_row) & (key_at <= query_at)) | (key_at == query_at)
    picked = (col_key == row_key) & (key_at < query_at)
    return allowed, picked


def penalty_kernel(
    block, place, n1_own, n1_other, first, first_moved, seg_pad, n1_out, penalty, qk0, first_out
):
    seq = n1_out.shape[0]
    half = seq // 2
    core = place[0]
    n1_out[pl.ds(pl.multiple_of(core * half, half), half), :] = n1_own[...]
    n1_out[pl.ds(pl.multiple_of((1 - core) * half, half), half), :] = n1_other[...]

    @pl.when(place[1] == 0)
    def _():
        first_out[...] = first[...]

    @pl.when(place[1] != 0)
    def _():
        first_out[...] = first_moved[...]

    qk = dot(first_out[...], n1_out[...], TT)
    q0 = (qk[:HEAD_DIM].astype(BF16) * 0.125).astype(BF16)
    k0 = qk[HEAD_DIM:].astype(BF16)
    qk0[:HEAD_DIM, :] = q0
    qk0[HEAD_DIM:, :] = k0
    seg_value = seg_pad[...]
    cols = seg_value.T
    earlier = lax.broadcasted_iota(jnp.int32, (block, block + 128), 0)
    later = lax.broadcasted_iota(jnp.int32, (block, block + 128), 1)
    sums = ((earlier < later) | (later >= block)).astype(F32).astype(BF16)
    carry = jnp.zeros((seq, 128), F32)
    for low in range(0, seq, block):
        high = low + block
        allowed, picked = masks(seg_value, cols, low, high)
        score = dot(k0[:, :high], q0[:, low:high], TN)
        small = jnp.exp(-jnp.abs(score))
        log1p = jnp.where(small < 1e-3, small - 0.5 * small * small, jnp.log(1.0 + small))
        select = jnp.where(picked, jnp.maximum(score, 0.0) + log1p, 0.0).astype(BF16)
        total = dot(select, sums, NN)
        before = jnp.concatenate([carry[:high]] * (block // 128), axis=1)
        penalty[:high, low:high] = jnp.where(allowed, total[:, :block] + before, FAR)
        if high % FORWARD_BLOCK:
            edge = high + FORWARD_BLOCK - high % FORWARD_BLOCK
            penalty[high:edge, low:high] = jnp.full((edge - high, block), FAR, F32)
        carry = jnp.concatenate([carry[:high] + total[:, block:], carry[high:]], axis=0)


def penalty_call(order, place, n1_own, n1_other, first, first_moved, seg_pad, after=()):
    half, dim = n1_own.shape
    seq = 2 * half
    return order.run(
        6.5,
        functools.partial(penalty_kernel, 256),
        (place, n1_own, n1_other, first, first_moved, seg_pad),
        [
            sds((seq, dim), BF16),
            sds((seq, seq), F32),
            sds((2 * HEAD_DIM, seq), BF16),
            sds(first.shape, BF16),
        ],
        [SMEM] + [VMEM] * 5,
        after,
    )


def forward_kernel(block, split, *refs):
    if split:
        place, n1, near, far, penalty, qkv, out, lse, weights = refs
    else:
        n1, weights, penalty, qkv, out, lse = refs
    head = pl.program_id(0)
    third = qkv.shape[0] // 3
    seq = qkv.shape[1]

    @pl.when(head == 0)
    def _():
        if split:
            join(place[2], weights, near, far)
        product = dot(weights[...], n1[...], TT).astype(BF16)
        qkv[:third, :] = (product[:third] * 0.125).astype(BF16)
        qkv[third:, :] = product[third:]

    at = pl.multiple_of(head * HEAD_DIM, HEAD_DIM)
    query = qkv[pl.ds(at, HEAD_DIM), :]
    key = qkv[pl.ds(third + at, HEAD_DIM), :]
    value = qkv[pl.ds(2 * third + at, HEAD_DIM), :]
    value = jnp.concatenate([value, jnp.ones((16, seq), BF16)], axis=0)
    for low in range(0, seq, block):
        high = low + block
        logits = dot(key[:, :high], query[:, low:high], TN) - penalty[:high, low:high]
        largest = jnp.max(logits, axis=0, keepdims=True)
        weight = jnp.exp(logits - largest).astype(BF16)
        result = dot(value[:, :high], weight, NN)
        total = result[HEAD_DIM : HEAD_DIM + 1, :]
        out[:, low:high] = (result[:HEAD_DIM] / total).astype(BF16)
        lse[:, low:high] = largest + jnp.log(total)


def join(bit, out, near, far):
    half = near.shape[0]
    out[pl.ds(pl.multiple_of(bit * half, half), half), :] = near[...]
    out[pl.ds(pl.multiple_of((1 - bit) * half, half), half), :] = far[...]


def forward_call(order, n1, weights, penalty, place=None, after=()):
    seq, dim = n1.shape
    split = place is not None
    width = weights[0].shape[1]
    heads = width // (3 * HEAD_DIM)
    operands = ((place,) if split else ()) + (n1,) + tuple(weights) + (penalty,)
    in_specs = [SMEM] if split else []
    in_specs += [whole(x.shape) for x in operands if x is not place]
    out_specs = [
        whole((width, seq)),
        pl.BlockSpec((HEAD_DIM, seq), lambda h: (h, 0)),
        pl.BlockSpec((None, 1, seq), lambda h: (h, 0, 0)),
    ]
    out_shape = [
        sds((width, seq), BF16),
        sds((heads * HEAD_DIM, seq), BF16),
        sds((heads, 1, seq), F32),
    ]
    if split:
        out_specs.append(whole((dim, width)))
        out_shape.append(sds((dim, width), BF16))
    return order.run(
        9.3,
        functools.partial(forward_kernel, FORWARD_BLOCK, split),
        operands,
        out_shape,
        in_specs,
        after,
        grid=(heads,),
        out_specs=out_specs,
    )


def project_kernel(place, out_l, out_r, w_l, w_r, own, send):
    half = own.shape[0]
    core = place[0]
    mixed = jnp.concatenate([w_l[...], w_r[...]], axis=0)

    def part(which):
        at = pl.ds(pl.multiple_of(which * half, half), half)
        heads = jnp.concatenate([out_l[:, at], out_r[:, at]], axis=0)
        return dot(heads, mixed, TN)

    send[...] = part(1 - core).astype(BF16)
    own[...] = part(core)


def project_call(order, place, out_l, out_r, w_l, w_r, after=()):
    half, dim = out_l.shape[1] // 2, w_l.shape[1]
    return order.run(
        3.5,
        project_kernel,
        (place, out_l, out_r, w_l, w_r),
        [sds((half, dim), F32), sds((half, dim), BF16)],
        [SMEM] + [VMEM] * 4,
        after,
    )


def norm2_kernel(tokens, own, received, gain, shift, hidden, out):
    total = tokens[...].astype(F32) + (own[...] + received[...].astype(F32))
    hidden[...] = total
    scaled, _ = normalize(total)
    out[...] = (scaled * gain[...] + shift[...]).astype(BF16)


def norm2_call(order, tokens, own, received, gain, shift, after=()):
    size, dim = tokens.shape
    rows = rows_spec(size // 4, dim)
    vector = whole((1, dim))
    return order.run(
        4,
        norm2_kernel,
        (tokens, own, received, gain, shift),
        [sds(tokens.shape, F32), sds(tokens.shape, BF16)],
        [rows] * 3 + [vector] * 2,
        after,
        grid=(4,),
        out_specs=[rows, rows],
    )


def mlp_kernel(first, steps, *refs):
    if first:
        n2_other, n2_own, g_other, g_own, w_up, w_down, *refs = refs
        mixed_send, mixed_own, back_send, back_own, up_grad, down_grad, *refs = refs
    else:
        place, n2_other, n2_own, g_other, g_own, *refs = refs
        up_near, up_far, down_near, down_far, *refs = refs
        mixed_in_send, mixed_in_own, back_in_send, back_in_own, down_l, *refs = refs
        mixed_send, mixed_own, back_send, back_own, up_grad, down_send, down_keep, *refs = refs
        w_up, w_down, *refs = refs
    rows, grads, actives, grad_ups = refs
    step = pl.program_id(0)
    block = n2_own.shape[0]
    early = step < steps // 2

    if not first:

        @pl.when(step == 0)
        def _():
            join(place[2], w_up, up_near, up_far)
            join(place[2], w_down, down_near, down_far)

    here = pl.ds(pl.multiple_of(step * block, block), block)
    row = jnp.where(early, n2_other[...], n2_own[...])
    grad = jnp.where(early, g_other[...], g_own[...])
    rows[here, :] = row
    grads[here, :] = grad
    active, slope = gelu_pair(dot(row, w_up[...], NN))
    active = active.astype(BF16)
    grad_up = (dot(grad, w_down[...], NT) * slope).astype(BF16)
    actives[here, :] = active
    grad_ups[here, :] = grad_up
    back = dot(grad_up, w_up[...], NT)
    mixed = dot(active, w_down[...], NN)

    @pl.when(early)
    def _():
        if first:
            back_send[...] = back.astype(back_send.dtype)
            mixed_send[...] = mixed.astype(mixed_send.dtype)
        else:
            back_send[...] = (back + back_in_send[...]).astype(back_send.dtype)
            mixed_send[...] = (mixed + mixed_in_send[...]).astype(mixed_send.dtype)

    @pl.when(jnp.logical_not(early))
    def _():
        if first:
            back_own[...] = back
            mixed_own[...] = mixed
        else:
            back_own[...] = back + back_in_own[...]
            mixed_own[...] = mixed + mixed_in_own[...]

    @pl.when(step == steps - 1)
    def _():
        up_grad[...] = dot(rows[...], grad_ups[...], TN).astype(BF16)
        down = dot(actives[...], grads[...], TN).astype(BF16)
        if first:
            down_grad[...] = down
        else:
            half = down.shape[0] // 2
            for bit in range(2):

                @pl.when(place[2] == bit)
                def _():
                    kept = slice(bit * half, (bit + 1) * half)
                    sent = slice((1 - bit) * half, (2 - bit) * half)
                    down_send[0] = down_l[sent, :]
                    down_send[1] = down[sent, :]
                    down_keep[0] = down_l[kept, :]
                    down_keep[1] = down[kept, :]


def mlp_call(order, n2_other, n2_own, g_other, g_own, weights, place=None, before=None, after=()):
    size, dim = n2_own.shape
    first = before is None
    units = weights[0].shape[1]
    block = min(256, size // 2)
    steps = 2 * size // block
    last = steps // 2 - 1
    sent = pl.BlockSpec((block, dim), lambda i: (jnp.minimum(i, last), 0))
    kept = pl.BlockSpec((block, dim), lambda i: (jnp.maximum(i - last - 1, 0), 0))
    operands = () if first else (place,)
    operands += (n2_other, n2_own, g_other, g_own) + tuple(weights)
    in_specs = [] if first else [SMEM]
    in_specs += [sent, kept, sent, kept] + [whole(weight.shape) for weight in weights]
    sent_type = F32 if first else BF16
    square = whole((dim, units))
    out_specs = [sent, kept, sent, kept, square]
    out_shape = [
        sds((size, dim), sent_type),
        sds((size, dim), F32),
        sds((size, dim), sent_type),
        sds((size, dim), F32),
        sds((dim, units), BF16),
    ]
    scratch = []
    if first:
        out_specs.append(whole((units, dim)))
        out_shape.append(sds((units, dim), BF16))
    else:
        operands += tuple(before)
        in_specs += [sent, kept, sent, kept, whole((units, dim))]
        out_specs += [whole((2, units // 2, dim))] * 2
        out_shape += [sds((2, units // 2, dim), BF16)] * 2
        scratch = [pltpu.VMEM((dim, units), BF16), pltpu.VMEM((units, dim), BF16)]
    tall = pltpu.VMEM((2 * size, dim), BF16)
    flat = pltpu.VMEM((2 * size, units), BF16)
    return order.run(
        14.6,
        functools.partial(mlp_kernel, first, steps),
        operands,
        out_shape,
        in_specs,
        after,
        grid=(steps,),
        out_specs=out_specs,
        scratch_shapes=scratch + [tall, tall, flat, flat],
    )


def norm2_back_kernel(hidden, own, received, grad, gain, grad_hidden, low, sums):
    normed_grad = own[...] + received[...].astype(F32)
    scaled, inverse = normalize(hidden[...])
    total = grad[...].astype(F32) + norm_back(normed_grad, scaled, inverse, gain[...])
    grad_hidden[...] = total
    low[...] = total.astype(BF16)
    add_sums(sums, normed_grad, scaled)


def add_sums(sums, normed_grad, scaled):
    @pl.when(pl.program_id(0) == 0)
    def _():
        sums[...] = jnp.zeros(sums.shape, F32)

    sums[0:1, :] += jnp.sum(normed_grad * scaled, axis=0, keepdims=True)
    sums[1:2, :] += jnp.sum(normed_grad, axis=0, keepdims=True)


def norm2_back_call(order, hidden, own, received, grad, gain, after=()):
    size, dim = hidden.shape
    rows = rows_spec(size // 4, dim)
    return order.run(
        5,
        norm2_back_kernel,
        (hidden, own, received, grad, gain),
        [sds(hidden.shape, F32), sds(hidden.shape, BF16), sds((8, dim), F32)],
        [rows] * 4 + [whole((1, dim))],
        after,
        grid=(4,),
        out_specs=[rows, rows, whole((8, dim))],
    )


def mixed_kernel(hidden, own, received, out):
    out[...] = (hidden[...] + (own[...] + received[...].astype(F32))).astype(BF16)


def mixed_call(order, hidden, own, received, after=()):
    size, dim = hidden.shape
    rows = rows_spec(size // 2, dim)
    return order.run(
        3,
        mixed_kernel,
        (hidden, own, received),
        sds(hidden.shape, BF16),
        [rows] * 3,
        after,
        grid=(2,),
        out_specs=rows,
    )


def backward_kernel(start, heads, first, final, wide, block, *refs):
    place, g_own, g_other, w_out, *refs = refs
    if wide:
        heads_out, *refs = refs
    qkv, lse, penalty, *refs = refs
    if not first:
        before, *refs = refs
    grads, *refs = refs
    if wide:
        w_grad, *refs = refs
    logit_sum, grad_full, grad_heads, key_sum, value_sum, *refs = refs
    head = pl.program_id(0)
    third = qkv.shape[0] // 3
    seq = qkv.shape[1]
    half = seq // 2
    total = refs[0] if final and heads > 1 else logit_sum

    @pl.when(head == 0)
    def _():
        core = place[0]
        grad_full[pl.ds(pl.multiple_of(core * half, half), half), :] = g_own[...]
        grad_full[pl.ds(pl.multiple_of((1 - core) * half, half), half), :] = g_other[...]
        whole_grad = grad_full[...]
        rows = slice(start * HEAD_DIM, (start + heads) * HEAD_DIM)
        grad_heads[...] = dot(w_out[rows, :], whole_grad, NT).astype(BF16)
        if wide:
            w_grad[...] = dot(heads_out[...], whole_grad, NN).astype(BF16)

    out_at = pl.multiple_of(head * HEAD_DIM, HEAD_DIM)
    at = pl.multiple_of((start + head) * HEAD_DIM, HEAD_DIM)
    size = heads * HEAD_DIM
    query = qkv[pl.ds(at, HEAD_DIM), :]
    key = qkv[pl.ds(third + at, HEAD_DIM), :]
    value = qkv[pl.ds(2 * third + at, HEAD_DIM), :]
    grad = grad_heads[pl.ds(out_at, HEAD_DIM), :]
    for low in range(0, seq, block):
        high = low + block
        cols = slice(low, high)
        score = dot(key[:, :high], query[:, cols], TN)
        probs = jnp.exp(score - penalty[:high, cols] - lse[:, cols])
        grad_probs = dot(value[:, :high], grad[:, cols], TN)
        row_dot = jnp.sum(probs * grad_probs, axis=0, keepdims=True)
        grad_logits = probs * (grad_probs - row_dot)
        if final and heads == 1:
            if first:
                logit_sum[:high, cols] = grad_logits.astype(logit_sum.dtype)
            else:
                logit_sum[:high, cols] = (before[:high, cols] + grad_logits).astype(BF16)
        else:

            @pl.when(head == 0)
            def _():
                if first:
                    total[:high, cols] = grad_logits
                else:
                    total[:high, cols] = before[:high, cols] + grad_logits

            @pl.when(head > 0)
            def _():
                total[:high, cols] += grad_logits

        low_logits = grad_logits.astype(BF16)
        low_probs = probs.astype(BF16)
        grads[pl.ds(out_at, HEAD_DIM), cols] = (
            dot(key[:, :high], low_logits, NN) * 0.125
        ).astype(BF16)
        value_new = dot(grad[:, cols], low_probs, NT)
        key_new = dot(query[:, cols], low_logits, NT)
        if low:
            key_sum[:, :low] += key_new[:, :low]
            value_sum[:, :low] += value_new[:, :low]
        key_sum[:, cols] = key_new[:, low:]
        value_sum[:, cols] = value_new[:, low:]
    grads[pl.ds(size + out_at, HEAD_DIM), :] = key_sum[...].astype(BF16)
    grads[pl.ds(2 * size + out_at, HEAD_DIM), :] = value_sum[...].astype(BF16)
    if final and heads > 1:

        @pl.when(head == heads - 1)
        def _():
            for low in range(0, seq, block):
                high = low + block
                logit_sum[:high, low:high] = total[:high, low:high].astype(BF16)


def backward_call(
    order, place, g_own, g_other, w_out, heads_out, qkv, lse, penalty, start, heads, before, final
):
    width, seq = qkv.shape
    half, dim = g_own.shape
    first, wide = before is None, heads_out is not None
    square = whole((seq, seq))
    operands = (place, g_own, g_other, w_out) + ((heads_out,) if wide else ())
    in_specs = [SMEM] + [whole(x.shape) for x in operands[1:]]
    operands += (qkv, lse, penalty)
    in_specs += [
        whole((width, seq)),
        pl.BlockSpec((None, 1, seq), lambda h: (h + start, 0, 0)),
        square,
    ]
    if not first:
        operands += (before,)
        in_specs.append(square)
    size = heads * HEAD_DIM
    out_specs = [whole((3 * size, seq))]
    out_shape = [sds((3 * size, seq), BF16)]
    if wide:
        out_specs.append(whole(w_out.shape))
        out_shape.append(sds(w_out.shape, BF16))
    out_specs.append(square)
    out_shape.append(sds((seq, seq), BF16 if final else F32))
    scratch = [
        pltpu.VMEM((seq, dim), BF16),
        pltpu.VMEM((size, seq), BF16),
        pltpu.VMEM((HEAD_DIM, seq), F32),
        pltpu.VMEM((HEAD_DIM, seq), F32),
    ]
    if final and heads > 1:
        scratch.append(pltpu.VMEM((seq, seq), F32))
    return order.run(
        5.5 * heads,
        functools.partial(backward_kernel, start, heads, first, final, wide, 256),
        operands,
        out_shape,
        in_specs,
        grid=(heads,),
        out_specs=out_specs,
        scratch_shapes=scratch,
    )


def halves(value):
    high = value.astype(BF16)
    return high, (value - high.astype(F32)).astype(BF16)


def select_back_kernel(block, place, own, received, qk0, seg_pad, n1, out, w_grad, total_grad):
    seq = own.shape[0]
    q0 = qk0[:HEAD_DIM, :]
    k0 = qk0[HEAD_DIM:, :]
    seg_value = seg_pad[...]
    cols = seg_value.T
    later = lax.broadcasted_iota(jnp.int32, (block, block + 128), 0)
    earlier = lax.broadcasted_iota(jnp.int32, (block, block + 128), 1)
    sums = ((later > earlier) | (earlier >= block)).astype(F32).astype(BF16)
    carry = jnp.zeros((seq, 128), F32)
    total_grad[...] = jnp.zeros(total_grad.shape, F32)
    for low in range(seq - block, -1, -block):
        high = low + block
        logit_sum = own[:high, low:high].astype(F32) + received[:high, low:high].astype(F32)
        top, bottom = halves(logit_sum)
        total = dot(top, sums, NN) + dot(bottom, sums, NN)
        after = jnp.concatenate([carry[:high]] * (block // 128), axis=1)
        select_grad = -(total[:, :block] + after)
        carry = carry[:high] + total[:, block:]
        _, picked = masks(seg_value, cols, low, high)
        score = dot(k0[:, :high], q0[:, low:high], TN)
        through = jnp.where(picked, select_grad / (1.0 + jnp.exp(-score)), 0.0)
        top, bottom = halves(through)
        total_grad[:HEAD_DIM, low:high] = 0.125 * (
            dot(k0[:, :high], top, NN) + dot(k0[:, :high], bottom, NN)
        )
        total_grad[HEAD_DIM:, :high] += dot(q0[:, low:high], top, NT) + dot(
            q0[:, low:high], bottom, NT
        )
    out[...] = jnp.where(place[0] == 0, total_grad[...], 0.0).astype(BF16)
    w_grad[...] = dot(out[...], n1[...], NN).astype(BF16)


def select_back_call(order, place, own, received, qk0, seg_pad, n1, after=()):
    return order.run(
        8.4,
        functools.partial(select_back_kernel, 256),
        (place, own, received, qk0, seg_pad, n1),
        [sds(qk0.shape, BF16), sds((qk0.shape[0], n1.shape[1]), BF16)],
        [SMEM] + [VMEM] * 5,
        after,
        scratch_shapes=[pltpu.VMEM(qk0.shape, F32)],
    )


def weights_first_kernel(place, n1, grads, weights, w_out, back, send, keep, late):
    width = grads.shape[0]
    third = width // 3
    half = keep.shape[0]
    early_out = 2 * half - 2 * (width // 3 - HEAD_DIM) - (third - HEAD_DIM)
    product = dot(grads[...], n1[...], NN).astype(BF16)
    tail = w_out[...]
    early = [product[i * third + HEAD_DIM : (i + 1) * third] for i in range(3)]
    early = jnp.concatenate(early + [tail[:early_out]], axis=0)
    for i in range(3):
        late[i * HEAD_DIM : (i + 1) * HEAD_DIM, :] = product[i * third : i * third + HEAD_DIM]
    late[3 * HEAD_DIM :, :] = tail[early_out:]
    for bit in range(2):

        @pl.when(place[2] == bit)
        def _():
            keep[...] = early[bit * half : (bit + 1) * half]
            send[...] = early[(1 - bit) * half : (2 - bit) * half]

    back[...] = dot(grads[...], weights[...], TT)


def weights_first_call(order, place, n1, grads, weights, w_out):
    seq, dim = n1.shape
    late = 4 * HEAD_DIM
    half = (grads.shape[0] + w_out.shape[0] - late) // 2
    return order.run(
        6,
        weights_first_kernel,
        (place, n1, grads, weights, w_out),
        [
            sds((seq, dim), F32),
            sds((half, dim), BF16),
            sds((half, dim), BF16),
            sds((late, dim), BF16),
        ],
        [SMEM] + [VMEM] * 4,
    )


def weights_middle_kernel(place, n1, grads, w_out, send, keep):
    half = keep.shape[0]
    product = dot(grads[...], n1[...], NN).astype(BF16)
    early = jnp.concatenate([product, w_out[: 2 * half - product.shape[0], :]], axis=0)
    for bit in range(2):

        @pl.when(place[2] == bit)
        def _():
            keep[...] = early[bit * half : (bit + 1) * half]
            send[...] = early[(1 - bit) * half : (2 - bit) * half]


def weights_middle_call(order, place, n1, grads, w_out):
    dim = n1.shape[1]
    half = (grads.shape[0] + w_out.shape[0] - HEAD_DIM) // 2
    return order.run(
        3,
        weights_middle_kernel,
        (place, n1, grads, w_out),
        [sds((half, dim), BF16)] * 2,
        [SMEM] + [VMEM] * 3,
    )


def weights_last_kernel(
    place, n1, grads_one, grads_rest, extra, weights, first, before, w_out, own, send, late
):
    half = own.shape[0]
    core = place[0]
    rest = grads_rest.shape[0] // 3
    pieces = []
    for i in range(3):
        pieces.append(grads_one[i * HEAD_DIM : (i + 1) * HEAD_DIM, :])
        pieces.append(grads_rest[i * rest : (i + 1) * rest, :])
    grads = jnp.concatenate(pieces, axis=0)
    late[: 3 * HEAD_DIM, :] = dot(grads_one[...], n1[...], NN)
    late[3 * HEAD_DIM :, :] = w_out[w_out.shape[0] - HEAD_DIM :, :].astype(F32)
    total = before[...] + dot(grads, weights[...], TT) + dot(extra[...], first[...], TT)

    for which in range(2):

        @pl.when(core == which)
        def _():
            own[...] = total[which * half : (which + 1) * half]
            send[...] = total[(1 - which) * half : (2 - which) * half].astype(BF16)


def weights_last_call(order, place, n1, grads_one, grads_rest, extra, weights, first, before, w_out):
    seq, dim = n1.shape
    return order.run(
        7,
        weights_last_kernel,
        (place, n1, grads_one, grads_rest, extra, weights, first, before, w_out),
        [
            sds((seq // 2, dim), F32),
            sds((seq // 2, dim), BF16),
            sds((4 * HEAD_DIM, dim), F32),
        ],
        [SMEM] + [VMEM] * 8,
    )


def norm1_back_kernel(tokens, own, received, grad_hidden, gain, out, sums):
    normed_grad = own[...] + received[...].astype(F32)
    scaled, inverse = normalize(tokens[...].astype(F32))
    total = grad_hidden[...] + norm_back(normed_grad, scaled, inverse, gain[...])
    out[...] = total.astype(BF16)
    add_sums(sums, normed_grad, scaled)


def norm1_back_call(order, tokens, own, received, grad_hidden, gain, after=()):
    size, dim = tokens.shape
    rows = rows_spec(size // 4, dim)
    return order.run(
        4.6,
        norm1_back_kernel,
        (tokens, own, received, grad_hidden, gain),
        [sds(tokens.shape, BF16), sds((8, dim), F32)],
        [rows] * 4 + [whole((1, dim))],
        after,
        grid=(4,),
        out_specs=[rows, whole((8, dim))],
    )


def low_sum(*terms):
    total = terms[0].astype(F32)
    for term in terms[1:]:
        total = total + term.astype(F32)
    return total.astype(BF16)


def split(place, bit, terms, keep, send):
    half = keep.shape[1]
    for out, which in ((keep, place[2 + bit]), (send, 1 - place[2 + bit])):
        rows = pl.ds(pl.multiple_of(which * half, half), half)
        out[...] = low_sum(*(term[:, rows, :] for term in terms))


def merge(place, bit, near, far, out):
    half = near.shape[1]
    for part, which in ((near, place[2 + bit]), (far, 1 - place[2 + bit])):
        out[:, pl.ds(pl.multiple_of(which * half, half), half), :] = part[...]


def step1_kernel(place, down_keep, down_got, up_l, up_got, down_near, down_move, up_keep, up_send):
    total = low_sum(down_keep[...], down_got[...])
    down_near[...] = total[0]
    down_move[...] = total[1]
    split(place, 0, (up_l, up_got), up_keep, up_send)


def step1_call(order, place, down_keep, down_got, up_l, up_got):
    _, half, dim = down_keep.shape
    return order.run(
        3,
        step1_kernel,
        (place, down_keep, down_got, up_l, up_got),
        [sds((half, dim), BF16)] * 2 + [sds((1, half, dim), BF16)] * 2,
        [SMEM] + [VMEM] * 4,
    )


def step2_kernel(place, at_keep, at_got, up_keep, up_got, near, got, at_move, ff_keep, ff_send, total):
    at_move[...] = low_sum(at_keep[...], at_got[...])
    total[0] = low_sum(up_keep[0], up_got[0])
    total[1] = low_sum(near[...], got[...])
    split(place, 1, (total,), ff_keep, ff_send)


def step2_call(order, place, at_keep, at_got, up_keep, up_got, near, got):
    half, dim = near.shape
    return order.run(
        3,
        step2_kernel,
        (place, at_keep, at_got, up_keep, up_got, near, got),
        [sds(at_keep.shape, BF16)] + [sds((2, half // 2, dim), BF16)] * 2,
        [SMEM] + [VMEM] * 6,
        scratch_shapes=[pltpu.VMEM((2, half, dim), BF16)],
    )


def step3_kernel(at_keep, at_got, at_got_r, ff_keep, ff_got, at, ff):
    at[...] = low_sum(at_keep[...], at_got[...], at_got_r[...])
    ff[...] = low_sum(ff_keep[...], ff_got[...])


def step3_call(order, at_terms, ff_terms):
    return order.run(
        3,
        step3_kernel,
        (*at_terms, *ff_terms),
        [sds(at_terms[0].shape, BF16), sds(ff_terms[0].shape, BF16)],
    )


def step4_kernel(place, late, late_got, extra_own, extra_moved, at_own, at_got, ff_own, ff_got, *outs):
    late_out, at, ff = outs
    at[...] = low_sum(at_own[...], at_got[...])
    ff[...] = low_sum(ff_own[...], ff_got[...])
    rows = extra_own.shape[0]
    ours = ((place[0] == 0) & (place[1] == 0)).astype(F32)
    total = late[...] + late_got[...].astype(F32)
    extra = extra_own[...].astype(F32) + extra_moved[...].astype(F32)
    late_out[:rows, :] = (total[:rows] + ours * extra).astype(BF16)
    late_out[rows:, :] = total[rows:].astype(BF16)


def step4_call(order, place, late, late_got, extra_own, extra_moved, at_terms, ff_terms):
    return order.run(
        3.5,
        step4_kernel,
        (place, late, late_got, extra_own, extra_moved, *at_terms, *ff_terms),
        [sds(late.shape, BF16), sds(at_terms[0].shape, BF16), sds(ff_terms[0].shape, BF16)],
        [SMEM] + [VMEM] * 8,
    )


def step5_kernel(place, late_own, late_got, norms_own, norms_got, at_own, at_got, ff_near, ff_far, *outs):
    late, at, ff = outs
    rows = late_own.shape[0]
    late[:rows, :] = low_sum(late_own[...], late_got[...])
    high, low = halves(norms_own[...] + norms_got[...])
    late[rows : rows + 8, :] = high
    late[rows + 8 :, :] = low
    at[...] = low_sum(at_own[...], at_got[...])
    merge(place, 1, ff_near, ff_far, ff)


def step5_call(order, place, late_terms, norms_terms, at_terms, ff_near, ff_far):
    rows, dim = late_terms[0].shape
    groups, size, _ = ff_near.shape
    return order.run(
        3.5,
        step5_kernel,
        (place, *late_terms, *norms_terms, *at_terms, ff_near, ff_far),
        [
            sds((rows + 16, dim), BF16),
            sds(at_terms[0].shape, BF16),
            sds((groups, 2 * size, dim), BF16),
        ],
        [SMEM] + [VMEM] * 8,
    )


def add_late(own, got, out):
    rows = own.shape[0] - 16
    out[:rows, :] = low_sum(own[:rows, :], got[:rows, :])

    def norms(ref):
        return ref[rows : rows + 8, :].astype(F32) + ref[rows + 8 :, :].astype(F32)

    high, low = halves(norms(own) + norms(got))
    out[rows : rows + 8, :] = high
    out[rows + 8 :, :] = low


def step6_kernel(place, late_own, late_got, at_near, at_far, ff_near, ff_far, late, at, ff):
    add_late(late_own, late_got, late)
    merge(place, 0, at_near, at_far, at)
    merge(place, 0, ff_near, ff_far, ff)


def step6_call(order, place, late_terms, at_near, at_far, ff_near, ff_far):
    dim = at_near.shape[2]
    groups, size, _ = ff_near.shape
    return order.run(
        3.5,
        step6_kernel,
        (place, *late_terms, at_near, at_far, ff_near, ff_far),
        [
            sds(late_terms[0].shape, BF16),
            sds((1, 2 * at_near.shape[1], dim), BF16),
            sds((groups, 2 * size, dim), BF16),
        ],
        [SMEM] + [VMEM] * 6,
    )


def step7_kernel(late_own, late_got, mixed, grad, late, mixed_out, grad_out):
    add_late(late_own, late_got, late)
    mixed_out[...] = mixed[...]
    grad_out[...] = grad[...]


def step7_call(order, late_terms, mixed, grad):
    shape = sds(mixed.shape, BF16)
    return order.run(
        2.5,
        step7_kernel,
        (*late_terms, mixed, grad),
        [sds(late_terms[0].shape, BF16), shape, shape],
    )


def finish_attention_kernel(place, near, far, late_near, late_far, w_query, w_key, w_value, w_out, norms):
    width = w_out.shape[0] // 2
    early = near.shape[0]
    pair = width - HEAD_DIM
    rows = 4 * HEAD_DIM
    total = jnp.zeros(norms.shape, F32)
    for ref in (late_near, late_far):
        total = total + (ref[rows : rows + 8, :].astype(F32) + ref[rows + 8 :, :].astype(F32))
    norms[...] = total
    for core in range(2):

        @pl.when(place[0] == core)
        def _():
            low, high = ((near, late_near), (far, late_far))[:: 1 if core == 0 else -1]
            for i, out in enumerate((w_query, w_key, w_value)):
                one = slice(i * HEAD_DIM, (i + 1) * HEAD_DIM)
                rest = slice(i * pair, (i + 1) * pair)
                both = [low[1][one, :], low[0][rest, :], high[1][one, :], high[0][rest, :]]
                out[...] = jnp.concatenate(both, axis=0).astype(F32).T
            for at, (most, last) in ((0, low), (width, high)):
                edge = at + early - 3 * pair
                w_out[at:edge, :] = most[3 * pair :, :].astype(F32)
                w_out[edge : at + width, :] = last[3 * HEAD_DIM : rows, :].astype(F32)


def finish_attention_call(order, place, near, far, late_near, late_far):
    rows, dim = near.shape
    width = (rows + 4 * HEAD_DIM) // 4
    return order.run(
        4.5,
        finish_attention_kernel,
        (place, near, far, late_near, late_far),
        [sds((dim, 2 * width), F32)] * 3 + [sds((2 * width, dim), F32), sds((8, dim), F32)],
        [SMEM] + [VMEM] * 4,
    )


def finish_mlp_kernel(place, near, far, w_up, w_down):
    units = near.shape[1]
    for core in range(2):

        @pl.when(place[0] == core)
        def _():
            low, high = (near, far) if core == 0 else (far, near)
            w_up[:, :units] = low[0].astype(F32)
            w_up[:, units:] = high[0].astype(F32)
            w_down[:units, :] = low[1].astype(F32)
            w_down[units:, :] = high[1].astype(F32)


def finish_mlp_call(order, place, near, far):
    _, units, dim = near.shape
    return order.run(
        6.8,
        finish_mlp_kernel,
        (place, near, far),
        [sds((dim, 2 * units), F32), sds((2 * units, dim), F32)],
        [SMEM] + [VMEM] * 2,
    )


def make_body(devices, parts):
    axes = ("dp", "tensor")
    chips = devices // 2
    in_order = [1 << bit for bit in range(chips.bit_length() - 1)]
    turned = in_order[1:] + in_order[:1]
    rounds = len(in_order)
    rounds_more = range(3, rounds)

    def pairs(move):
        found = []
        for device in range(devices):
            for part in range(parts):
                to_chip, to_core, to_part = move(device // 2, device % 2, part)
                source = device * parts + part
                found.append((source, (to_chip * 2 + to_core) * parts + to_part))
        return found

    def by_bit(bit):
        return pairs(
            lambda chip, core, part: (chip ^ (turned if core else in_order)[bit], core, part)
        )

    by_role = pairs(lambda chip, core, part: (chip, part, core))
    by_core = pairs(lambda chip, core, part: (chip, 1 - core, part))
    by_part = pairs(lambda chip, core, part: (chip, core, 1 - part))
    from_first_part = [pair for pair in by_part if pair[0] % parts == 0]
    extra_to_first = [
        pair for pair in by_part if pair[0] % parts == 1 and (pair[0] // parts) % 2 == 0
    ]
    to_first_core = [pair for pair in by_core if (pair[0] // parts) % 2 == 1]
    by_chip = [by_bit(bit) for bit in range(rounds)]

    def move(value, how):
        return lax.ppermute(value, axes, how)

    def add_more(value):
        for bit in rounds_more:
            other = move(value, by_chip[bit])
            value = (value.astype(F32) + other.astype(F32)).astype(value.dtype)
        return value

    def body(
        tokens,
        segment_ids,
        pad_mask,
        norm1_gain,
        norm1_shift,
        w_query,
        w_key,
        w_value,
        w_out,
        norm2_gain,
        norm2_shift,
        w_up,
        w_down,
        cotangent,
    ):
        order = Order()
        device = lax.axis_index("dp")
        part = lax.axis_index("tensor")
        core = device % 2
        chip = device // 2
        bits = [
            jnp.where(core == 1, (chip & turned[i]) != 0, (chip & in_order[i]) != 0)
            for i in range(rounds)
        ]
        place = jnp.stack([core, part] + bits).astype(jnp.int32)
        gain1, shift1, gain2, shift2 = (
            vector[None, :] for vector in (norm1_gain, norm1_shift, norm2_gain, norm2_shift)
        )

        mine = move(tokens, by_role)
        ints = jnp.concatenate([segment_ids, pad_mask], axis=0)
        ints = jnp.where(core == part, ints, move(ints, by_core)).astype(F32)
        seg_pad = jnp.concatenate([ints, jnp.zeros((6, ints.shape[1]), F32)], axis=0)

        qkv_l, qkv_s, first = pack_first_call(order, place, w_query, w_key, w_value)
        first_moved = move(first, from_first_part)
        qkv_near = move(qkv_s, by_part)
        n1_own = norm1_call(order, mine, gain1, shift1)
        n1_other = move(n1_own, by_core)
        out_l, up_l, up_s, down_l, down_s, grad = pack_last_call(
            order, place, w_out, w_up, w_down, cotangent
        )
        out_r = move(out_l, by_part)
        up_near = move(up_s, by_part)
        grad_own = move(grad, by_role)
        down_near = move(down_s, by_part)
        n1, penalty, qk0, first = penalty_call(
            order, place, n1_own, n1_other, first, first_moved, seg_pad
        )
        qkv_near = hold(qkv_near, (penalty,))
        qkv_far = move(qkv_near, by_chip[0])
        qkvt_l, heads_l, lse_l = forward_call(order, n1, (qkv_l,), penalty)
        qkvt_r, heads_r, lse_r, qkv_r = forward_call(
            order, n1, (qkv_near, qkv_far), penalty, place, after=(up_near,)
        )
        up_near = hold(up_near, (lse_r,))
        up_far = move(up_near, by_chip[0])
        grad_own = hold(grad_own, (lse_r,))
        grad_other = move(grad_own, by_core)
        own, send = project_call(order, place, heads_l, heads_r, out_l, out_r, after=(down_near,))
        down_near = hold(down_near, (send,))
        down_far = move(down_near, by_chip[0])
        hidden, n2_own = norm2_call(order, mine, own, move(send, by_core), gain2, shift2)
        n2_other = move(n2_own, by_core)
        mixed_send, mixed_own, back_send, back_own, up_sum_l, down_sum_l = mlp_call(
            order, n2_other, n2_own, grad_other, grad_own, (up_l, down_l)
        )
        before = (mixed_send, mixed_own, back_send, back_own, down_sum_l)
        mixed_send, mixed_own, back_send, back_own, up_sum_r, down_send, down_keep = mlp_call(
            order,
            n2_other,
            n2_own,
            grad_other,
            grad_own,
            (up_near, up_far, down_near, down_far),
            place,
            before,
        )
        down_got = move(down_send, by_chip[0])
        up_got = move(up_sum_r, by_part)

        grad_hidden, low_own, sums2 = norm2_back_call(
            order, hidden, back_own, move(back_send, by_core), grad_own, gain2
        )
        low_other = move(low_own, by_core)
        mixed = mixed_call(order, hidden, mixed_own, move(mixed_send, by_core))
        mixed = move(mixed, by_role)

        low = (low_own, low_other)
        grads_r, wo_r, logit_sum = backward_call(
            order, place, *low, out_r, heads_r, qkvt_r, lse_r, penalty, 0, 3, None, False
        )
        back, at_send_r, at_keep_r, late_r = weights_first_call(
            order, place, n1, grads_r, qkv_r, wo_r
        )
        late_got = move(late_r, by_part)
        at_got_r = move(at_send_r, by_chip[0])
        down_near, down_move, up_keep, up_send = step1_call(
            order, place, down_keep, down_got, up_sum_l[None], up_got[None]
        )
        down_got = move(down_move, by_part)
        up_got = move(up_send, by_chip[0])
        grads_rest, wo_l, logit_sum = backward_call(
            order, place, *low, out_l, heads_l, qkvt_l, lse_l, penalty, 1, 2, logit_sum, False
        )
        at_send, at_keep = weights_middle_call(order, place, n1, grads_rest, wo_l)
        at_got = move(at_send, by_chip[0])
        at_r, ff, ff_send = step2_call(
            order, place, at_keep_r, at_got_r, up_keep, up_got, down_near, down_got
        )
        at_got_r = move(at_r, by_part)
        ff_got = move(ff_send, by_chip[1])
        grads_one, logit_sum = backward_call(
            order, place, *low, out_l, None, qkvt_l, lse_l, penalty, 0, 1, logit_sum, True
        )
        logit_got = move(logit_sum, to_first_core)
        at, ff = step3_call(order, (at_keep[None], at_got[None], at_got_r[None]), (ff, ff_got))
        at_got = move(at, by_chip[1])
        ff_got = move(ff, by_chip[2])
        extra, extra_w = select_back_call(order, place, logit_sum, logit_got, qk0, seg_pad, n1)
        extra_moved = move(extra_w, extra_to_first)
        own, send, late = weights_last_call(
            order, place, n1, grads_one, grads_rest, extra, qkv_l, first, back, wo_l
        )
        received = move(send, by_core)
        late, at, ff = step4_call(
            order, place, late, late_got, extra_w, extra_moved, (at, at_got), (ff, ff_got)
        )
        late_got = move(late, by_chip[0])
        at_got = move(at, by_chip[2])
        ff = add_more(ff)
        ff_far = move(ff, by_chip[1])
        tokens_grad, sums1 = norm1_back_call(order, mine, own, received, grad_hidden, gain1)
        tokens_grad = move(tokens_grad, by_role)
        norms = jnp.concatenate([sums1[:2], sums2[:2], sums1[4:]], axis=0)
        norms = norms + move(norms, by_part)
        norms_got = move(norms, by_chip[0])
        late, at, ff = step5_call(
            order, place, (late, late_got), (norms, norms_got), (at, at_got), ff, ff_far
        )
        late_got = move(late, by_chip[1])
        at = add_more(at)
        at_far = move(at, by_chip[0])
        ff_far = move(ff, by_chip[0])
        late, at, ff = step6_call(order, place, (late, late_got), at, at_far, ff, ff_far)
        late_got = move(late, by_chip[2])
        at_far = move(at, by_core)
        ff_far = move(ff, by_core)
        up_grad, down_grad = finish_mlp_call(order, place, ff, ff_far)
        late, mixed, tokens_grad = step7_call(order, (late, late_got), mixed, tokens_grad)
        late = add_more(late)
        query_grad, key_grad, value_grad, out_grad, norms = finish_attention_call(
            order, place, at[0], at_far[0], late, move(late, by_core)
        )
        return (
            mixed,
            tokens_grad,
            norms[0],
            norms[1],
            query_grad,
            key_grad,
            value_grad,
            out_grad,
            norms[2],
            norms[3],
            up_grad,
            down_grad,
        )

    return body


def solution(mesh):
    in_specs = (
        P(("dp", "tensor"), None),
        P("dp", None),
        P("dp", None),
        P(),
        P(),
        P(None, "tensor"),
        P(None, "tensor"),
        P(None, "tensor"),
        P("tensor", None),
        P(),
        P(),
        P(None, "tensor"),
        P("tensor", None),
        P(("dp", "tensor"), None),
    )
    out_specs = (
        P(("dp", "tensor"), None),
        P(("dp", "tensor"), None),
        P(),
        P(),
        P(None, "tensor"),
        P(None, "tensor"),
        P(None, "tensor"),
        P("tensor", None),
        P(),
        P(),
        P(None, "tensor"),
        P("tensor", None),
    )
    body = make_body(mesh.shape["dp"], mesh.shape["tensor"])
    return jax.shard_map(body, mesh=mesh, in_specs=in_specs, out_specs=out_specs, check_vma=False)
```

```python
import functools

import jax
import jax.numpy as jnp
from jax import lax
from jax.experimental import pallas as pl
from jax.experimental.pallas import tpu as pltpu
from jax.sharding import PartitionSpec as P

HEAD_DIM = 64
EPS = 1e-05
FAR = 1e30
FORWARD_BLOCK = 512
BF16 = jnp.bfloat16
F32 = jnp.float32
TN = (((0,), (0,)), ((), ()))
NT = (((1,), (1,)), ((), ()))
NN = (((1,), (0,)), ((), ()))
TT = (((0,), (1,)), ((), ()))
ERF_C = (
    1.5897294934128858e-07,
    -5.985900079472216e-06,
    8.971378204617447e-05,
    -0.0006257225011275588,
    -0.0001843806018428344,
    0.10276548023357895,
    1.1283797055884355,
)
ERF_X = tuple(c * 0.5 ** (6 - i) * 0.7071067811865476 for i, c in enumerate(ERF_C))


def dot(left, right, dims):
    return lax.dot_general(left, right, dims, preferred_element_type=F32)


def sds(shape, dtype):
    return jax.ShapeDtypeStruct(shape, dtype)


SMEM = pl.BlockSpec(memory_space=pltpu.SMEM)
VMEM = pl.BlockSpec(memory_space=pltpu.VMEM)
ANY = pl.BlockSpec(memory_space=pl.ANY)


WEIGHT = 20.0


class Order:
    def __init__(self):
        self.last = None

    def run(self, us, kernel, operands, out_shape, in_specs=None, after=(), **rest):
        after = tuple(after) + (() if self.last is None else (self.last,))
        count, extra = len(operands), len(after)
        in_specs = list(in_specs or [VMEM] * count) + [ANY] * extra

        def body(*refs):
            kernel(*refs[:count], *refs[count + extra :])

        out = pl.pallas_call(
            body,
            out_shape=out_shape,
            in_specs=in_specs,
            compiler_params=pltpu.CompilerParams(vmem_limit_bytes=58 << 20),
            cost_estimate=pl.CostEstimate(
                flops=int(us * WEIGHT * 1.15e9), bytes_accessed=0, transcendentals=0
            ),
            **rest,
        )(*operands, *after)
        self.last = out[-1] if isinstance(out, (list, tuple)) else out
        return out

    def hold(self, values, after):
        count = len(values)

        def kernel(*refs):
            pass

        held = pl.pallas_call(
            kernel,
            out_shape=[sds(value.shape, value.dtype) for value in values],
            in_specs=[ANY] * (count + len(after)),
            out_specs=[ANY] * count,
            input_output_aliases={i: i for i in range(count)},
            compiler_params=pltpu.CompilerParams(has_side_effects=True),
            cost_estimate=pl.CostEstimate(flops=0, bytes_accessed=0, transcendentals=0),
        )(*values, *after)
        for value, same in zip(values, held):
            if self.last is value:
                self.last = same
        return held


def whole(shape):
    return pl.BlockSpec(shape, lambda *_: (0,) * len(shape))


def low_sum(*terms):
    total = terms[0].astype(F32)
    for term in terms[1:]:
        total = total + term.astype(F32)
    return total.astype(BF16)


def part_rows(index, size):
    return pl.ds(pl.multiple_of(index * size, size), size)


def split(place, bit, source, keep, send):
    half = keep.shape[1]
    keep[...] = source[:, part_rows(place[2 + bit], half), :]
    send[...] = source[:, part_rows(1 - place[2 + bit], half), :]


def quarter(place):
    return 2 * place[2] + place[3]


def scatter(place, source, outs):
    for partner, out in enumerate(outs):
        out[...] = source[:, part_rows(quarter(place) ^ partner, out.shape[1]), :]


def gather(place, pieces, out):
    for partner, piece in enumerate(pieces):
        out[:, part_rows(quarter(place) ^ partner, piece.shape[1]), :] = piece[...]


def normalize(values):
    center = values - jnp.mean(values, axis=-1, keepdims=True)
    inverse = lax.rsqrt(jnp.mean(center * center, axis=-1, keepdims=True) + EPS)
    return center * inverse, inverse


def norm_back(grad_normed, scaled, inverse, gain):
    grad_scaled = grad_normed * gain
    return inverse * (
        grad_scaled
        - jnp.mean(grad_scaled, axis=-1, keepdims=True)
        - scaled * jnp.mean(grad_scaled * scaled, axis=-1, keepdims=True)
    )


def gelu_pair(x):
    square = x * x
    near = jnp.minimum(square, 64.0)
    poly = ERF_X[0]
    for coefficient in ERF_X[1:]:
        poly = poly * near + coefficient
    phi = 0.5 * jnp.tanh(x * poly) + 0.5
    bell = jnp.exp(square * -0.5)
    return x * phi, phi + x * (bell * 0.3989422804014327)


def pack_first_kernel(place, w_query, w_key, w_value, qkv, qkv_send, first):
    width = qkv.shape[1] // 3
    half = qkv_send.shape[0]
    first[:, :HEAD_DIM] = w_query[:, :HEAD_DIM]
    first[:, HEAD_DIM:] = w_key[:, :HEAD_DIM]
    for core in range(2):

        @pl.when(place[0] == core)
        def _():
            narrow = slice(core * width, (core + 1) * width)
            for i, weight in enumerate((w_query, w_key, w_value)):
                qkv[:, i * width : (i + 1) * width] = weight[:, narrow]

    qkv_send[...] = qkv[pl.ds(pl.multiple_of(place[2] * half, half), half), :]


def pack_first_call(order, place, w_query, w_key, w_value):
    dim, width = w_query.shape[0], w_query.shape[1] // 2
    return order.run(
        4,
        pack_first_kernel,
        (place, w_query, w_key, w_value),
        [
            sds((dim, 3 * width), BF16),
            sds((dim // 2, 3 * width), BF16),
            sds((dim, 2 * HEAD_DIM), BF16),
        ],
        [SMEM] + [VMEM] * 3,
    )


def pack_last_kernel(place, w_out, w_up, w_down, grad, out, up, up_send, down, down_send, grad_out):
    width = out.shape[0]
    units = down.shape[0]
    half = units // 2
    grad_out[...] = grad[...]
    for core in range(2):

        @pl.when(place[0] == core)
        def _():
            wide = slice(core * units, (core + 1) * units)
            out[...] = w_out[core * width : (core + 1) * width, :]
            up[...] = w_up[:, wide]
            down[...] = w_down[wide, :]

    rows = pl.ds(pl.multiple_of(place[2] * half, half), half)
    up_send[...] = up[rows, :]
    down_send[...] = down[rows, :]


def pack_last_call(order, place, w_out, w_up, w_down, grad):
    width, dim = w_out.shape[0] // 2, w_out.shape[1]
    units = w_up.shape[1] // 2
    return order.run(
        5,
        pack_last_kernel,
        (place, w_out, w_up, w_down, grad),
        [
            sds((width, dim), BF16),
            sds((dim, units), BF16),
            sds((dim // 2, units), BF16),
            sds((units, dim), BF16),
            sds((units // 2, dim), BF16),
            sds(grad.shape, BF16),
        ],
        [SMEM] + [VMEM] * 4,
    )


def norm1_kernel(tokens, gain, shift, out):
    scaled, _ = normalize(tokens[...].astype(F32))
    out[...] = (scaled * gain[...] + shift[...]).astype(BF16)


def rows_spec(block, dim):
    return pl.BlockSpec((block, dim), lambda i: (i, 0))


def norm1_call(order, tokens, gain, shift):
    return order.run(2.5, norm1_kernel, (tokens, gain, shift), sds(tokens.shape, BF16))


def masks(seg_pad, cols, low, high):
    width = high - low
    seg_row = seg_pad[0:1, low:high]
    pad_row = seg_pad[1:2, low:high]
    row_key = jnp.where(pad_row > 0, seg_row, -2.0)
    col_seg = cols[:high, 0:1]
    col_pad = cols[:high, 1:2]
    col_key = jnp.where(col_pad > 0, col_seg, -1.0)
    key_at = lax.broadcasted_iota(jnp.int32, (high, width), 0)
    query_at = lax.broadcasted_iota(jnp.int32, (high, width), 1) + low
    allowed = ((col_key == seg_row) & (key_at <= query_at)) | (key_at == query_at)
    picked = (col_key == row_key) & (key_at < query_at)
    return allowed, picked


def penalty_kernel(
    block, place, n1_own, n1_other, first, first_moved, seg_pad, n1_out, penalty, qk0, first_out
):
    seq = n1_out.shape[0]
    half = seq // 2
    core = place[0]
    n1_out[pl.ds(pl.multiple_of(core * half, half), half), :] = n1_own[...]
    n1_out[pl.ds(pl.multiple_of((1 - core) * half, half), half), :] = n1_other[...]

    @pl.when(place[1] == 0)
    def _():
        first_out[...] = first[...]

    @pl.when(place[1] != 0)
    def _():
        first_out[...] = first_moved[...]

    qk = dot(first_out[...], n1_out[...], TT)
    q0 = (qk[:HEAD_DIM].astype(BF16) * 0.125).astype(BF16)
    k0 = qk[HEAD_DIM:].astype(BF16)
    qk0[:HEAD_DIM, :] = q0
    qk0[HEAD_DIM:, :] = k0
    seg_value = seg_pad[...]
    cols = seg_value.T
    earlier = lax.broadcasted_iota(jnp.int32, (block, block + 128), 0)
    later = lax.broadcasted_iota(jnp.int32, (block, block + 128), 1)
    sums = ((earlier < later) | (later >= block)).astype(F32).astype(BF16)
    carry = jnp.zeros((seq, 128), F32)
    for low in range(0, seq, block):
        high = low + block
        allowed, picked = masks(seg_value, cols, low, high)
        score = dot(k0[:, :high], q0[:, low:high], TN)
        small = jnp.exp(-jnp.abs(score))
        log1p = jnp.where(small < 1e-3, small - 0.5 * small * small, jnp.log(1.0 + small))
        select = jnp.where(picked, jnp.maximum(score, 0.0) + log1p, 0.0).astype(BF16)
        total = dot(select, sums, NN)
        before = jnp.concatenate([carry[:high]] * (block // 128), axis=1)
        penalty[:high, low:high] = jnp.where(allowed, total[:, :block] + before, FAR)
        if high % FORWARD_BLOCK:
            edge = high + FORWARD_BLOCK - high % FORWARD_BLOCK
            penalty[high:edge, low:high] = jnp.full((edge - high, block), FAR, F32)
        carry = jnp.concatenate([carry[:high] + total[:, block:], carry[high:]], axis=0)


def penalty_call(order, place, n1_own, n1_other, first, first_moved, seg_pad, after=()):
    half, dim = n1_own.shape
    seq = 2 * half
    return order.run(
        6.5,
        functools.partial(penalty_kernel, 256),
        (place, n1_own, n1_other, first, first_moved, seg_pad),
        [
            sds((seq, dim), BF16),
            sds((seq, seq), F32),
            sds((2 * HEAD_DIM, seq), BF16),
            sds(first.shape, BF16),
        ],
        [SMEM] + [VMEM] * 5,
        after,
    )


def forward_kernel(block, split, *refs):
    if split:
        place, n1, near, far, penalty, qkv, out, lse, weights = refs
    else:
        n1, weights, penalty, qkv, out, lse = refs
    head = pl.program_id(0)
    third = qkv.shape[0] // 3
    seq = qkv.shape[1]

    @pl.when(head == 0)
    def _():
        if split:
            join(place[2], weights, near, far)
        product = dot(weights[...], n1[...], TT).astype(BF16)
        qkv[:third, :] = (product[:third] * 0.125).astype(BF16)
        qkv[third:, :] = product[third:]

    at = pl.multiple_of(head * HEAD_DIM, HEAD_DIM)
    query = qkv[pl.ds(at, HEAD_DIM), :]
    key = qkv[pl.ds(third + at, HEAD_DIM), :]
    value = qkv[pl.ds(2 * third + at, HEAD_DIM), :]
    value = jnp.concatenate([value, jnp.ones((16, seq), BF16)], axis=0)
    for low in range(0, seq, block):
        high = low + block
        logits = dot(key[:, :high], query[:, low:high], TN) - penalty[:high, low:high]
        largest = jnp.max(logits, axis=0, keepdims=True)
        weight = jnp.exp(logits - largest).astype(BF16)
        result = dot(value[:, :high], weight, NN)
        total = result[HEAD_DIM : HEAD_DIM + 1, :]
        out[:, low:high] = (result[:HEAD_DIM] / total).astype(BF16)
        lse[:, low:high] = largest + jnp.log(total)


def join(bit, out, near, far):
    half = near.shape[0]
    out[pl.ds(pl.multiple_of(bit * half, half), half), :] = near[...]
    out[pl.ds(pl.multiple_of((1 - bit) * half, half), half), :] = far[...]


def forward_call(order, n1, weights, penalty, place=None, after=()):
    seq, dim = n1.shape
    split = place is not None
    width = weights[0].shape[1]
    heads = width // (3 * HEAD_DIM)
    operands = ((place,) if split else ()) + (n1,) + tuple(weights) + (penalty,)
    in_specs = [SMEM] if split else []
    in_specs += [whole(x.shape) for x in operands if x is not place]
    out_specs = [
        whole((width, seq)),
        pl.BlockSpec((HEAD_DIM, seq), lambda h: (h, 0)),
        pl.BlockSpec((None, 1, seq), lambda h: (h, 0, 0)),
    ]
    out_shape = [
        sds((width, seq), BF16),
        sds((heads * HEAD_DIM, seq), BF16),
        sds((heads, 1, seq), F32),
    ]
    if split:
        out_specs.append(whole((dim, width)))
        out_shape.append(sds((dim, width), BF16))
    return order.run(
        9.3,
        functools.partial(forward_kernel, FORWARD_BLOCK, split),
        operands,
        out_shape,
        in_specs,
        after,
        grid=(heads,),
        out_specs=out_specs,
    )


def project_kernel(place, out_l, out_r, w_l, w_r, own, send):
    half = own.shape[0]
    core = place[0]
    mixed = jnp.concatenate([w_l[...], w_r[...]], axis=0)

    def part(which):
        at = pl.ds(pl.multiple_of(which * half, half), half)
        heads = jnp.concatenate([out_l[:, at], out_r[:, at]], axis=0)
        return dot(heads, mixed, TN)

    send[...] = part(1 - core).astype(BF16)
    own[...] = part(core)


def project_call(order, place, out_l, out_r, w_l, w_r, after=()):
    half, dim = out_l.shape[1] // 2, w_l.shape[1]
    return order.run(
        3.5,
        project_kernel,
        (place, out_l, out_r, w_l, w_r),
        [sds((half, dim), F32), sds((half, dim), BF16)],
        [SMEM] + [VMEM] * 4,
        after,
    )


def norm2_kernel(tokens, own, received, gain, shift, hidden, out):
    total = tokens[...].astype(F32) + (own[...] + received[...].astype(F32))
    hidden[...] = total
    scaled, _ = normalize(total)
    out[...] = (scaled * gain[...] + shift[...]).astype(BF16)


def norm2_call(order, tokens, own, received, gain, shift, after=()):
    size, dim = tokens.shape
    rows = rows_spec(size // 4, dim)
    vector = whole((1, dim))
    return order.run(
        4,
        norm2_kernel,
        (tokens, own, received, gain, shift),
        [sds(tokens.shape, F32), sds(tokens.shape, BF16)],
        [rows] * 3 + [vector] * 2,
        after,
        grid=(4,),
        out_specs=[rows, rows],
    )


def mlp_kernel(first, steps, *refs):
    if first:
        place, n2_other, n2_own, g_other, g_own, w_up, w_down, *refs = refs
        mixed_send, mixed_own, back_send, back_own, keep, send, *refs = refs
    else:
        place, n2_other, n2_own, g_other, g_own, *refs = refs
        up_near, up_far, down_near, down_far, *refs = refs
        mixed_in_send, mixed_in_own, back_in_send, back_in_own, *refs = refs
        mixed_send, mixed_own, back_send, back_own, *refs = refs
        parts, refs = refs[:4], refs[4:]
        w_up, w_down, *refs = refs
    rows, grads, actives, grad_ups, w_grads = refs
    step = pl.program_id(0)
    block = n2_own.shape[0]
    early = step < steps // 2

    if not first:

        @pl.when(step == 0)
        def _():
            join(place[2], w_up, up_near, up_far)
            join(place[2], w_down, down_near, down_far)

    here = pl.ds(pl.multiple_of(step * block, block), block)
    row = jnp.where(early, n2_other[...], n2_own[...])
    grad = jnp.where(early, g_other[...], g_own[...])
    rows[here, :] = row
    grads[here, :] = grad
    active, slope = gelu_pair(dot(row, w_up[...], NN))
    active = active.astype(BF16)
    grad_up = (dot(grad, w_down[...], NT) * slope).astype(BF16)
    actives[here, :] = active
    grad_ups[here, :] = grad_up
    back = dot(grad_up, w_up[...], NT)
    mixed = dot(active, w_down[...], NN)

    @pl.when(early)
    def _():
        if first:
            back_send[...] = back.astype(back_send.dtype)
            mixed_send[...] = mixed.astype(mixed_send.dtype)
        else:
            back_send[...] = (back + back_in_send[...]).astype(back_send.dtype)
            mixed_send[...] = (mixed + mixed_in_send[...]).astype(mixed_send.dtype)

    @pl.when(jnp.logical_not(early))
    def _():
        if first:
            back_own[...] = back
            mixed_own[...] = mixed
        else:
            back_own[...] = back + back_in_own[...]
            mixed_own[...] = mixed + mixed_in_own[...]

    @pl.when(step == steps - 1)
    def _():
        w_grads[0] = dot(rows[...], grad_ups[...], TN).astype(BF16)
        w_grads[1] = dot(actives[...], grads[...], TN).astype(BF16)
        if first:
            split(place, 0, w_grads, keep, send)
        else:
            scatter(place, w_grads, parts)


def mlp_call(order, place, n2_other, n2_own, g_other, g_own, weights, before=None, after=()):
    size, dim = n2_own.shape
    first = before is None
    units = weights[0].shape[1]
    block = min(256, size // 2)
    steps = 2 * size // block
    last = steps // 2 - 1
    sent = pl.BlockSpec((block, dim), lambda i: (jnp.minimum(i, last), 0))
    kept = pl.BlockSpec((block, dim), lambda i: (jnp.maximum(i - last - 1, 0), 0))
    operands = (place, n2_other, n2_own, g_other, g_own) + tuple(weights)
    in_specs = [SMEM, sent, kept, sent, kept] + [whole(weight.shape) for weight in weights]
    sent_type = F32 if first else BF16
    scratch = []
    if not first:
        operands += tuple(before)
        in_specs += [sent, kept, sent, kept]
        scratch = [pltpu.VMEM((dim, units), BF16), pltpu.VMEM((units, dim), BF16)]
    count = 2 if first else 4
    part = (2, units // count, dim)
    tall = pltpu.VMEM((2 * size, dim), BF16)
    flat = pltpu.VMEM((2 * size, units), BF16)
    return order.run(
        14.6,
        functools.partial(mlp_kernel, first, steps),
        operands,
        [
            sds((size, dim), sent_type),
            sds((size, dim), F32),
            sds((size, dim), sent_type),
            sds((size, dim), F32),
        ]
        + [sds(part, BF16)] * count,
        in_specs,
        after,
        grid=(steps,),
        out_specs=[sent, kept, sent, kept] + [whole(part)] * count,
        scratch_shapes=scratch + [tall, tall, flat, flat, pltpu.VMEM((2, units, dim), BF16)],
    )


def norm2_back_kernel(hidden, own, received, grad, gain, grad_hidden, low, sums):
    normed_grad = own[...] + received[...].astype(F32)
    scaled, inverse = normalize(hidden[...])
    total = grad[...].astype(F32) + norm_back(normed_grad, scaled, inverse, gain[...])
    grad_hidden[...] = total
    low[...] = total.astype(BF16)
    add_sums(sums, normed_grad, scaled)


def add_sums(sums, normed_grad, scaled):
    @pl.when(pl.program_id(0) == 0)
    def _():
        sums[...] = jnp.zeros(sums.shape, F32)

    sums[0:1, :] += jnp.sum(normed_grad * scaled, axis=0, keepdims=True)
    sums[1:2, :] += jnp.sum(normed_grad, axis=0, keepdims=True)


def norm2_back_call(order, hidden, own, received, grad, gain, after=()):
    size, dim = hidden.shape
    rows = rows_spec(size // 4, dim)
    return order.run(
        5,
        norm2_back_kernel,
        (hidden, own, received, grad, gain),
        [sds(hidden.shape, F32), sds(hidden.shape, BF16), sds((8, dim), F32)],
        [rows] * 4 + [whole((1, dim))],
        after,
        grid=(4,),
        out_specs=[rows, rows, whole((8, dim))],
    )


def mixed_kernel(place, hidden, own, received, near, far, out, keep, send, total):
    out[...] = (hidden[...] + (own[...] + received[...].astype(F32))).astype(BF16)
    total[...] = low_sum(near[...], far[...])
    split(place, 1, total, keep, send)


def mixed_call(order, place, hidden, own, received, near, far):
    groups, rows, dim = near.shape
    return order.run(
        4,
        mixed_kernel,
        (place, hidden, own, received, near, far),
        [sds(hidden.shape, BF16)] + [sds((groups, rows // 2, dim), BF16)] * 2,
        [SMEM] + [VMEM] * 5,
        scratch_shapes=[pltpu.VMEM(near.shape, BF16)],
    )


def backward_kernel(first, block, *refs):
    place, g_own, g_other, w_out, heads_out, qkv, lse, penalty, *refs = refs
    if not first:
        before, *refs = refs
    grads, w_grad, logit_sum, grad_full, grad_heads, key_sum, value_sum, *refs = refs
    head = pl.program_id(0)
    third = qkv.shape[0] // 3
    seq = qkv.shape[1]
    half = seq // 2
    total = logit_sum if first else refs[0]

    @pl.when(head == 0)
    def _():
        core = place[0]
        grad_full[pl.ds(pl.multiple_of(core * half, half), half), :] = g_own[...]
        grad_full[pl.ds(pl.multiple_of((1 - core) * half, half), half), :] = g_other[...]
        whole_grad = grad_full[...]
        grad_heads[...] = dot(w_out[...], whole_grad, NT).astype(BF16)
        w_grad[...] = dot(heads_out[...], whole_grad, NN).astype(BF16)
        for low in range(0, seq, block):
            high = low + block
            if first:
                total[:high, low:high] = jnp.zeros((high, block), F32)
            else:
                total[:high, low:high] = before[:high, low:high]

    at = pl.multiple_of(head * HEAD_DIM, HEAD_DIM)
    query = qkv[pl.ds(at, HEAD_DIM), :]
    key = qkv[pl.ds(third + at, HEAD_DIM), :]
    value = qkv[pl.ds(2 * third + at, HEAD_DIM), :]
    grad = grad_heads[pl.ds(at, HEAD_DIM), :]
    for low in range(0, seq, block):
        high = low + block
        cols = slice(low, high)
        score = dot(key[:, :high], query[:, cols], TN)
        probs = jnp.exp(score - penalty[:high, cols] - lse[:, cols])
        grad_probs = dot(value[:, :high], grad[:, cols], TN)
        row_dot = jnp.sum(probs * grad_probs, axis=0, keepdims=True)
        grad_logits = probs * (grad_probs - row_dot)
        total[:high, cols] += grad_logits
        low_logits = grad_logits.astype(BF16)
        low_probs = probs.astype(BF16)
        grads[pl.ds(at, HEAD_DIM), cols] = (
            dot(key[:, :high], low_logits, NN) * 0.125
        ).astype(BF16)
        value_new = dot(grad[:, cols], low_probs, NT)
        key_new = dot(query[:, cols], low_logits, NT)
        if low:
            key_sum[:, :low] += key_new[:, :low]
            value_sum[:, :low] += value_new[:, :low]
        key_sum[:, cols] = key_new[:, low:]
        value_sum[:, cols] = value_new[:, low:]
    grads[pl.ds(third + at, HEAD_DIM), :] = key_sum[...].astype(BF16)
    grads[pl.ds(2 * third + at, HEAD_DIM), :] = value_sum[...].astype(BF16)
    if not first:

        @pl.when(head == pl.num_programs(0) - 1)
        def _():
            for low in range(0, seq, block):
                high = low + block
                logit_sum[:high, low:high] = total[:high, low:high].astype(BF16)


def backward_call(order, place, g_own, g_other, w_out, heads_out, qkv, lse, penalty, before=None):
    width, seq = qkv.shape
    half, dim = g_own.shape
    heads = width // (3 * HEAD_DIM)
    first = before is None
    square = whole((seq, seq))
    operands = (place, g_own, g_other, w_out, heads_out, qkv, lse, penalty)
    in_specs = [SMEM] + [whole(x.shape) for x in operands[1:6]]
    in_specs += [pl.BlockSpec((None, 1, seq), lambda h: (h, 0, 0)), square]
    scratch = [
        pltpu.VMEM((seq, dim), BF16),
        pltpu.VMEM((width // 3, seq), BF16),
        pltpu.VMEM((HEAD_DIM, seq), F32),
        pltpu.VMEM((HEAD_DIM, seq), F32),
    ]
    if not first:
        operands += (before,)
        in_specs.append(square)
        scratch.append(pltpu.VMEM((seq, seq), F32))
    return order.run(
        17,
        functools.partial(backward_kernel, first, 256),
        operands,
        [
            sds((width, seq), BF16),
            sds(w_out.shape, BF16),
            sds((seq, seq), F32 if first else BF16),
        ],
        in_specs,
        grid=(heads,),
        out_specs=[whole((width, seq)), whole(w_out.shape), square],
        scratch_shapes=scratch,
    )


def halves(value):
    high = value.astype(BF16)
    return high, (value - high.astype(F32)).astype(BF16)


def select_back(block, core, own, received, qk0, seg_pad, n1, out, w_grad, total_grad):
    seq = own.shape[0]
    q0 = qk0[:HEAD_DIM, :]
    k0 = qk0[HEAD_DIM:, :]
    seg_value = seg_pad[...]
    cols = seg_value.T
    later = lax.broadcasted_iota(jnp.int32, (block, block + 128), 0)
    earlier = lax.broadcasted_iota(jnp.int32, (block, block + 128), 1)
    sums = ((later > earlier) | (earlier >= block)).astype(F32).astype(BF16)
    carry = jnp.zeros((seq, 128), F32)
    total_grad[...] = jnp.zeros(total_grad.shape, F32)
    for low in range(seq - block, -1, -block):
        high = low + block
        logit_sum = own[:high, low:high].astype(F32) + received[:high, low:high].astype(F32)
        top, bottom = halves(logit_sum)
        total = dot(top, sums, NN) + dot(bottom, sums, NN)
        after = jnp.concatenate([carry[:high]] * (block // 128), axis=1)
        select_grad = -(total[:, :block] + after)
        carry = carry[:high] + total[:, block:]
        _, picked = masks(seg_value, cols, low, high)
        score = dot(k0[:, :high], q0[:, low:high], TN)
        through = jnp.where(picked, select_grad / (1.0 + jnp.exp(-score)), 0.0)
        top, bottom = halves(through)
        total_grad[:HEAD_DIM, low:high] = 0.125 * (
            dot(k0[:, :high], top, NN) + dot(k0[:, :high], bottom, NN)
        )
        total_grad[HEAD_DIM:, :high] += dot(q0[:, low:high], top, NT) + dot(
            q0[:, low:high], bottom, NT
        )
    out[...] = jnp.where(core == 0, total_grad[...], 0.0).astype(BF16)
    w_grad[...] = dot(out[...], n1[...], NN).astype(BF16)


def weights_first_kernel(place, n1, grads, weights, w_out, *refs):
    ff_near, ff_far, *refs = refs
    ff_parts, refs = refs[:4], refs[4:]
    back, ff, ff_move, *refs = refs
    parts, total = refs[:4], refs[4]
    width = grads.shape[0]
    ff[...] = low_sum(ff_near[...], ff_far[...])
    ff_move[...] = low_sum(*(part[...] for part in ff_parts))
    total[0, :width, :] = dot(grads[...], n1[...], NN).astype(BF16)
    total[0, width:, :] = w_out[...]
    scatter(place, total, parts)
    back[...] = dot(grads[...], weights[...], TT)


def weights_first_call(order, place, n1, grads, weights, w_out, ff_terms, ff_parts, after=()):
    seq, dim = n1.shape
    rows = grads.shape[0] + w_out.shape[0]
    shape = ff_parts[0].shape
    return order.run(
        8,
        weights_first_kernel,
        (place, n1, grads, weights, w_out, *ff_terms, *ff_parts),
        [sds((seq, dim), F32), sds(shape, BF16), sds(shape, BF16)]
        + [sds((1, rows // 4, dim), BF16)] * 4,
        [SMEM] + [VMEM] * 10,
        after,
        scratch_shapes=[pltpu.VMEM((1, rows, dim), BF16)],
    )


def weights_second_kernel(place, n1, grads, w_out, *refs):
    parts_r, refs = refs[:4], refs[4:]
    ff_own, ff_got, move_r, ff, *refs = refs
    parts, total = refs[:4], refs[4]
    width = grads.shape[0]
    move_r[...] = low_sum(*(part[...] for part in parts_r))
    ff[...] = low_sum(ff_own[...], ff_got[...])
    total[0, :width, :] = dot(grads[...], n1[...], NN).astype(BF16)
    total[0, width:, :] = w_out[...]
    scatter(place, total, parts)


def weights_second_call(order, place, n1, grads, w_out, parts_r, ff_terms):
    dim = n1.shape[1]
    rows = grads.shape[0] + w_out.shape[0]
    part = sds((1, rows // 4, dim), BF16)
    return order.run(
        6,
        weights_second_kernel,
        (place, n1, grads, w_out, *parts_r, *ff_terms),
        [part, sds(ff_terms[0].shape, BF16)] + [part] * 4,
        [SMEM] + [VMEM] * 9,
        scratch_shapes=[pltpu.VMEM((1, rows, dim), BF16)],
    )


def norm1_grad_kernel(block, place, logit_own, logit_got, qk0, seg_pad, n1, grads, weights, first, *refs):
    before, gain, shift, sums2, own, send, late, extra, extra_w, total_grad = refs
    select_back(
        block, place[0], logit_own, logit_got, qk0, seg_pad, n1, extra, extra_w, total_grad
    )
    half = own.shape[0]
    total = before[...] + dot(grads[...], weights[...], TT) + dot(extra[...], first[...], TT)
    for core in range(2):

        @pl.when(place[0] == core)
        def _():
            own[...] = total[core * half : (core + 1) * half]
            send[...] = total[(1 - core) * half : (2 - core) * half].astype(BF16)

    scaled = (n1[...].astype(F32) - shift[...]) * (1.0 / gain[...])
    gain_sum = jnp.sum(total * scaled, axis=0, keepdims=True)
    shift_sum = jnp.sum(total, axis=0, keepdims=True)
    norms = jnp.concatenate([gain_sum, shift_sum, sums2[0:2, :], sums2[4:8, :]], axis=0)
    rows = extra_w.shape[0]
    late[:rows, :] = extra_w[...]
    high, low = halves(norms)
    late[rows : rows + 8, :] = high
    late[rows + 8 :, :] = low


def norm1_grad_call(order, place, logits, qk0, seg_pad, n1, grads, weights, first, *rest):
    seq, dim = n1.shape
    rows = qk0.shape[0]
    return order.run(
        14,
        functools.partial(norm1_grad_kernel, 256),
        (place, *logits, qk0, seg_pad, n1, grads, weights, first, *rest),
        [
            sds((seq // 2, dim), F32),
            sds((seq // 2, dim), BF16),
            sds((rows + 16, dim), BF16),
        ],
        [SMEM] + [VMEM] * 12,
        scratch_shapes=[
            pltpu.VMEM((rows, seq), BF16),
            pltpu.VMEM((rows, dim), BF16),
            pltpu.VMEM((rows, seq), F32),
        ],
    )


def norm1_back_kernel(tokens, own, received, grad_hidden, gain, out):
    normed_grad = own[...] + received[...].astype(F32)
    scaled, inverse = normalize(tokens[...].astype(F32))
    total = grad_hidden[...] + norm_back(normed_grad, scaled, inverse, gain[...])
    out[...] = total.astype(BF16)


def norm1_back_call(order, tokens, own, received, grad_hidden, gain, after=()):
    size, dim = tokens.shape
    rows = rows_spec(size // 2, dim)
    return order.run(
        4,
        norm1_back_kernel,
        (tokens, own, received, grad_hidden, gain),
        sds(tokens.shape, BF16),
        [rows] * 4 + [whole((1, dim))],
        after,
        grid=(2,),
        out_specs=rows,
    )


def add_late(terms, out):
    def pairs(values):
        while len(values) > 1:
            values = [values[i] + values[i + 1] for i in range(0, len(values), 2)]
        return values[0]

    rows = out.shape[0] - 16
    out[:rows, :] = pairs([term[:rows, :].astype(F32) for term in terms]).astype(BF16)
    norms = pairs(
        [term[rows : rows + 8, :].astype(F32) + term[rows + 8 :, :].astype(F32) for term in terms]
    )
    high, low = halves(norms)
    out[rows : rows + 8, :] = high
    out[rows + 8 :, :] = low


def step1_kernel(late_own, late_got, *refs):
    at_terms, refs = refs[:5], refs[5:]
    ff_own, ff_got, both, ff = refs
    size = at_terms[0].shape[1]
    both[:size, :] = low_sum(*(term[0] for term in at_terms))
    add_late((late_own, late_got), both.at[size:, :])
    ff[...] = low_sum(ff_own[...], ff_got[...])


def step1_call(order, late_terms, at_terms, ff_terms):
    _, size, dim = at_terms[0].shape
    rows = size + late_terms[0].shape[0]
    return order.run(
        3.5,
        step1_kernel,
        (*late_terms, *at_terms, *ff_terms),
        [sds((rows, dim), BF16), sds(ff_terms[0].shape, BF16)],
    )


def step2_kernel(size, place, own, got, *refs):
    *ff_parts, both, ff = refs
    both[:size, :] = low_sum(own[:size, :], got[:size, :])
    add_late((own.at[size:, :], got.at[size:, :]), both.at[size:, :])
    gather(place, ff_parts, ff)


def step2_call(order, place, size, own, got, ff_parts, after=()):
    groups, rows, dim = ff_parts[0].shape
    return order.run(
        4.5,
        functools.partial(step2_kernel, size),
        (place, own, got, *ff_parts),
        [sds(own.shape, BF16), sds((groups, 4 * rows, dim), BF16)],
        [SMEM] + [VMEM] * 6,
        after,
    )


def step3_kernel(size, place, *refs):
    parts, refs = refs[:4], refs[4:]
    mixed, grad, both, mixed_out, grad_out = refs
    for partner, part in enumerate(parts):
        both[part_rows(quarter(place) ^ partner, size), :] = part[:size, :]
    add_late([part.at[size:, :] for part in parts], both.at[4 * size :, :])
    mixed_out[...] = mixed[...]
    grad_out[...] = grad[...]


def step3_call(order, place, size, parts, mixed, grad):
    rows, dim = parts[0].shape
    return order.run(
        3.5,
        functools.partial(step3_kernel, size),
        (place, *parts, mixed, grad),
        [sds((rows + 3 * size, dim), BF16), sds(mixed.shape, BF16), sds(grad.shape, BF16)],
        [SMEM] + [VMEM] * 6,
    )


def finish_attention_kernel(place, near, far, w_query, w_key, w_value, w_out, norms):
    width = w_out.shape[0] // 2
    late = 4 * width
    rows = late + 2 * HEAD_DIM
    total = jnp.zeros(norms.shape, F32)
    for ref in (near, far):
        total = total + (ref[rows : rows + 8, :].astype(F32) + ref[rows + 8 :, :].astype(F32))
    norms[...] = total
    extra = near[late:rows, :].astype(F32) + far[late:rows, :].astype(F32)
    extra = jnp.where(place[1] == 0, extra, 0.0)
    for core in range(2):

        @pl.when(place[0] == core)
        def _():
            low, high = (near, far) if core == 0 else (far, near)
            for i, out in enumerate((w_query, w_key, w_value)):
                piece = slice(i * width, (i + 1) * width)
                part = low[piece, :].astype(F32)
                if i < 2:
                    more = extra[i * HEAD_DIM : (i + 1) * HEAD_DIM]
                    part = jnp.concatenate([part[:HEAD_DIM] + more, part[HEAD_DIM:]], axis=0)
                out[...] = jnp.concatenate([part, high[piece, :].astype(F32)], axis=0).T
            w_out[:width, :] = low[3 * width : late, :].astype(F32)
            w_out[width:, :] = high[3 * width : late, :].astype(F32)


def finish_attention_call(order, place, width, near, far):
    dim = near.shape[1]
    return order.run(
        4.5,
        finish_attention_kernel,
        (place, near, far),
        [sds((dim, 2 * width), F32)] * 3 + [sds((2 * width, dim), F32), sds((8, dim), F32)],
        [SMEM] + [VMEM] * 2,
    )


def finish_mlp_kernel(place, near, far, w_up, w_down):
    units = near.shape[1]
    for core in range(2):

        @pl.when(place[0] == core)
        def _():
            low, high = (near, far) if core == 0 else (far, near)
            w_up[:, :units] = low[0].astype(F32)
            w_up[:, units:] = high[0].astype(F32)
            w_down[:units, :] = low[1].astype(F32)
            w_down[units:, :] = high[1].astype(F32)


def finish_mlp_call(order, place, near, far):
    _, units, dim = near.shape
    return order.run(
        6.8,
        finish_mlp_kernel,
        (place, near, far),
        [sds((dim, 2 * units), F32), sds((2 * units, dim), F32)],
        [SMEM] + [VMEM] * 2,
    )


def make_body(devices, parts):
    axes = ("dp", "tensor")
    chips = devices // 2
    in_order = [1 << bit for bit in range(chips.bit_length() - 1)]
    turned = [in_order[1], in_order[0], *in_order[2:]]
    rounds = len(in_order)
    rounds_more = range(3, rounds)

    def pairs(move):
        found = []
        for device in range(devices):
            for part in range(parts):
                to_chip, to_core, to_part = move(device // 2, device % 2, part)
                source = device * parts + part
                found.append((source, (to_chip * 2 + to_core) * parts + to_part))
        return found

    def by_bit(bit):
        return pairs(
            lambda chip, core, part: (chip ^ (turned if core else in_order)[bit], core, part)
        )

    by_role = pairs(lambda chip, core, part: (chip, part, core))
    by_core = pairs(lambda chip, core, part: (chip, 1 - core, part))
    by_part = pairs(lambda chip, core, part: (chip, core, 1 - part))
    from_first_part = [pair for pair in by_part if pair[0] % parts == 0]
    extra_to_first = [
        pair for pair in by_part if pair[0] % parts == 1 and (pair[0] // parts) % 2 == 0
    ]
    to_first_core = [pair for pair in by_core if (pair[0] // parts) % 2 == 1]
    by_chip = [by_bit(bit) for bit in range(rounds)]

    def by_quarter(partner):
        def across(chip, core, part):
            for bit in range(2):
                if partner >> (1 - bit) & 1:
                    chip ^= (turned if core else in_order)[bit]
            return chip, core, part

        return pairs(across)

    def move(value, how):
        return lax.ppermute(value, axes, how)

    def add_more(value):
        for bit in rounds_more:
            other = move(value, by_chip[bit])
            value = (value.astype(F32) + other.astype(F32)).astype(value.dtype)
        return value

    def exchange(values):
        return [values[0]] + [move(values[i], by_quarter(i)) for i in range(1, 4)]

    def body(
        tokens,
        segment_ids,
        pad_mask,
        norm1_gain,
        norm1_shift,
        w_query,
        w_key,
        w_value,
        w_out,
        norm2_gain,
        norm2_shift,
        w_up,
        w_down,
        cotangent,
    ):
        order = Order()
        device = lax.axis_index("dp")
        part = lax.axis_index("tensor")
        core = device % 2
        chip = device // 2
        bits = [
            jnp.where(core == 1, (chip & turned[i]) != 0, (chip & in_order[i]) != 0)
            for i in range(rounds)
        ]
        place = jnp.stack([core, part] + bits).astype(jnp.int32)
        gain1, shift1, gain2, shift2 = (
            vector[None, :] for vector in (norm1_gain, norm1_shift, norm2_gain, norm2_shift)
        )

        mine = move(tokens, by_role)
        ints = jnp.concatenate([segment_ids, pad_mask], axis=0)
        ints = jnp.where(core == part, ints, move(ints, by_core)).astype(F32)
        seg_pad = jnp.concatenate([ints, jnp.zeros((6, ints.shape[1]), F32)], axis=0)

        qkv_l, qkv_s, first = pack_first_call(order, place, w_query, w_key, w_value)
        first_moved = move(first, from_first_part)
        qkv_near = move(qkv_s, by_part)
        n1_own = norm1_call(order, mine, gain1, shift1)
        n1_other = move(n1_own, by_core)
        out_l, up_l, up_s, down_l, down_s, grad = pack_last_call(
            order, place, w_out, w_up, w_down, cotangent
        )
        out_r = move(out_l, by_part)
        up_near = move(up_s, by_part)
        grad_own = move(grad, by_role)
        down_near = move(down_s, by_part)
        n1, penalty, qk0, first = penalty_call(
            order, place, n1_own, n1_other, first, first_moved, seg_pad
        )
        (qkv_near,) = order.hold((qkv_near,), (penalty,))
        qkv_far = move(qkv_near, by_chip[0])
        qkvt_l, heads_l, lse_l = forward_call(order, n1, (qkv_l,), penalty)
        qkvt_r, heads_r, lse_r, qkv_r = forward_call(
            order, n1, (qkv_near, qkv_far), penalty, place, after=(up_near,)
        )
        (up_near,) = order.hold((up_near,), (lse_r,))
        up_far = move(up_near, by_chip[0])
        (grad_own,) = order.hold((grad_own,), (lse_r,))
        grad_other = move(grad_own, by_core)
        own, send = project_call(order, place, heads_l, heads_r, out_l, out_r, after=(down_near,))
        (down_near,) = order.hold((down_near,), (send,))
        down_far = move(down_near, by_chip[0])
        hidden, n2_own = norm2_call(order, mine, own, move(send, by_core), gain2, shift2)
        n2_other = move(n2_own, by_core)
        *before, keep, send = mlp_call(
            order, place, n2_other, n2_own, grad_other, grad_own, (up_l, down_l)
        )
        got = move(send, by_chip[0])
        weights = (up_near, up_far, down_near, down_far)
        mixed_send, mixed_own, back_send, back_own, *ff_r = mlp_call(
            order, place, n2_other, n2_own, grad_other, grad_own, weights, before
        )
        back_send, mixed_send, *ff_r = order.hold((back_send, mixed_send, *ff_r), (got,))
        ff_r = exchange(ff_r)
        grad_hidden, low_own, sums2 = norm2_back_call(
            order, hidden, back_own, move(back_send, by_core), grad_own, gain2
        )
        low_other = move(low_own, by_core)
        mixed, keep, send = mixed_call(
            order, place, hidden, mixed_own, move(mixed_send, by_core), keep, got
        )
        mixed = move(mixed, by_role)
        got = move(send, by_chip[1])

        low = (low_own, low_other)
        grads_r, wo_r, logit_sum = backward_call(
            order, place, *low, out_r, heads_r, qkvt_r, lse_r, penalty
        )
        back, ff, ff_move, *at_r = weights_first_call(
            order, place, n1, grads_r, qkv_r, wo_r, (keep, got), ff_r, (mixed,)
        )
        ff_got = move(ff_move, by_part)
        at_r = exchange(at_r)
        grads_l, wo_l, logit_sum = backward_call(
            order, place, *low, out_l, heads_l, qkvt_l, lse_l, penalty, logit_sum
        )
        logit_got = move(logit_sum, to_first_core)
        at_r, ff, *at = weights_second_call(
            order, place, n1, grads_l, wo_l, at_r, (ff, ff_got)
        )
        at_r = move(at_r, by_part)
        ff_got = move(ff, by_chip[2])
        at = exchange(at)
        own, send, late = norm1_grad_call(
            order,
            place,
            (logit_sum, logit_got),
            qk0,
            seg_pad,
            n1,
            grads_l,
            qkv_l,
            first,
            back,
            gain1,
            shift1,
            sums2,
        )
        send, late = order.hold((send, late), (*at, at_r))
        received = move(send, by_core)
        late_got = move(late, by_part)
        both, ff = step1_call(order, (late, late_got), (*at, at_r), (ff, ff_got))
        size = at_r.shape[1]
        both_got = move(both, by_chip[2])
        ff = exchange([add_more(ff)] * 4)
        tokens_grad = norm1_back_call(order, mine, own, received, grad_hidden, gain1)
        tokens_grad = move(tokens_grad, by_role)
        both, ff = step2_call(order, place, size, both, both_got, ff)
        both = exchange([add_more(both)] * 4)
        ff_far = move(ff, by_core)
        up_grad, down_grad = finish_mlp_call(order, place, ff, ff_far)
        both, mixed, tokens_grad = step3_call(order, place, size, both, mixed, tokens_grad)
        query_grad, key_grad, value_grad, out_grad, norms = finish_attention_call(
            order, place, size, both, move(both, by_core)
        )
        return (
            mixed,
            tokens_grad,
            norms[0],
            norms[1],
            query_grad,
            key_grad,
            value_grad,
            out_grad,
            norms[2],
            norms[3],
            up_grad,
            down_grad,
        )

    return body


def solution(mesh):
    in_specs = (
        P(("dp", "tensor"), None),
        P("dp", None),
        P("dp", None),
        P(),
        P(),
        P(None, "tensor"),
        P(None, "tensor"),
        P(None, "tensor"),
        P("tensor", None),
        P(),
        P(),
        P(None, "tensor"),
        P("tensor", None),
        P(("dp", "tensor"), None),
    )
    out_specs = (
        P(("dp", "tensor"), None),
        P(("dp", "tensor"), None),
        P(),
        P(),
        P(None, "tensor"),
        P(None, "tensor"),
        P(None, "tensor"),
        P("tensor", None),
        P(),
        P(),
        P(None, "tensor"),
        P("tensor", None),
    )
    body = make_body(mesh.shape["dp"], mesh.shape["tensor"])
    return jax.shard_map(body, mesh=mesh, in_specs=in_specs, out_specs=out_specs, check_vma=False)
```

```python
import functools

import jax
import jax.numpy as jnp
from jax import lax
from jax.experimental import pallas as pl
from jax.experimental.pallas import tpu as pltpu
from jax.sharding import PartitionSpec as P

HEAD_DIM = 64
EPS = 1e-05
FAR = 1e30
FORWARD_BLOCK = 512
BF16 = jnp.bfloat16
F32 = jnp.float32
TN = (((0,), (0,)), ((), ()))
NT = (((1,), (1,)), ((), ()))
NN = (((1,), (0,)), ((), ()))
TT = (((0,), (1,)), ((), ()))
ERF_C = (
    1.5897294934128858e-07,
    -5.985900079472216e-06,
    8.971378204617447e-05,
    -0.0006257225011275588,
    -0.0001843806018428344,
    0.10276548023357895,
    1.1283797055884355,
)
ERF_X = tuple(c * 0.5 ** (6 - i) * 0.7071067811865476 for i, c in enumerate(ERF_C))


def dot(left, right, dims):
    return lax.dot_general(left, right, dims, preferred_element_type=F32)


def sds(shape, dtype):
    return jax.ShapeDtypeStruct(shape, dtype)


SMEM = pl.BlockSpec(memory_space=pltpu.SMEM)
VMEM = pl.BlockSpec(memory_space=pltpu.VMEM)
ANY = pl.BlockSpec(memory_space=pl.ANY)


WEIGHT = 20.0


class Order:
    def __init__(self):
        self.last = None

    def run(self, us, kernel, operands, out_shape, in_specs=None, after=(), **rest):
        after = tuple(after) + (() if self.last is None else (self.last,))
        count, extra = len(operands), len(after)
        in_specs = list(in_specs or [VMEM] * count) + [ANY] * extra

        def body(*refs):
            kernel(*refs[:count], *refs[count + extra :])

        out = pl.pallas_call(
            body,
            out_shape=out_shape,
            in_specs=in_specs,
            compiler_params=pltpu.CompilerParams(vmem_limit_bytes=58 << 20),
            cost_estimate=pl.CostEstimate(
                flops=int(us * WEIGHT * 1.15e9), bytes_accessed=0, transcendentals=0
            ),
            **rest,
        )(*operands, *after)
        self.last = out[-1] if isinstance(out, (list, tuple)) else out
        return out

    def hold(self, values, after):
        count = len(values)

        def kernel(*refs):
            pass

        held = pl.pallas_call(
            kernel,
            out_shape=[sds(value.shape, value.dtype) for value in values],
            in_specs=[ANY] * (count + len(after)),
            out_specs=[ANY] * count,
            input_output_aliases={i: i for i in range(count)},
            compiler_params=pltpu.CompilerParams(has_side_effects=True),
            cost_estimate=pl.CostEstimate(flops=0, bytes_accessed=0, transcendentals=0),
        )(*values, *after)
        for value, same in zip(values, held):
            if self.last is value:
                self.last = same
        return held


def whole(shape):
    return pl.BlockSpec(shape, lambda *_: (0,) * len(shape))


def low_sum(*terms):
    total = terms[0].astype(F32)
    for term in terms[1:]:
        total = total + term.astype(F32)
    return total.astype(BF16)


def part_rows(index, size):
    return pl.ds(pl.multiple_of(index * size, size), size)


def split(place, bit, source, keep, send):
    half = keep.shape[1]
    keep[...] = source[:, part_rows(place[2 + bit], half), :]
    send[...] = source[:, part_rows(1 - place[2 + bit], half), :]


def quarter(place):
    return 2 * place[2] + place[3]


def scatter(place, source, outs):
    for partner, out in enumerate(outs):
        out[...] = source[:, part_rows(quarter(place) ^ partner, out.shape[1]), :]


def gather(place, pieces, out):
    for partner, piece in enumerate(pieces):
        out[:, part_rows(quarter(place) ^ partner, piece.shape[1]), :] = piece[...]


def normalize(values):
    center = values - jnp.mean(values, axis=-1, keepdims=True)
    inverse = lax.rsqrt(jnp.mean(center * center, axis=-1, keepdims=True) + EPS)
    return center * inverse, inverse


def norm_back(grad_normed, scaled, inverse, gain):
    grad_scaled = grad_normed * gain
    return inverse * (
        grad_scaled
        - jnp.mean(grad_scaled, axis=-1, keepdims=True)
        - scaled * jnp.mean(grad_scaled * scaled, axis=-1, keepdims=True)
    )


def gelu_pair(x):
    square = x * x
    near = jnp.minimum(square, 64.0)
    poly = ERF_X[0]
    for coefficient in ERF_X[1:]:
        poly = poly * near + coefficient
    phi = 0.5 * jnp.tanh(x * poly) + 0.5
    bell = jnp.exp(square * -0.5)
    return x * phi, phi + x * (bell * 0.3989422804014327)


def pack_first_kernel(place, w_query, w_key, w_value, qkv, qkv_send, first):
    width = qkv.shape[1] // 3
    half = qkv_send.shape[0]
    first[:, :HEAD_DIM] = w_query[:, :HEAD_DIM]
    first[:, HEAD_DIM:] = w_key[:, :HEAD_DIM]
    for core in range(2):

        @pl.when(place[0] == core)
        def _():
            narrow = slice(core * width, (core + 1) * width)
            for i, weight in enumerate((w_query, w_key, w_value)):
                qkv[:, i * width : (i + 1) * width] = weight[:, narrow]

    qkv_send[...] = qkv[pl.ds(pl.multiple_of(place[2] * half, half), half), :]


def pack_first_call(order, place, w_query, w_key, w_value):
    dim, width = w_query.shape[0], w_query.shape[1] // 2
    return order.run(
        4,
        pack_first_kernel,
        (place, w_query, w_key, w_value),
        [
            sds((dim, 3 * width), BF16),
            sds((dim // 2, 3 * width), BF16),
            sds((dim, 2 * HEAD_DIM), BF16),
        ],
        [SMEM] + [VMEM] * 3,
    )


def pack_last_kernel(place, w_out, w_up, w_down, grad, out, up, up_send, down, down_send, grad_out):
    width = out.shape[0]
    units = down.shape[0]
    half = units // 2
    grad_out[...] = grad[...]
    for core in range(2):

        @pl.when(place[0] == core)
        def _():
            wide = slice(core * units, (core + 1) * units)
            out[...] = w_out[core * width : (core + 1) * width, :]
            up[...] = w_up[:, wide]
            down[...] = w_down[wide, :]

    rows = pl.ds(pl.multiple_of(place[2] * half, half), half)
    up_send[...] = up[rows, :]
    down_send[...] = down[rows, :]


def pack_last_call(order, place, w_out, w_up, w_down, grad):
    width, dim = w_out.shape[0] // 2, w_out.shape[1]
    units = w_up.shape[1] // 2
    return order.run(
        5,
        pack_last_kernel,
        (place, w_out, w_up, w_down, grad),
        [
            sds((width, dim), BF16),
            sds((dim, units), BF16),
            sds((dim // 2, units), BF16),
            sds((units, dim), BF16),
            sds((units // 2, dim), BF16),
            sds(grad.shape, BF16),
        ],
        [SMEM] + [VMEM] * 4,
    )


def norm1_kernel(tokens, gain, shift, out):
    scaled, _ = normalize(tokens[...].astype(F32))
    out[...] = (scaled * gain[...] + shift[...]).astype(BF16)


def rows_spec(block, dim):
    return pl.BlockSpec((block, dim), lambda i: (i, 0))


def norm1_call(order, tokens, gain, shift):
    return order.run(2.5, norm1_kernel, (tokens, gain, shift), sds(tokens.shape, BF16))


def masks(seg_pad, cols, low, high):
    width = high - low
    seg_row = seg_pad[0:1, low:high]
    pad_row = seg_pad[1:2, low:high]
    row_key = jnp.where(pad_row > 0, seg_row, -2.0)
    col_seg = cols[:high, 0:1]
    col_pad = cols[:high, 1:2]
    col_key = jnp.where(col_pad > 0, col_seg, -1.0)
    key_at = lax.broadcasted_iota(jnp.int32, (high, width), 0)
    query_at = lax.broadcasted_iota(jnp.int32, (high, width), 1) + low
    allowed = ((col_key == seg_row) & (key_at <= query_at)) | (key_at == query_at)
    picked = (col_key == row_key) & (key_at < query_at)
    return allowed, picked


def penalty_kernel(
    block, place, n1_own, n1_other, first, first_moved, seg_pad, n1_out, penalty, qk0, first_out
):
    seq = n1_out.shape[0]
    half = seq // 2
    core = place[0]
    n1_out[pl.ds(pl.multiple_of(core * half, half), half), :] = n1_own[...]
    n1_out[pl.ds(pl.multiple_of((1 - core) * half, half), half), :] = n1_other[...]

    @pl.when(place[1] == 0)
    def _():
        first_out[...] = first[...]

    @pl.when(place[1] != 0)
    def _():
        first_out[...] = first_moved[...]

    qk = dot(first_out[...], n1_out[...], TT)
    q0 = (qk[:HEAD_DIM].astype(BF16) * 0.125).astype(BF16)
    k0 = qk[HEAD_DIM:].astype(BF16)
    qk0[:HEAD_DIM, :] = q0
    qk0[HEAD_DIM:, :] = k0
    seg_value = seg_pad[...]
    cols = seg_value.T
    earlier = lax.broadcasted_iota(jnp.int32, (block, block + 128), 0)
    later = lax.broadcasted_iota(jnp.int32, (block, block + 128), 1)
    sums = ((earlier < later) | (later >= block)).astype(F32).astype(BF16)
    carry = jnp.zeros((seq, 128), F32)
    for low in range(0, seq, block):
        high = low + block
        allowed, picked = masks(seg_value, cols, low, high)
        score = dot(k0[:, :high], q0[:, low:high], TN)
        small = jnp.exp(-jnp.abs(score))
        log1p = jnp.where(small < 1e-3, small - 0.5 * small * small, jnp.log(1.0 + small))
        select = jnp.where(picked, jnp.maximum(score, 0.0) + log1p, 0.0).astype(BF16)
        total = dot(select, sums, NN)
        before = jnp.concatenate([carry[:high]] * (block // 128), axis=1)
        penalty[:high, low:high] = jnp.where(allowed, total[:, :block] + before, FAR)
        if high % FORWARD_BLOCK:
            edge = high + FORWARD_BLOCK - high % FORWARD_BLOCK
            penalty[high:edge, low:high] = jnp.full((edge - high, block), FAR, F32)
        carry = jnp.concatenate([carry[:high] + total[:, block:], carry[high:]], axis=0)


def penalty_call(order, place, n1_own, n1_other, first, first_moved, seg_pad, after=()):
    half, dim = n1_own.shape
    seq = 2 * half
    return order.run(
        6.5,
        functools.partial(penalty_kernel, 256),
        (place, n1_own, n1_other, first, first_moved, seg_pad),
        [
            sds((seq, dim), BF16),
            sds((seq, seq), F32),
            sds((2 * HEAD_DIM, seq), BF16),
            sds(first.shape, BF16),
        ],
        [SMEM] + [VMEM] * 5,
        after,
    )


def forward_kernel(block, last, *refs):
    if last:
        place, n1, near, far, penalty, out_l, w_l, w_r, *refs = refs
        qkv, out, lse, weights, own, send, out_r = refs
    else:
        n1, weights, penalty, qkv, out, lse = refs
    head = pl.program_id(0)
    third = qkv.shape[0] // 3
    seq = qkv.shape[1]

    @pl.when(head == 0)
    def _():
        if last:
            join(place[2], weights, near, far)
        product = dot(weights[...], n1[...], TT).astype(BF16)
        qkv[:third, :] = (product[:third] * 0.125).astype(BF16)
        qkv[third:, :] = product[third:]

    at = pl.multiple_of(head * HEAD_DIM, HEAD_DIM)
    query = qkv[pl.ds(at, HEAD_DIM), :]
    key = qkv[pl.ds(third + at, HEAD_DIM), :]
    value = qkv[pl.ds(2 * third + at, HEAD_DIM), :]
    value = jnp.concatenate([value, jnp.ones((16, seq), BF16)], axis=0)
    for low in range(0, seq, block):
        high = low + block
        logits = dot(key[:, :high], query[:, low:high], TN) - penalty[:high, low:high]
        largest = jnp.max(logits, axis=0, keepdims=True)
        weight = jnp.exp(logits - largest).astype(BF16)
        result = dot(value[:, :high], weight, NN)
        total = result[HEAD_DIM : HEAD_DIM + 1, :]
        out[:, low:high] = (result[:HEAD_DIM] / total).astype(BF16)
        lse[:, low:high] = largest + jnp.log(total)
    if last:
        out_r[pl.ds(at, HEAD_DIM), :] = out[...]

        @pl.when(head == pl.num_programs(0) - 1)
        def _():
            project(place, out_l, out_r, w_l, w_r, own, send)


def join(bit, out, near, far):
    half = near.shape[0]
    out[pl.ds(pl.multiple_of(bit * half, half), half), :] = near[...]
    out[pl.ds(pl.multiple_of((1 - bit) * half, half), half), :] = far[...]


def forward_call(order, n1, weights, penalty, place=None, others=(), after=()):
    seq, dim = n1.shape
    last = place is not None
    width = weights[0].shape[1]
    heads = width // (3 * HEAD_DIM)
    operands = ((place,) if last else ()) + (n1,) + tuple(weights) + (penalty,) + tuple(others)
    in_specs = [SMEM] if last else []
    in_specs += [whole(x.shape) for x in operands if x is not place]
    out_specs = [
        whole((width, seq)),
        pl.BlockSpec((HEAD_DIM, seq), lambda h: (h, 0)),
        pl.BlockSpec((None, 1, seq), lambda h: (h, 0, 0)),
    ]
    out_shape = [
        sds((width, seq), BF16),
        sds((heads * HEAD_DIM, seq), BF16),
        sds((heads, 1, seq), F32),
    ]
    scratch = []
    if last:
        out_specs += [whole((dim, width)), whole((seq // 2, dim)), whole((seq // 2, dim))]
        out_shape += [sds((dim, width), BF16), sds((seq // 2, dim), F32), sds((seq // 2, dim), BF16)]
        scratch.append(pltpu.VMEM((heads * HEAD_DIM, seq), BF16))
    return order.run(
        10,
        functools.partial(forward_kernel, FORWARD_BLOCK, last),
        operands,
        out_shape,
        in_specs,
        after,
        grid=(heads,),
        out_specs=out_specs,
        scratch_shapes=scratch,
    )


def project(place, out_l, out_r, w_l, w_r, own, send):
    half = own.shape[0]
    core = place[0]
    mixed = jnp.concatenate([w_l[...], w_r[...]], axis=0)

    def part(which):
        heads = jnp.concatenate([out_l[:, part_rows(which, half)], out_r[:, part_rows(which, half)]], axis=0)
        return dot(heads, mixed, TN)

    send[...] = part(1 - core).astype(BF16)
    own[...] = part(core)


def norm2_kernel(tokens, own, received, gain, shift, hidden, out):
    total = tokens[...].astype(F32) + (own[...] + received[...].astype(F32))
    hidden[...] = total
    scaled, _ = normalize(total)
    out[...] = (scaled * gain[...] + shift[...]).astype(BF16)


def norm2_call(order, tokens, own, received, gain, shift, after=()):
    size, dim = tokens.shape
    rows = rows_spec(size // 2, dim)
    vector = whole((1, dim))
    return order.run(
        4,
        norm2_kernel,
        (tokens, own, received, gain, shift),
        [sds(tokens.shape, F32), sds(tokens.shape, BF16)],
        [rows] * 3 + [vector] * 2,
        after,
        grid=(2,),
        out_specs=[rows, rows],
    )


def mlp_kernel(first, *refs):
    place, n2_other, n2_own, g_other, g_own, *refs = refs
    if first:
        w_up, w_down, *refs = refs
        before = (None,) * 4
    else:
        up_near, up_far, down_near, down_far, *refs = refs
        before, refs = refs[:4], refs[4:]
    outs, refs = refs[:4], refs[4:]
    count = 2 if first else 4
    parts, refs = refs[:count], refs[count:]
    if not first:
        w_up, w_down, *refs = refs
        join(place[2], w_up, up_near, up_far)
        join(place[2], w_down, down_near, down_far)
    actives, grad_ups, w_grads = refs
    size = n2_own.shape[0]

    def put(out, rows, value, more):
        out[rows, :] = (value if more is None else value + more[rows, :]).astype(out.dtype)

    block = min(256, size)
    for at, n2, g in ((0, n2_other, g_other), (1, n2_own, g_own)):

        def work(step, _):
            rows = part_rows(step, block)
            here = part_rows(step + at * (size // block), block)
            active, slope = gelu_pair(dot(n2[rows, :], w_up[...], NN))
            active = active.astype(BF16)
            grad_up = (dot(g[rows, :], w_down[...], NT) * slope).astype(BF16)
            actives[here, :] = active
            grad_ups[here, :] = grad_up
            put(outs[2 + at], rows, dot(grad_up, w_up[...], NT), before[2 + at])
            put(outs[at], rows, dot(active, w_down[...], NN), before[at])
            return 0

        lax.fori_loop(0, size // block, work, 0)
    w_grads[0] = (
        dot(n2_other[...], grad_ups[:size, :], TN) + dot(n2_own[...], grad_ups[size:, :], TN)
    ).astype(BF16)
    w_grads[1] = (
        dot(actives[:size, :], g_other[...], TN) + dot(actives[size:, :], g_own[...], TN)
    ).astype(BF16)
    if first:
        split(place, 0, w_grads, *parts)
    else:
        scatter(place, w_grads, parts)


def mlp_call(order, place, n2_other, n2_own, g_other, g_own, weights, before=(), after=()):
    size, dim = n2_own.shape
    first = not before
    units = weights[0].shape[1]
    count = 2 if first else 4
    sent = sds((size, dim), F32 if first else BF16)
    kept = sds((size, dim), F32)
    rows = pltpu.VMEM((2 * size, units), BF16)
    scratch = [rows, rows, pltpu.VMEM((2, units, dim), BF16)]
    if not first:
        scratch = [pltpu.VMEM((dim, units), BF16), pltpu.VMEM((units, dim), BF16)] + scratch
    operands = (n2_other, n2_own, g_other, g_own, *weights, *before)
    return order.run(
        14.6,
        functools.partial(mlp_kernel, first),
        (place, *operands),
        [sent, kept, sent, kept] + [sds((2, units // count, dim), BF16)] * count,
        [SMEM] + [VMEM] * len(operands),
        after,
        scratch_shapes=scratch,
    )


def norm2_back_kernel(hidden, own, received, grad, gain, grad_hidden, low, sums):
    normed_grad = own[...] + received[...].astype(F32)
    scaled, inverse = normalize(hidden[...])
    total = grad[...].astype(F32) + norm_back(normed_grad, scaled, inverse, gain[...])
    grad_hidden[...] = total
    low[...] = total.astype(BF16)
    add_sums(sums, normed_grad, scaled)


def add_sums(sums, normed_grad, scaled):
    @pl.when(pl.program_id(0) == 0)
    def _():
        sums[...] = jnp.zeros(sums.shape, F32)

    sums[0:1, :] += jnp.sum(normed_grad * scaled, axis=0, keepdims=True)
    sums[1:2, :] += jnp.sum(normed_grad, axis=0, keepdims=True)


def norm2_back_call(order, hidden, own, received, grad, gain, after=()):
    size, dim = hidden.shape
    rows = rows_spec(size // 2, dim)
    return order.run(
        5,
        norm2_back_kernel,
        (hidden, own, received, grad, gain),
        [sds(hidden.shape, F32), sds(hidden.shape, BF16), sds((8, dim), F32)],
        [rows] * 4 + [whole((1, dim))],
        after,
        grid=(2,),
        out_specs=[rows, rows, whole((8, dim))],
    )


def mixed_kernel(place, hidden, own, received, near, far, out, keep, send, total):
    out[...] = (hidden[...] + (own[...] + received[...].astype(F32))).astype(BF16)
    total[...] = low_sum(near[...], far[...])
    split(place, 1, total, keep, send)


def mixed_call(order, place, hidden, own, received, near, far):
    groups, rows, dim = near.shape
    return order.run(
        4,
        mixed_kernel,
        (place, hidden, own, received, near, far),
        [sds(hidden.shape, BF16)] + [sds((groups, rows // 2, dim), BF16)] * 2,
        [SMEM] + [VMEM] * 5,
        scratch_shapes=[pltpu.VMEM(near.shape, BF16)],
    )


def backward_kernel(first, block, *refs):
    place, g_own, g_other, w_out, heads_out, qkv, lse, penalty, *refs = refs
    if not first:
        before, *refs = refs
    grads, w_grad, logit_sum, grad_full, key_sum, value_sum, *refs = refs
    third = qkv.shape[0] // 3
    seq = qkv.shape[1]
    half = seq // 2
    total = logit_sum if first else refs[0]
    core = place[0]
    grad_full[part_rows(core, half), :] = g_own[...]
    grad_full[part_rows(1 - core, half), :] = g_other[...]
    whole_grad = grad_full[...]
    grad_heads = dot(w_out[...], whole_grad, NT).astype(BF16)
    w_grad[...] = dot(heads_out[...], whole_grad, NN).astype(BF16)
    heads = third // HEAD_DIM
    for head in range(heads):
        rows = slice(head * HEAD_DIM, (head + 1) * HEAD_DIM)
        query = qkv[rows, :]
        key = qkv[third + head * HEAD_DIM : third + (head + 1) * HEAD_DIM, :]
        value = qkv[2 * third + head * HEAD_DIM : 2 * third + (head + 1) * HEAD_DIM, :]
        grad = grad_heads[rows]
        for low in range(0, seq, block):
            high = low + block
            cols = slice(low, high)
            score = dot(key[:, :high], query[:, cols], TN)
            probs = jnp.exp(score - penalty[:high, cols] - lse[head, :, cols])
            grad_probs = dot(value[:, :high], grad[:, cols], TN)
            row_dot = jnp.sum(probs * grad_probs, axis=0, keepdims=True)
            grad_logits = probs * (grad_probs - row_dot)
            if head:
                sum_now = total[:high, cols] + grad_logits
            elif first:
                sum_now = grad_logits
            else:
                sum_now = before[:high, cols] + grad_logits
            if first or head < heads - 1:
                total[:high, cols] = sum_now
            else:
                logit_sum[:high, cols] = sum_now.astype(BF16)
            low_logits = grad_logits.astype(BF16)
            low_probs = probs.astype(BF16)
            grads[rows, cols] = (dot(key[:, :high], low_logits, NN) * 0.125).astype(BF16)
            value_new = dot(grad[:, cols], low_probs, NT)
            key_new = dot(query[:, cols], low_logits, NT)
            if low:
                key_sum[head, :, :low] += key_new[:, :low]
                value_sum[head, :, :low] += value_new[:, :low]
            key_sum[head, :, cols] = key_new[:, low:]
            value_sum[head, :, cols] = value_new[:, low:]
        at = third + head * HEAD_DIM
        grads[at : at + HEAD_DIM, :] = key_sum[head].astype(BF16)
        at = at + third
        grads[at : at + HEAD_DIM, :] = value_sum[head].astype(BF16)


def backward_call(order, place, g_own, g_other, w_out, heads_out, qkv, lse, penalty, before=None):
    width, seq = qkv.shape
    heads = width // (3 * HEAD_DIM)
    first = before is None
    operands = (g_own, g_other, w_out, heads_out, qkv, lse, penalty)
    operands += () if first else (before,)
    sums = pltpu.VMEM((heads, HEAD_DIM, seq), F32)
    scratch = [pltpu.VMEM((seq, g_own.shape[1]), BF16), sums, sums]
    scratch += [] if first else [pltpu.VMEM((seq, seq), F32)]
    return order.run(
        16,
        functools.partial(backward_kernel, first, 256),
        (place, *operands),
        [
            sds((width, seq), BF16),
            sds(w_out.shape, BF16),
            sds((seq, seq), F32 if first else BF16),
        ],
        [SMEM] + [VMEM] * len(operands),
        scratch_shapes=scratch,
    )


def halves(value):
    high = value.astype(BF16)
    return high, (value - high.astype(F32)).astype(BF16)


def select_back(block, core, own, received, qk0, seg_pad, n1, out, w_grad, total_grad):
    seq = own.shape[0]
    q0 = qk0[:HEAD_DIM, :]
    k0 = qk0[HEAD_DIM:, :]
    seg_value = seg_pad[...]
    cols = seg_value.T
    later = lax.broadcasted_iota(jnp.int32, (block, block + 128), 0)
    earlier = lax.broadcasted_iota(jnp.int32, (block, block + 128), 1)
    sums = ((later > earlier) | (earlier >= block)).astype(F32).astype(BF16)
    carry = jnp.zeros((seq, 128), F32)
    total_grad[...] = jnp.zeros(total_grad.shape, F32)
    for low in range(seq - block, -1, -block):
        high = low + block
        logit_sum = own[:high, low:high].astype(F32) + received[:high, low:high].astype(F32)
        top, bottom = halves(logit_sum)
        total = dot(top, sums, NN) + dot(bottom, sums, NN)
        after = jnp.concatenate([carry[:high]] * (block // 128), axis=1)
        select_grad = -(total[:, :block] + after)
        carry = carry[:high] + total[:, block:]
        _, picked = masks(seg_value, cols, low, high)
        score = dot(k0[:, :high], q0[:, low:high], TN)
        through = jnp.where(picked, select_grad / (1.0 + jnp.exp(-score)), 0.0)
        top, bottom = halves(through)

        @pl.when(core == 0)
        def _():
            total_grad[:, low:high] = 0.125 * (
                dot(k0[:, :high], top, NN) + dot(k0[:, :high], bottom, NN)
            )

        @pl.when(core == 1)
        def _():
            total_grad[:, :high] += dot(q0[:, low:high], top, NT) + dot(
                q0[:, low:high], bottom, NT
            )

    out[...] = total_grad[...].astype(BF16)
    w_grad[...] = dot(out[...], n1[...], NN).astype(BF16)


def weights_first_kernel(place, n1, grads, weights, w_out, back, *refs):
    parts, total = refs[:4], refs[4]
    width = grads.shape[0]
    total[0, :width, :] = dot(grads[...], n1[...], NN).astype(BF16)
    total[0, width:, :] = w_out[...]
    scatter(place, total, parts)
    back[...] = dot(grads[...], weights[...], TT)


def weights_first_call(order, place, n1, grads, weights, w_out):
    seq, dim = n1.shape
    rows = grads.shape[0] + w_out.shape[0]
    return order.run(
        6,
        weights_first_kernel,
        (place, n1, grads, weights, w_out),
        [sds((seq, dim), F32)] + [sds((1, rows // 4, dim), BF16)] * 4,
        [SMEM] + [VMEM] * 4,
        scratch_shapes=[pltpu.VMEM((1, rows, dim), BF16)],
    )


def weights_second_kernel(place, n1, grads, w_out, *refs):
    parts_r, ff_terms, refs = refs[:4], refs[4:6], refs[6:]
    move_r, ff, *refs = refs
    parts, total = refs[:4], refs[4]
    width = grads.shape[0]
    move_r[...] = low_sum(*(part[...] for part in parts_r))
    ff[...] = low_sum(*(term[...] for term in ff_terms))
    total[0, :width, :] = dot(grads[...], n1[...], NN).astype(BF16)
    total[0, width:, :] = w_out[...]
    scatter(place, total, parts)


def weights_second_call(order, place, n1, grads, w_out, parts_r, ff_terms):
    dim = n1.shape[1]
    rows = grads.shape[0] + w_out.shape[0]
    part = sds((1, rows // 4, dim), BF16)
    return order.run(
        6,
        weights_second_kernel,
        (place, n1, grads, w_out, *parts_r, *ff_terms),
        [part, sds(ff_terms[0].shape, BF16)] + [part] * 4,
        [SMEM] + [VMEM] * 9,
        scratch_shapes=[pltpu.VMEM((1, rows, dim), BF16)],
    )


def norm1_grad_kernel(block, place, logit_own, logit_got, qk0, seg_pad, n1, grads, weights, first, *refs):
    before, gain, shift, sums2, own, send, late, extra, extra_w, total_grad = refs
    select_back(
        block, place[0], logit_own, logit_got, qk0, seg_pad, n1, extra, extra_w, total_grad
    )
    half = own.shape[0]
    mine = jnp.where(place[0] == 0, first[:, :HEAD_DIM], first[:, HEAD_DIM:])
    total = before[...] + dot(grads[...], weights[...], TT) + dot(extra[...], mine, TT)
    for core in range(2):

        @pl.when(place[0] == core)
        def _():
            own[...] = total[core * half : (core + 1) * half]
            send[...] = total[(1 - core) * half : (2 - core) * half].astype(BF16)

    scaled = (n1[...].astype(F32) - shift[...]) * (1.0 / gain[...])
    gain_sum = jnp.sum(total * scaled, axis=0, keepdims=True)
    shift_sum = jnp.sum(total, axis=0, keepdims=True)
    norms = jnp.concatenate([gain_sum, shift_sum, sums2[0:2, :], sums2[4:8, :]], axis=0)
    rows = extra_w.shape[0]
    late[:rows, :] = extra_w[...]
    high, low = halves(norms)
    late[rows : rows + 8, :] = high
    late[rows + 8 :, :] = low


def norm1_grad_call(order, place, logits, qk0, seg_pad, n1, grads, weights, first, *rest):
    seq, dim = n1.shape
    rows = HEAD_DIM
    return order.run(
        14,
        functools.partial(norm1_grad_kernel, 256),
        (place, *logits, qk0, seg_pad, n1, grads, weights, first, *rest),
        [
            sds((seq // 2, dim), F32),
            sds((seq // 2, dim), BF16),
            sds((rows + 16, dim), BF16),
        ],
        [SMEM] + [VMEM] * 12,
        scratch_shapes=[
            pltpu.VMEM((rows, seq), BF16),
            pltpu.VMEM((rows, dim), BF16),
            pltpu.VMEM((rows, seq), F32),
        ],
    )


def norm1_back_kernel(tokens, own, received, grad_hidden, gain, out):
    normed_grad = own[...] + received[...].astype(F32)
    scaled, inverse = normalize(tokens[...].astype(F32))
    total = grad_hidden[...] + norm_back(normed_grad, scaled, inverse, gain[...])
    out[...] = total.astype(BF16)


def norm1_back_call(order, tokens, own, received, grad_hidden, gain, after=()):
    size, dim = tokens.shape
    rows = rows_spec(size // 2, dim)
    return order.run(
        4,
        norm1_back_kernel,
        (tokens, own, received, grad_hidden, gain),
        sds(tokens.shape, BF16),
        [rows] * 4 + [whole((1, dim))],
        after,
        grid=(2,),
        out_specs=rows,
    )


def add_late(terms, out):
    def pairs(values):
        while len(values) > 1:
            values = [values[i] + values[i + 1] for i in range(0, len(values), 2)]
        return values[0]

    rows = out.shape[0] - 16
    out[:rows, :] = pairs([term[:rows, :].astype(F32) for term in terms]).astype(BF16)
    norms = pairs(
        [term[rows : rows + 8, :].astype(F32) + term[rows + 8 :, :].astype(F32) for term in terms]
    )
    high, low = halves(norms)
    out[rows : rows + 8, :] = high
    out[rows + 8 :, :] = low


def first_sums_kernel(*refs):
    near, far, *refs = refs
    *parts, ff, ff_move = refs
    ff[...] = low_sum(near[...], far[...])
    ff_move[...] = low_sum(*(part[...] for part in parts))


def first_sums_call(order, terms, parts):
    shape = sds(parts[0].shape, BF16)
    return order.run(3, first_sums_kernel, (*terms, *parts), [shape, shape])


def step0_kernel(own, got, out):
    out[...] = low_sum(own[...], got[...])


def step0_call(order, terms):
    return order.run(2, step0_kernel, terms, sds(terms[0].shape, BF16))


def step1_kernel(late_own, late_got, *refs):
    *at_terms, both = refs
    size = at_terms[0].shape[1]
    both[:size, :] = low_sum(*(term[0] for term in at_terms))
    add_late((late_own, late_got), both.at[size:, :])


def step1_call(order, late_terms, at_terms):
    _, size, dim = at_terms[0].shape
    rows = size + late_terms[0].shape[0]
    return order.run(3, step1_kernel, (*late_terms, *at_terms), sds((rows, dim), BF16))


def step2_kernel(size, place, own, got, *refs):
    *ff_parts, both, ff = refs
    both[:size, :] = low_sum(own[:size, :], got[:size, :])
    add_late((own.at[size:, :], got.at[size:, :]), both.at[size:, :])
    gather(place, ff_parts, ff)


def step2_call(order, place, size, own, got, ff_parts, after=()):
    groups, rows, dim = ff_parts[0].shape
    return order.run(
        4.5,
        functools.partial(step2_kernel, size),
        (place, own, got, *ff_parts),
        [sds(own.shape, BF16), sds((groups, 4 * rows, dim), BF16)],
        [SMEM] + [VMEM] * 6,
        after,
    )


def step3_kernel(size, place, *refs):
    parts, refs = refs[:4], refs[4:]
    mixed, grad, both, mixed_out, grad_out = refs
    for partner, part in enumerate(parts):
        both[part_rows(quarter(place) ^ partner, size), :] = part[:size, :]
    add_late([part.at[size:, :] for part in parts], both.at[4 * size :, :])
    mixed_out[...] = mixed[...]
    grad_out[...] = grad[...]


def step3_call(order, place, size, parts, mixed, grad):
    rows, dim = parts[0].shape
    return order.run(
        3.5,
        functools.partial(step3_kernel, size),
        (place, *parts, mixed, grad),
        [sds((rows + 3 * size, dim), BF16), sds(mixed.shape, BF16), sds(grad.shape, BF16)],
        [SMEM] + [VMEM] * 6,
    )


def finish_attention_kernel(place, near, far, w_query, w_key, w_value, w_out, *norms):
    width = w_out.shape[0] // 2
    late = 4 * width
    rows = late + HEAD_DIM
    total = jnp.zeros((8, near.shape[1]), F32)
    for ref in (near, far):
        total = total + (ref[rows : rows + 8, :].astype(F32) + ref[rows + 8 :, :].astype(F32))
    for i, out in enumerate(norms):
        out[...] = total[i]
    here = (place[1] == 0).astype(F32)
    for core in range(2):

        @pl.when(place[0] == core)
        def _():
            low, high = (near, far) if core == 0 else (far, near)
            for i, out in enumerate((w_query, w_key, w_value)):
                piece = slice(i * width, (i + 1) * width)
                part = low[piece, :].astype(F32)
                if i < 2:
                    more = here * (low, high)[i][late:rows, :].astype(F32)
                    part = jnp.concatenate([part[:HEAD_DIM] + more, part[HEAD_DIM:]], axis=0)
                out[...] = jnp.concatenate([part, high[piece, :].astype(F32)], axis=0).T
            w_out[:width, :] = low[3 * width : late, :].astype(F32)
            w_out[width:, :] = high[3 * width : late, :].astype(F32)


def finish_attention_call(order, place, width, near, far):
    dim = near.shape[1]
    return order.run(
        4.5,
        finish_attention_kernel,
        (place, near, far),
        [sds((dim, 2 * width), F32)] * 3 + [sds((2 * width, dim), F32)] + [sds((dim,), F32)] * 4,
        [SMEM] + [VMEM] * 2,
    )


def finish_mlp_kernel(place, near, far, w_up, w_down):
    units = near.shape[1]
    for core in range(2):

        @pl.when(place[0] == core)
        def _():
            low, high = (near, far) if core == 0 else (far, near)
            w_up[:, :units] = low[0].astype(F32)
            w_up[:, units:] = high[0].astype(F32)
            w_down[:units, :] = low[1].astype(F32)
            w_down[units:, :] = high[1].astype(F32)


def finish_mlp_call(order, place, near, far):
    _, units, dim = near.shape
    return order.run(
        6.8,
        finish_mlp_kernel,
        (place, near, far),
        [sds((dim, 2 * units), F32), sds((2 * units, dim), F32)],
        [SMEM] + [VMEM] * 2,
    )


def make_body(devices, parts):
    axes = ("dp", "tensor")
    chips = devices // 2
    in_order = [1 << bit for bit in range(chips.bit_length() - 1)]
    turned = [in_order[1], in_order[0], *in_order[2:]]
    rounds = len(in_order)
    rounds_more = range(3, rounds)

    def pairs(move):
        found = []
        for device in range(devices):
            for part in range(parts):
                to_chip, to_core, to_part = move(device // 2, device % 2, part)
                source = device * parts + part
                found.append((source, (to_chip * 2 + to_core) * parts + to_part))
        return found

    def by_bit(bit):
        return pairs(
            lambda chip, core, part: (chip ^ (turned if core else in_order)[bit], core, part)
        )

    by_role = pairs(lambda chip, core, part: (chip, part, core))
    by_core = pairs(lambda chip, core, part: (chip, 1 - core, part))
    by_part = pairs(lambda chip, core, part: (chip, core, 1 - part))
    from_first_part = [pair for pair in by_part if pair[0] % parts == 0]
    by_chip = [by_bit(bit) for bit in range(rounds)]

    def by_quarter(partner):
        def across(chip, core, part):
            for bit in range(2):
                if partner >> (1 - bit) & 1:
                    chip ^= (turned if core else in_order)[bit]
            return chip, core, part

        return pairs(across)

    def move(value, how):
        return lax.ppermute(value, axes, how)

    def add_more(value):
        for bit in rounds_more:
            other = move(value, by_chip[bit])
            value = (value.astype(F32) + other.astype(F32)).astype(value.dtype)
        return value

    def exchange(values):
        return [values[0]] + [move(values[i], by_quarter(i)) for i in range(1, 4)]

    def body(
        tokens,
        segment_ids,
        pad_mask,
        norm1_gain,
        norm1_shift,
        w_query,
        w_key,
        w_value,
        w_out,
        norm2_gain,
        norm2_shift,
        w_up,
        w_down,
        cotangent,
    ):
        order = Order()
        device = lax.axis_index("dp")
        part = lax.axis_index("tensor")
        core = device % 2
        chip = device // 2
        bits = [
            jnp.where(core == 1, (chip & turned[i]) != 0, (chip & in_order[i]) != 0)
            for i in range(rounds)
        ]
        place = jnp.stack([core, part] + bits).astype(jnp.int32)
        gain1, shift1, gain2, shift2 = (
            vector[None, :] for vector in (norm1_gain, norm1_shift, norm2_gain, norm2_shift)
        )

        mine = move(tokens, by_role)
        ints = jnp.concatenate([segment_ids, pad_mask], axis=0)
        ints = jnp.where(core == part, ints, move(ints, by_core)).astype(F32)
        seg_pad = jnp.concatenate([ints, jnp.zeros((6, ints.shape[1]), F32)], axis=0)

        qkv_l, qkv_s, first = pack_first_call(order, place, w_query, w_key, w_value)
        first_moved = move(first, from_first_part)
        qkv_near = move(qkv_s, by_part)
        n1_own = norm1_call(order, mine, gain1, shift1)
        n1_other = move(n1_own, by_core)
        out_l, up_l, up_s, down_l, down_s, grad = pack_last_call(
            order, place, w_out, w_up, w_down, cotangent
        )
        out_r = move(out_l, by_part)
        up_near = move(up_s, by_part)
        grad_own = move(grad, by_role)
        down_near = move(down_s, by_part)
        n1, penalty, qk0, first = penalty_call(
            order, place, n1_own, n1_other, first, first_moved, seg_pad
        )
        (qkv_near,) = order.hold((qkv_near,), (penalty,))
        qkv_far = move(qkv_near, by_chip[0])
        qkvt_l, heads_l, lse_l = forward_call(order, n1, (qkv_l,), penalty)
        qkvt_r, heads_r, lse_r, qkv_r, own, send = forward_call(
            order,
            n1,
            (qkv_near, qkv_far),
            penalty,
            place,
            (heads_l, out_l, out_r),
            (up_near,),
        )
        (send,) = order.hold((send,), (down_near,))
        (up_near,) = order.hold((up_near,), (lse_r,))
        up_far = move(up_near, by_chip[0])
        (grad_own,) = order.hold((grad_own,), (lse_r,))
        grad_other = move(grad_own, by_core)
        (down_near,) = order.hold((down_near,), (lse_r,))
        down_far = move(down_near, by_chip[0])
        hidden, n2_own = norm2_call(order, mine, own, move(send, by_core), gain2, shift2)
        n2_other = move(n2_own, by_core)
        *before, keep, send = mlp_call(
            order, place, n2_other, n2_own, grad_other, grad_own, (up_l, down_l)
        )
        got = move(send, by_chip[0])
        weights = (up_near, up_far, down_near, down_far)
        mixed_send, mixed_own, back_send, back_own, *ff_r = mlp_call(
            order, place, n2_other, n2_own, grad_other, grad_own, weights, before
        )
        back_send, mixed_send, *ff_r = order.hold((back_send, mixed_send, *ff_r), (got,))
        ff_r = exchange(ff_r)
        grad_hidden, low_own, sums2 = norm2_back_call(
            order, hidden, back_own, move(back_send, by_core), grad_own, gain2
        )
        low_other = move(low_own, by_core)
        mixed, keep, send = mixed_call(
            order, place, hidden, mixed_own, move(mixed_send, by_core), keep, got
        )
        got = move(send, by_chip[1])

        low = (low_own, low_other)
        grads_r, wo_r, logit_sum = backward_call(
            order, place, *low, out_r, heads_r, qkvt_r, lse_r, penalty
        )
        back, *at_r = weights_first_call(order, place, n1, grads_r, qkv_r, wo_r)
        ff, ff_move = first_sums_call(order, (keep, got), ff_r)
        ff_got = move(ff_move, by_part)
        at_r = exchange(at_r)
        grads_l, wo_l, logit_sum = backward_call(
            order, place, *low, out_l, heads_l, qkvt_l, lse_l, penalty, logit_sum
        )
        logit_got = move(logit_sum, by_core)
        at_r, ff, *at = weights_second_call(
            order, place, n1, grads_l, wo_l, at_r, (ff, ff_got)
        )
        at_r = move(at_r, by_part)
        ff_got = move(ff, by_chip[2])
        at = exchange(at)
        own, send, late = norm1_grad_call(
            order,
            place,
            (logit_sum, logit_got),
            qk0,
            seg_pad,
            n1,
            grads_l,
            qkv_l,
            first,
            back,
            gain1,
            shift1,
            sums2,
        )
        send, late = order.hold((send, late), (*at, at_r))
        received = move(send, by_core)
        late_got = move(late, by_part)
        ff = step0_call(order, (ff, ff_got))
        ff = exchange([add_more(ff)] * 4)
        both = step1_call(order, (late, late_got), (*at, at_r))
        size = at_r.shape[1]
        both_got = move(both, by_chip[2])
        tokens_grad = norm1_back_call(order, mine, own, received, grad_hidden, gain1)
        mixed, tokens_grad = order.hold((mixed, tokens_grad), (both_got,))
        mixed = move(mixed, by_role)
        tokens_grad = move(tokens_grad, by_role)
        both, ff = step2_call(order, place, size, both, both_got, ff)
        both = exchange([add_more(both)] * 4)
        ff_far = move(ff, by_core)
        up_grad, down_grad = finish_mlp_call(order, place, ff, ff_far)
        both, mixed, tokens_grad = step3_call(order, place, size, both, mixed, tokens_grad)
        query_grad, key_grad, value_grad, out_grad, *norms = finish_attention_call(
            order, place, size, both, move(both, by_core)
        )
        return (
            mixed,
            tokens_grad,
            norms[0],
            norms[1],
            query_grad,
            key_grad,
            value_grad,
            out_grad,
            norms[2],
            norms[3],
            up_grad,
            down_grad,
        )

    return body


def solution(mesh):
    in_specs = (
        P(("dp", "tensor"), None),
        P("dp", None),
        P("dp", None),
        P(),
        P(),
        P(None, "tensor"),
        P(None, "tensor"),
        P(None, "tensor"),
        P("tensor", None),
        P(),
        P(),
        P(None, "tensor"),
        P("tensor", None),
        P(("dp", "tensor"), None),
    )
    out_specs = (
        P(("dp", "tensor"), None),
        P(("dp", "tensor"), None),
        P(),
        P(),
        P(None, "tensor"),
        P(None, "tensor"),
        P(None, "tensor"),
        P("tensor", None),
        P(),
        P(),
        P(None, "tensor"),
        P("tensor", None),
    )
    body = make_body(mesh.shape["dp"], mesh.shape["tensor"])
    return jax.shard_map(body, mesh=mesh, in_specs=in_specs, out_specs=out_specs, check_vma=False)
```

```python
import functools

import jax
import jax.numpy as jnp
from jax import lax
from jax.experimental import pallas as pl
from jax.experimental.pallas import tpu as pltpu
from jax.sharding import PartitionSpec as P

HEAD_DIM = 64
EPS = 1e-05
FAR = 1e30
FORWARD_BLOCK = 512
BF16 = jnp.bfloat16
F32 = jnp.float32
TN = (((0,), (0,)), ((), ()))
NT = (((1,), (1,)), ((), ()))
NN = (((1,), (0,)), ((), ()))
TT = (((0,), (1,)), ((), ()))
ERF_C = (
    1.5897294934128858e-07,
    -5.985900079472216e-06,
    8.971378204617447e-05,
    -0.0006257225011275588,
    -0.0001843806018428344,
    0.10276548023357895,
    1.1283797055884355,
)
ERF_X = tuple(c * 0.5 ** (6 - i) * 0.7071067811865476 for i, c in enumerate(ERF_C))


def dot(left, right, dims):
    return lax.dot_general(left, right, dims, preferred_element_type=F32)


def sds(shape, dtype):
    return jax.ShapeDtypeStruct(shape, dtype)


SMEM = pl.BlockSpec(memory_space=pltpu.SMEM)
VMEM = pl.BlockSpec(memory_space=pltpu.VMEM)
ANY = pl.BlockSpec(memory_space=pl.ANY)


WEIGHT = 20.0


class Order:
    def __init__(self):
        self.last = None

    def run(self, us, kernel, operands, out_shape, in_specs=None, after=(), **rest):
        after = tuple(after) + (() if self.last is None else (self.last,))
        count, extra = len(operands), len(after)
        in_specs = list(in_specs or [VMEM] * count) + [ANY] * extra

        def body(*refs):
            kernel(*refs[:count], *refs[count + extra :])

        out = pl.pallas_call(
            body,
            out_shape=out_shape,
            in_specs=in_specs,
            compiler_params=pltpu.CompilerParams(vmem_limit_bytes=58 << 20),
            cost_estimate=pl.CostEstimate(
                flops=int(us * WEIGHT * 1.15e9), bytes_accessed=0, transcendentals=0
            ),
            **rest,
        )(*operands, *after)
        self.last = out[-1] if isinstance(out, (list, tuple)) else out
        return out

    def hold(self, values, after):
        count = len(values)

        def kernel(*refs):
            pass

        held = pl.pallas_call(
            kernel,
            out_shape=[sds(value.shape, value.dtype) for value in values],
            in_specs=[ANY] * (count + len(after)),
            out_specs=[ANY] * count,
            input_output_aliases={i: i for i in range(count)},
            compiler_params=pltpu.CompilerParams(has_side_effects=True),
            cost_estimate=pl.CostEstimate(flops=0, bytes_accessed=0, transcendentals=0),
        )(*values, *after)
        for value, same in zip(values, held):
            if self.last is value:
                self.last = same
        return held


def whole(shape):
    return pl.BlockSpec(shape, lambda *_: (0,) * len(shape))


def low_sum(*terms):
    total = terms[0].astype(F32)
    for term in terms[1:]:
        total = total + term.astype(F32)
    return total.astype(BF16)


def part_rows(index, size):
    return pl.ds(pl.multiple_of(index * size, size), size)


def split(place, bit, source, keep, send):
    half = keep.shape[1]
    keep[...] = source[:, part_rows(place[2 + bit], half), :]
    send[...] = source[:, part_rows(1 - place[2 + bit], half), :]


def quarter(place):
    return 2 * place[2] + place[3]


def scatter(place, source, outs):
    for partner, out in enumerate(outs):
        out[...] = source[:, part_rows(quarter(place) ^ partner, out.shape[1]), :]


def gather(place, pieces, out):
    for partner, piece in enumerate(pieces):
        out[:, part_rows(quarter(place) ^ partner, piece.shape[1]), :] = piece[...]


def normalize(values):
    center = values - jnp.mean(values, axis=-1, keepdims=True)
    inverse = lax.rsqrt(jnp.mean(center * center, axis=-1, keepdims=True) + EPS)
    return center * inverse, inverse


def norm_back(grad_normed, scaled, inverse, gain):
    grad_scaled = grad_normed * gain
    return inverse * (
        grad_scaled
        - jnp.mean(grad_scaled, axis=-1, keepdims=True)
        - scaled * jnp.mean(grad_scaled * scaled, axis=-1, keepdims=True)
    )


def gelu_pair(x):
    square = x * x
    near = jnp.minimum(square, 64.0)
    poly = ERF_X[0]
    for coefficient in ERF_X[1:]:
        poly = poly * near + coefficient
    phi = 0.5 * jnp.tanh(x * poly) + 0.5
    bell = jnp.exp(square * -0.5)
    return x * phi, phi + x * (bell * 0.3989422804014327)


def pack_first_kernel(place, w_query, w_key, w_value, qkv, qkv_send, first):
    width = qkv.shape[1] // 3
    half = qkv_send.shape[0]
    first[:, :HEAD_DIM] = w_query[:, :HEAD_DIM]
    first[:, HEAD_DIM:] = w_key[:, :HEAD_DIM]
    for core in range(2):

        @pl.when(place[0] == core)
        def _():
            narrow = slice(core * width, (core + 1) * width)
            for i, weight in enumerate((w_query, w_key, w_value)):
                qkv[:, i * width : (i + 1) * width] = weight[:, narrow]

    qkv_send[...] = qkv[pl.ds(pl.multiple_of(place[2] * half, half), half), :]


def pack_first_call(order, place, w_query, w_key, w_value):
    dim, width = w_query.shape[0], w_query.shape[1] // 2
    return order.run(
        4,
        pack_first_kernel,
        (place, w_query, w_key, w_value),
        [
            sds((dim, 3 * width), BF16),
            sds((dim // 2, 3 * width), BF16),
            sds((dim, 2 * HEAD_DIM), BF16),
        ],
        [SMEM] + [VMEM] * 3,
    )


def pack_last_kernel(place, w_out, w_up, w_down, grad, out, up, up_send, down, down_send, grad_out):
    width = out.shape[0]
    units = down.shape[0]
    half = units // 2
    grad_out[...] = grad[...]
    for core in range(2):

        @pl.when(place[0] == core)
        def _():
            wide = slice(core * units, (core + 1) * units)
            out[...] = w_out[core * width : (core + 1) * width, :]
            up[...] = w_up[:, wide]
            down[...] = w_down[wide, :]

    rows = pl.ds(pl.multiple_of(place[2] * half, half), half)
    up_send[...] = up[rows, :]
    down_send[...] = down[rows, :]


def pack_last_call(order, place, w_out, w_up, w_down, grad):
    width, dim = w_out.shape[0] // 2, w_out.shape[1]
    units = w_up.shape[1] // 2
    return order.run(
        5,
        pack_last_kernel,
        (place, w_out, w_up, w_down, grad),
        [
            sds((width, dim), BF16),
            sds((dim, units), BF16),
            sds((dim // 2, units), BF16),
            sds((units, dim), BF16),
            sds((units // 2, dim), BF16),
            sds(grad.shape, BF16),
        ],
        [SMEM] + [VMEM] * 4,
    )


def norm1_kernel(tokens, gain, shift, out):
    scaled, _ = normalize(tokens[...].astype(F32))
    out[...] = (scaled * gain[...] + shift[...]).astype(BF16)


def rows_spec(block, dim):
    return pl.BlockSpec((block, dim), lambda i: (i, 0))


def norm1_call(order, tokens, gain, shift):
    return order.run(2.5, norm1_kernel, (tokens, gain, shift), sds(tokens.shape, BF16))


def masks(seg_pad, cols, low, high):
    width = high - low
    seg_row = seg_pad[0:1, low:high]
    pad_row = seg_pad[1:2, low:high]
    row_key = jnp.where(pad_row > 0, seg_row, -2.0)
    col_seg = cols[:high, 0:1]
    col_pad = cols[:high, 1:2]
    col_key = jnp.where(col_pad > 0, col_seg, -1.0)
    key_at = lax.broadcasted_iota(jnp.int32, (high, width), 0)
    query_at = lax.broadcasted_iota(jnp.int32, (high, width), 1) + low
    allowed = ((col_key == seg_row) & (key_at <= query_at)) | (key_at == query_at)
    picked = (col_key == row_key) & (key_at < query_at)
    return allowed, picked


def penalty_kernel(
    block, place, n1_own, n1_other, first, first_moved, seg_pad, n1_out, penalty, qk0, first_out
):
    seq = n1_out.shape[0]
    half = seq // 2
    core = place[0]
    n1_out[pl.ds(pl.multiple_of(core * half, half), half), :] = n1_own[...]
    n1_out[pl.ds(pl.multiple_of((1 - core) * half, half), half), :] = n1_other[...]

    @pl.when(place[1] == 0)
    def _():
        first_out[...] = first[...]

    @pl.when(place[1] != 0)
    def _():
        first_out[...] = first_moved[...]

    qk = dot(first_out[...], n1_out[...], TT)
    q0 = (qk[:HEAD_DIM].astype(BF16) * 0.125).astype(BF16)
    k0 = qk[HEAD_DIM:].astype(BF16)
    qk0[:HEAD_DIM, :] = q0
    qk0[HEAD_DIM:, :] = k0
    seg_value = seg_pad[...]
    cols = seg_value.T
    earlier = lax.broadcasted_iota(jnp.int32, (block, block + 128), 0)
    later = lax.broadcasted_iota(jnp.int32, (block, block + 128), 1)
    sums = ((earlier < later) | (later >= block)).astype(F32).astype(BF16)
    carry = jnp.zeros((seq, 128), F32)
    for low in range(0, seq, block):
        high = low + block
        allowed, picked = masks(seg_value, cols, low, high)
        score = dot(k0[:, :high], q0[:, low:high], TN)
        small = jnp.exp(-jnp.abs(score))
        log1p = jnp.where(small < 1e-3, small - 0.5 * small * small, jnp.log(1.0 + small))
        select = jnp.where(picked, jnp.maximum(score, 0.0) + log1p, 0.0).astype(BF16)
        total = dot(select, sums, NN)
        before = jnp.concatenate([carry[:high]] * (block // 128), axis=1)
        penalty[:high, low:high] = jnp.where(allowed, total[:, :block] + before, FAR)
        if high % FORWARD_BLOCK:
            edge = high + FORWARD_BLOCK - high % FORWARD_BLOCK
            penalty[high:edge, low:high] = jnp.full((edge - high, block), FAR, F32)
        carry = jnp.concatenate([carry[:high] + total[:, block:], carry[high:]], axis=0)


def penalty_call(order, place, n1_own, n1_other, first, first_moved, seg_pad, after=()):
    half, dim = n1_own.shape
    seq = 2 * half
    return order.run(
        6.5,
        functools.partial(penalty_kernel, 256),
        (place, n1_own, n1_other, first, first_moved, seg_pad),
        [
            sds((seq, dim), BF16),
            sds((seq, seq), F32),
            sds((2 * HEAD_DIM, seq), BF16),
            sds(first.shape, BF16),
        ],
        [SMEM] + [VMEM] * 5,
        after,
    )


def forward_kernel(block, last, *refs):
    if last:
        place, n1, near, far, penalty, out_l, w_l, w_r, *refs = refs
        qkv, out, lse, weights, own, send, out_r = refs
    else:
        n1, weights, penalty, qkv, out, lse = refs
    head = pl.program_id(0)
    third = qkv.shape[0] // 3
    seq = qkv.shape[1]

    @pl.when(head == 0)
    def _():
        if last:
            join(place[2], weights, near, far)
        product = dot(weights[...], n1[...], TT).astype(BF16)
        qkv[:third, :] = (product[:third] * 0.125).astype(BF16)
        qkv[third:, :] = product[third:]

    at = pl.multiple_of(head * HEAD_DIM, HEAD_DIM)
    query = qkv[pl.ds(at, HEAD_DIM), :]
    key = qkv[pl.ds(third + at, HEAD_DIM), :]
    value = qkv[pl.ds(2 * third + at, HEAD_DIM), :]
    value = jnp.concatenate([value, jnp.ones((16, seq), BF16)], axis=0)
    for low in range(0, seq, block):
        high = low + block
        logits = dot(key[:, :high], query[:, low:high], TN) - penalty[:high, low:high]
        largest = jnp.max(logits, axis=0, keepdims=True)
        weight = jnp.exp(logits - largest).astype(BF16)
        result = dot(value[:, :high], weight, NN)
        total = result[HEAD_DIM : HEAD_DIM + 1, :]
        out[:, low:high] = (result[:HEAD_DIM] / total).astype(BF16)
        lse[:, low:high] = largest + jnp.log(total)
    if last:
        out_r[pl.ds(at, HEAD_DIM), :] = out[...]

        @pl.when(head == pl.num_programs(0) - 1)
        def _():
            project(place, out_l, out_r, w_l, w_r, own, send)


def join(bit, out, near, far):
    half = near.shape[0]
    out[pl.ds(pl.multiple_of(bit * half, half), half), :] = near[...]
    out[pl.ds(pl.multiple_of((1 - bit) * half, half), half), :] = far[...]


def forward_call(order, n1, weights, penalty, place=None, others=(), after=()):
    seq, dim = n1.shape
    last = place is not None
    width = weights[0].shape[1]
    heads = width // (3 * HEAD_DIM)
    operands = ((place,) if last else ()) + (n1,) + tuple(weights) + (penalty,) + tuple(others)
    in_specs = [SMEM] if last else []
    in_specs += [whole(x.shape) for x in operands if x is not place]
    out_specs = [
        whole((width, seq)),
        pl.BlockSpec((HEAD_DIM, seq), lambda h: (h, 0)),
        pl.BlockSpec((None, 1, seq), lambda h: (h, 0, 0)),
    ]
    out_shape = [
        sds((width, seq), BF16),
        sds((heads * HEAD_DIM, seq), BF16),
        sds((heads, 1, seq), F32),
    ]
    scratch = []
    if last:
        out_specs += [whole((dim, width)), whole((seq // 2, dim)), whole((seq // 2, dim))]
        out_shape += [sds((dim, width), BF16), sds((seq // 2, dim), F32), sds((seq // 2, dim), BF16)]
        scratch.append(pltpu.VMEM((heads * HEAD_DIM, seq), BF16))
    return order.run(
        10,
        functools.partial(forward_kernel, FORWARD_BLOCK, last),
        operands,
        out_shape,
        in_specs,
        after,
        grid=(heads,),
        out_specs=out_specs,
        scratch_shapes=scratch,
    )


def project(place, out_l, out_r, w_l, w_r, own, send):
    half = own.shape[0]
    core = place[0]
    mixed = jnp.concatenate([w_l[...], w_r[...]], axis=0)

    def part(which):
        heads = jnp.concatenate([out_l[:, part_rows(which, half)], out_r[:, part_rows(which, half)]], axis=0)
        return dot(heads, mixed, TN)

    send[...] = part(1 - core).astype(BF16)
    own[...] = part(core)


def norm2_kernel(tokens, own, received, gain, shift, hidden, out):
    total = tokens[...].astype(F32) + (own[...] + received[...].astype(F32))
    hidden[...] = total
    scaled, _ = normalize(total)
    out[...] = (scaled * gain[...] + shift[...]).astype(BF16)


def norm2_call(order, tokens, own, received, gain, shift, after=()):
    size, dim = tokens.shape
    rows = rows_spec(size // 2, dim)
    vector = whole((1, dim))
    return order.run(
        4,
        norm2_kernel,
        (tokens, own, received, gain, shift),
        [sds(tokens.shape, F32), sds(tokens.shape, BF16)],
        [rows] * 3 + [vector] * 2,
        after,
        grid=(2,),
        out_specs=[rows, rows],
    )


def mlp_kernel(first, *refs):
    place, n2_other, n2_own, g_other, g_own, *refs = refs
    if first:
        w_up, w_down, *refs = refs
        before = (None,) * 4
    else:
        up_near, up_far, down_near, down_far, *refs = refs
        before, refs = refs[:4], refs[4:]
    outs, refs = refs[:4], refs[4:]
    count = 2 if first else 4
    parts, refs = refs[:count], refs[count:]
    if not first:
        w_up, w_down, *refs = refs
        join(place[2], w_up, up_near, up_far)
        join(place[2], w_down, down_near, down_far)
    actives, grad_ups, w_grads = refs
    size = n2_own.shape[0]

    def put(out, rows, value, more):
        out[rows, :] = (value if more is None else value + more[rows, :].astype(F32)).astype(out.dtype)

    block = min(256, size)
    for at, n2, g in ((0, n2_other, g_other), (1, n2_own, g_own)):

        def work(step, _):
            rows = part_rows(step, block)
            here = part_rows(step + at * (size // block), block)
            active, slope = gelu_pair(dot(n2[rows, :], w_up[...], NN))
            active = active.astype(BF16)
            grad_up = (dot(g[rows, :], w_down[...], NT) * slope).astype(BF16)
            actives[here, :] = active
            grad_ups[here, :] = grad_up
            put(outs[2 + at], rows, dot(grad_up, w_up[...], NT), before[2 + at])
            put(outs[at], rows, dot(active, w_down[...], NN), before[at])
            return 0

        lax.fori_loop(0, size // block, work, 0)
    w_grads[0] = (
        dot(n2_other[...], grad_ups[:size, :], TN) + dot(n2_own[...], grad_ups[size:, :], TN)
    ).astype(BF16)
    w_grads[1] = (
        dot(actives[:size, :], g_other[...], TN) + dot(actives[size:, :], g_own[...], TN)
    ).astype(BF16)
    if first:
        split(place, 0, w_grads, *parts)
    else:
        scatter(place, w_grads, parts)


def mlp_call(order, place, n2_other, n2_own, g_other, g_own, weights, before=(), after=()):
    size, dim = n2_own.shape
    first = not before
    units = weights[0].shape[1]
    count = 2 if first else 4
    sent = sds((size, dim), BF16)
    kept = sent
    rows = pltpu.VMEM((2 * size, units), BF16)
    scratch = [rows, rows, pltpu.VMEM((2, units, dim), BF16)]
    if not first:
        scratch = [pltpu.VMEM((dim, units), BF16), pltpu.VMEM((units, dim), BF16)] + scratch
    operands = (n2_other, n2_own, g_other, g_own, *weights, *before)
    return order.run(
        14.6,
        functools.partial(mlp_kernel, first),
        (place, *operands),
        [sent, kept, sent, kept] + [sds((2, units // count, dim), BF16)] * count,
        [SMEM] + [VMEM] * len(operands),
        after,
        scratch_shapes=scratch,
    )


def norm2_back_kernel(hidden, own, received, grad, gain, grad_hidden, low, sums):
    normed_grad = own[...].astype(F32) + received[...].astype(F32)
    scaled, inverse = normalize(hidden[...])
    total = grad[...].astype(F32) + norm_back(normed_grad, scaled, inverse, gain[...])
    grad_hidden[...] = total
    low[...] = total.astype(BF16)
    add_sums(sums, normed_grad, scaled)


def add_sums(sums, normed_grad, scaled):
    @pl.when(pl.program_id(0) == 0)
    def _():
        sums[...] = jnp.zeros(sums.shape, F32)

    sums[0:1, :] += jnp.sum(normed_grad * scaled, axis=0, keepdims=True)
    sums[1:2, :] += jnp.sum(normed_grad, axis=0, keepdims=True)


def norm2_back_call(order, hidden, own, received, grad, gain, after=()):
    size, dim = hidden.shape
    rows = rows_spec(size // 2, dim)
    return order.run(
        5,
        norm2_back_kernel,
        (hidden, own, received, grad, gain),
        [sds(hidden.shape, F32), sds(hidden.shape, BF16), sds((8, dim), F32)],
        [rows] * 4 + [whole((1, dim))],
        after,
        grid=(2,),
        out_specs=[rows, rows, whole((8, dim))],
    )


def half_sums_kernel(place, near, far, keep, send):
    half = keep.shape[1]
    for out, which in ((keep, place[3]), (send, 1 - place[3])):
        rows = part_rows(which, half)
        out[...] = low_sum(near[:, rows, :], far[:, rows, :])


def half_sums_call(order, place, near, far):
    groups, rows, dim = near.shape
    return order.run(
        3,
        half_sums_kernel,
        (place, near, far),
        [sds((groups, rows // 2, dim), BF16)] * 2,
        [SMEM] + [VMEM] * 2,
    )


def backward_kernel(first, block, *refs):
    place, g_own, g_other, w_out, heads_out, qkv, lse, penalty, *refs = refs
    if not first:
        before, *refs = refs
    grads, w_grad, logit_sum, grad_full, key_sum, value_sum, *refs = refs
    third = qkv.shape[0] // 3
    seq = qkv.shape[1]
    half = seq // 2
    total = logit_sum if first else refs[0]
    core = place[0]
    grad_full[part_rows(core, half), :] = g_own[...]
    grad_full[part_rows(1 - core, half), :] = g_other[...]
    whole_grad = grad_full[...]
    grad_heads = dot(w_out[...], whole_grad, NT).astype(BF16)
    w_grad[...] = dot(heads_out[...], whole_grad, NN).astype(BF16)
    heads = third // HEAD_DIM
    for head in range(heads):
        rows = slice(head * HEAD_DIM, (head + 1) * HEAD_DIM)
        query = qkv[rows, :]
        key = qkv[third + head * HEAD_DIM : third + (head + 1) * HEAD_DIM, :]
        value = qkv[2 * third + head * HEAD_DIM : 2 * third + (head + 1) * HEAD_DIM, :]
        grad = grad_heads[rows]
        for low in range(0, seq, block):
            high = low + block
            cols = slice(low, high)
            score = dot(key[:, :high], query[:, cols], TN)
            probs = jnp.exp(score - penalty[:high, cols] - lse[head, :, cols])
            grad_probs = dot(value[:, :high], grad[:, cols], TN)
            row_dot = jnp.sum(probs * grad_probs, axis=0, keepdims=True)
            grad_logits = probs * (grad_probs - row_dot)
            if head:
                sum_now = total[:high, cols] + grad_logits
            elif first:
                sum_now = grad_logits
            else:
                sum_now = before[:high, cols] + grad_logits
            if first or head < heads - 1:
                total[:high, cols] = sum_now
            else:
                logit_sum[:high, cols] = sum_now.astype(BF16)
            low_logits = grad_logits.astype(BF16)
            low_probs = probs.astype(BF16)
            grads[rows, cols] = (dot(key[:, :high], low_logits, NN) * 0.125).astype(BF16)
            value_new = dot(grad[:, cols], low_probs, NT)
            key_new = dot(query[:, cols], low_logits, NT)
            if low:
                key_sum[head, :, :low] += key_new[:, :low]
                value_sum[head, :, :low] += value_new[:, :low]
            key_sum[head, :, cols] = key_new[:, low:]
            value_sum[head, :, cols] = value_new[:, low:]
        at = third + head * HEAD_DIM
        grads[at : at + HEAD_DIM, :] = key_sum[head].astype(BF16)
        at = at + third
        grads[at : at + HEAD_DIM, :] = value_sum[head].astype(BF16)


def backward_call(order, place, g_own, g_other, w_out, heads_out, qkv, lse, penalty, before=None):
    width, seq = qkv.shape
    heads = width // (3 * HEAD_DIM)
    first = before is None
    operands = (g_own, g_other, w_out, heads_out, qkv, lse, penalty)
    operands += () if first else (before,)
    sums = pltpu.VMEM((heads, HEAD_DIM, seq), F32)
    scratch = [pltpu.VMEM((seq, g_own.shape[1]), BF16), sums, sums]
    scratch += [] if first else [pltpu.VMEM((seq, seq), F32)]
    return order.run(
        16,
        functools.partial(backward_kernel, first, 256),
        (place, *operands),
        [
            sds((width, seq), BF16),
            sds(w_out.shape, BF16),
            sds((seq, seq), F32 if first else BF16),
        ],
        [SMEM] + [VMEM] * len(operands),
        scratch_shapes=scratch,
    )


def halves(value):
    high = value.astype(BF16)
    return high, (value - high.astype(F32)).astype(BF16)


def select_back(block, core, own, received, qk0, seg_pad, n1, out, w_grad, total_grad):
    seq = own.shape[0]
    q0 = qk0[:HEAD_DIM, :]
    k0 = qk0[HEAD_DIM:, :]
    seg_value = seg_pad[...]
    cols = seg_value.T
    later = lax.broadcasted_iota(jnp.int32, (block, block + 128), 0)
    earlier = lax.broadcasted_iota(jnp.int32, (block, block + 128), 1)
    sums = ((later > earlier) | (earlier >= block)).astype(F32).astype(BF16)
    carry = jnp.zeros((seq, 128), F32)
    total_grad[...] = jnp.zeros(total_grad.shape, F32)
    for low in range(seq - block, -1, -block):
        high = low + block
        logit_sum = own[:high, low:high].astype(F32) + received[:high, low:high].astype(F32)
        top, bottom = halves(logit_sum)
        total = dot(top, sums, NN) + dot(bottom, sums, NN)
        after = jnp.concatenate([carry[:high]] * (block // 128), axis=1)
        select_grad = -(total[:, :block] + after)
        carry = carry[:high] + total[:, block:]
        _, picked = masks(seg_value, cols, low, high)
        score = dot(k0[:, :high], q0[:, low:high], TN)
        through = jnp.where(picked, select_grad / (1.0 + jnp.exp(-score)), 0.0)
        top, bottom = halves(through)

        @pl.when(core == 0)
        def _():
            total_grad[:, low:high] = 0.125 * (
                dot(k0[:, :high], top, NN) + dot(k0[:, :high], bottom, NN)
            )

        @pl.when(core == 1)
        def _():
            total_grad[:, :high] += dot(q0[:, low:high], top, NT) + dot(
                q0[:, low:high], bottom, NT
            )

    out[...] = total_grad[...].astype(BF16)
    w_grad[...] = dot(out[...], n1[...], NN).astype(BF16)


def weights_first_kernel(place, n1, grads, w_out, *refs):
    parts, total = refs[:4], refs[4]
    width = grads.shape[0]
    total[0, :width, :] = dot(grads[...], n1[...], NN).astype(BF16)
    total[0, width:, :] = w_out[...]
    scatter(place, total, parts)


def weights_first_call(order, place, n1, grads, w_out):
    dim = n1.shape[1]
    rows = grads.shape[0] + w_out.shape[0]
    return order.run(
        4,
        weights_first_kernel,
        (place, n1, grads, w_out),
        [sds((1, rows // 4, dim), BF16)] * 4,
        [SMEM] + [VMEM] * 3,
        scratch_shapes=[pltpu.VMEM((1, rows, dim), BF16)],
    )


def weights_second_kernel(place, n1, grads, w_out, *refs):
    parts_r, ff_terms, refs = refs[:4], refs[4:6], refs[6:]
    move_r, ff, *refs = refs
    parts, total = refs[:4], refs[4]
    width = grads.shape[0]
    move_r[...] = low_sum(*(part[...] for part in parts_r))
    ff[...] = low_sum(*(term[...] for term in ff_terms))
    total[0, :width, :] = dot(grads[...], n1[...], NN).astype(BF16)
    total[0, width:, :] = w_out[...]
    scatter(place, total, parts)


def weights_second_call(order, place, n1, grads, w_out, parts_r, ff_terms):
    dim = n1.shape[1]
    rows = grads.shape[0] + w_out.shape[0]
    part = sds((1, rows // 4, dim), BF16)
    return order.run(
        6,
        weights_second_kernel,
        (place, n1, grads, w_out, *parts_r, *ff_terms),
        [part, sds(ff_terms[0].shape, BF16)] + [part] * 4,
        [SMEM] + [VMEM] * 9,
        scratch_shapes=[pltpu.VMEM((1, rows, dim), BF16)],
    )


def norm1_grad_kernel(block, place, logit_own, logit_got, qk0, seg_pad, n1, grads, weights, first, *refs):
    grads_r, weights_r, gain, shift, sums2, own, send, late, extra, extra_w, total_grad = refs
    select_back(
        block, place[0], logit_own, logit_got, qk0, seg_pad, n1, extra, extra_w, total_grad
    )
    half = own.shape[0]
    mine = jnp.where(place[0] == 0, first[:, :HEAD_DIM], first[:, HEAD_DIM:])
    total = dot(grads[...], weights[...], TT) + dot(grads_r[...], weights_r[...], TT)
    total = total + dot(extra[...], mine, TT)
    for core in range(2):

        @pl.when(place[0] == core)
        def _():
            own[...] = total[core * half : (core + 1) * half]
            send[...] = total[(1 - core) * half : (2 - core) * half].astype(BF16)

    scaled = (n1[...].astype(F32) - shift[...]) * (1.0 / gain[...])
    gain_sum = jnp.sum(total * scaled, axis=0, keepdims=True)
    shift_sum = jnp.sum(total, axis=0, keepdims=True)
    norms = jnp.concatenate([gain_sum, shift_sum, sums2[0:2, :], sums2[4:8, :]], axis=0)
    rows = extra_w.shape[0]
    late[:rows, :] = extra_w[...]
    high, low = halves(norms)
    late[rows : rows + 8, :] = high
    late[rows + 8 :, :] = low


def norm1_grad_call(order, place, logits, qk0, seg_pad, n1, grads, weights, first, *rest):
    seq, dim = n1.shape
    rows = HEAD_DIM
    return order.run(
        14,
        functools.partial(norm1_grad_kernel, 256),
        (place, *logits, qk0, seg_pad, n1, grads, weights, first, *rest),
        [
            sds((seq // 2, dim), F32),
            sds((seq // 2, dim), BF16),
            sds((rows + 16, dim), BF16),
        ],
        [SMEM] + [VMEM] * 13,
        scratch_shapes=[
            pltpu.VMEM((rows, seq), BF16),
            pltpu.VMEM((rows, dim), BF16),
            pltpu.VMEM((rows, seq), F32),
        ],
    )


def results_kernel(tokens, own, received, grad_hidden, gain, hidden, mixed_own, mixed_received, out):
    mixed = hidden[...] + (mixed_own[...].astype(F32) + mixed_received[...].astype(F32))
    out[0] = mixed.astype(BF16)
    normed_grad = own[...] + received[...].astype(F32)
    scaled, inverse = normalize(tokens[...].astype(F32))
    total = grad_hidden[...] + norm_back(normed_grad, scaled, inverse, gain[...])
    out[1] = total.astype(BF16)


def results_call(order, tokens, own, received, grad_hidden, gain, hidden, mixed_own, mixed_received):
    size, dim = tokens.shape
    rows = rows_spec(size // 2, dim)
    return order.run(
        5,
        results_kernel,
        (tokens, own, received, grad_hidden, gain, hidden, mixed_own, mixed_received),
        sds((2, size, dim), BF16),
        [rows] * 4 + [whole((1, dim))] + [rows] * 3,
        grid=(2,),
        out_specs=pl.BlockSpec((2, size // 2, dim), lambda i: (0, i, 0)),
    )


def add_late(terms, out):
    def pairs(values):
        while len(values) > 1:
            values = [values[i] + values[i + 1] for i in range(0, len(values), 2)]
        return values[0]

    rows = out.shape[0] - 16
    out[:rows, :] = pairs([term[:rows, :].astype(F32) for term in terms]).astype(BF16)
    norms = pairs(
        [term[rows : rows + 8, :].astype(F32) + term[rows + 8 :, :].astype(F32) for term in terms]
    )
    high, low = halves(norms)
    out[rows : rows + 8, :] = high
    out[rows + 8 :, :] = low


def first_sums_kernel(*refs):
    near, far, *refs = refs
    *parts, ff, ff_move = refs
    ff[...] = low_sum(near[...], far[...])
    ff_move[...] = low_sum(*(part[...] for part in parts))


def first_sums_call(order, terms, parts):
    shape = sds(parts[0].shape, BF16)
    return order.run(3, first_sums_kernel, (*terms, *parts), [shape, shape])


def step0_kernel(own, got, out):
    out[...] = low_sum(own[...], got[...])


def step0_call(order, terms):
    return order.run(2, step0_kernel, terms, sds(terms[0].shape, BF16))


def step1_kernel(late_own, late_got, *refs):
    *at_terms, both = refs
    size = at_terms[0].shape[1]
    both[:size, :] = low_sum(*(term[0] for term in at_terms))
    add_late((late_own, late_got), both.at[size:, :])


def step1_call(order, late_terms, at_terms):
    _, size, dim = at_terms[0].shape
    rows = size + late_terms[0].shape[0]
    return order.run(3, step1_kernel, (*late_terms, *at_terms), sds((rows, dim), BF16))


def step2_kernel(size, place, own, got, *refs):
    *parts, both, ff = refs
    both[:size, :] = low_sum(own[:size, :], got[:size, :])
    add_late((own.at[size:, :], got.at[size:, :]), both.at[size:, :])
    gather(place, parts, ff)


def step2_call(order, place, size, own, got, parts):
    groups, rows, dim = parts[0].shape
    return order.run(
        4.5,
        functools.partial(step2_kernel, size),
        (place, own, got, *parts),
        [sds(own.shape, BF16), sds((groups, 4 * rows, dim), BF16)],
        [SMEM] + [VMEM] * 6,
    )


def step3_kernel(size, place, *refs):
    parts, refs = refs[:4], refs[4:]
    results, both, mixed_out, grad_out = refs
    for partner, part in enumerate(parts):
        both[part_rows(quarter(place) ^ partner, size), :] = part[:size, :]
    add_late([part.at[size:, :] for part in parts], both.at[4 * size :, :])
    mixed_out[...] = results[0]
    grad_out[...] = results[1]


def step3_call(order, place, size, parts, results):
    rows, dim = parts[0].shape
    half = sds(results.shape[1:], BF16)
    return order.run(
        3.5,
        functools.partial(step3_kernel, size),
        (place, *parts, results),
        [sds((rows + 3 * size, dim), BF16), half, half],
        [SMEM] + [VMEM] * 5,
    )


def finish_attention_kernel(place, near, far, w_query, w_key, w_value, w_out, *norms):
    width = w_out.shape[0] // 2
    late = 4 * width
    rows = late + HEAD_DIM
    total = jnp.zeros((8, near.shape[1]), F32)
    for ref in (near, far):
        total = total + (ref[rows : rows + 8, :].astype(F32) + ref[rows + 8 :, :].astype(F32))
    for i, out in enumerate(norms):
        out[...] = total[i]
    here = (place[1] == 0).astype(F32)
    for core in range(2):

        @pl.when(place[0] == core)
        def _():
            low, high = (near, far) if core == 0 else (far, near)
            for i, out in enumerate((w_query, w_key, w_value)):
                piece = slice(i * width, (i + 1) * width)
                part = low[piece, :].astype(F32)
                if i < 2:
                    more = here * (low, high)[i][late:rows, :].astype(F32)
                    part = jnp.concatenate([part[:HEAD_DIM] + more, part[HEAD_DIM:]], axis=0)
                out[...] = jnp.concatenate([part, high[piece, :].astype(F32)], axis=0).T
            w_out[:width, :] = low[3 * width : late, :].astype(F32)
            w_out[width:, :] = high[3 * width : late, :].astype(F32)


def finish_attention_call(order, place, width, near, far):
    dim = near.shape[1]
    return order.run(
        4.5,
        finish_attention_kernel,
        (place, near, far),
        [sds((dim, 2 * width), F32)] * 3 + [sds((2 * width, dim), F32)] + [sds((dim,), F32)] * 4,
        [SMEM] + [VMEM] * 2,
    )


def finish_mlp_kernel(place, near, far, w_up, w_down):
    units = near.shape[1]
    for core in range(2):

        @pl.when(place[0] == core)
        def _():
            low, high = (near, far) if core == 0 else (far, near)
            w_up[:, :units] = low[0].astype(F32)
            w_up[:, units:] = high[0].astype(F32)
            w_down[:units, :] = low[1].astype(F32)
            w_down[units:, :] = high[1].astype(F32)


def finish_mlp_call(order, place, near, far):
    _, units, dim = near.shape
    return order.run(
        6.8,
        finish_mlp_kernel,
        (place, near, far),
        [sds((dim, 2 * units), F32), sds((2 * units, dim), F32)],
        [SMEM] + [VMEM] * 2,
    )


def make_body(devices, parts):
    axes = ("dp", "tensor")
    chips = devices // 2
    in_order = [1 << bit for bit in range(chips.bit_length() - 1)]
    turned = [in_order[1], in_order[0], *in_order[2:]]
    rounds = len(in_order)
    rounds_more = range(3, rounds)

    def pairs(move):
        found = []
        for device in range(devices):
            for part in range(parts):
                to_chip, to_core, to_part = move(device // 2, device % 2, part)
                source = device * parts + part
                found.append((source, (to_chip * 2 + to_core) * parts + to_part))
        return found

    def by_bit(bit):
        return pairs(
            lambda chip, core, part: (chip ^ (turned if core else in_order)[bit], core, part)
        )

    by_role = pairs(lambda chip, core, part: (chip, part, core))
    by_core = pairs(lambda chip, core, part: (chip, 1 - core, part))
    by_part = pairs(lambda chip, core, part: (chip, core, 1 - part))
    from_first_part = [pair for pair in by_part if pair[0] % parts == 0]
    by_chip = [by_bit(bit) for bit in range(rounds)]

    def by_quarter(partner):
        def across(chip, core, part):
            for bit in range(2):
                if partner >> (1 - bit) & 1:
                    chip ^= (turned if core else in_order)[bit]
            return chip, core, part

        return pairs(across)

    def move(value, how):
        return lax.ppermute(value, axes, how)

    def add_more(value):
        for bit in rounds_more:
            other = move(value, by_chip[bit])
            value = (value.astype(F32) + other.astype(F32)).astype(value.dtype)
        return value

    def exchange(values):
        return [values[0]] + [move(values[i], by_quarter(i)) for i in range(1, 4)]

    def body(
        tokens,
        segment_ids,
        pad_mask,
        norm1_gain,
        norm1_shift,
        w_query,
        w_key,
        w_value,
        w_out,
        norm2_gain,
        norm2_shift,
        w_up,
        w_down,
        cotangent,
    ):
        order = Order()
        device = lax.axis_index("dp")
        part = lax.axis_index("tensor")
        core = device % 2
        chip = device // 2
        bits = [
            jnp.where(core == 1, (chip & turned[i]) != 0, (chip & in_order[i]) != 0)
            for i in range(rounds)
        ]
        place = jnp.stack([core, part] + bits).astype(jnp.int32)
        gain1, shift1, gain2, shift2 = (
            vector[None, :] for vector in (norm1_gain, norm1_shift, norm2_gain, norm2_shift)
        )

        mine = move(tokens, by_role)
        ints = jnp.concatenate([segment_ids, pad_mask], axis=0)
        ints = jnp.where(core == part, ints, move(ints, by_core)).astype(F32)
        seg_pad = jnp.concatenate([ints, jnp.zeros((6, ints.shape[1]), F32)], axis=0)

        qkv_l, qkv_s, first = pack_first_call(order, place, w_query, w_key, w_value)
        first_moved = move(first, from_first_part)
        qkv_near = move(qkv_s, by_part)
        n1_own = norm1_call(order, mine, gain1, shift1)
        n1_other = move(n1_own, by_core)
        out_l, up_l, up_s, down_l, down_s, grad = pack_last_call(
            order, place, w_out, w_up, w_down, cotangent
        )
        out_r = move(out_l, by_part)
        up_near = move(up_s, by_part)
        grad_own = move(grad, by_role)
        down_near = move(down_s, by_part)
        n1, penalty, qk0, first = penalty_call(
            order, place, n1_own, n1_other, first, first_moved, seg_pad
        )
        (qkv_near,) = order.hold((qkv_near,), (penalty,))
        qkv_far = move(qkv_near, by_chip[0])
        qkvt_l, heads_l, lse_l = forward_call(order, n1, (qkv_l,), penalty)
        qkvt_r, heads_r, lse_r, qkv_r, own, send = forward_call(
            order,
            n1,
            (qkv_near, qkv_far),
            penalty,
            place,
            (heads_l, out_l, out_r),
            (up_near,),
        )
        (send,) = order.hold((send,), (down_near,))
        (up_near,) = order.hold((up_near,), (lse_r,))
        up_far = move(up_near, by_chip[0])
        (grad_own,) = order.hold((grad_own,), (lse_r,))
        grad_other = move(grad_own, by_core)
        (down_near,) = order.hold((down_near,), (lse_r,))
        down_far = move(down_near, by_chip[0])
        hidden, n2_own = norm2_call(order, mine, own, move(send, by_core), gain2, shift2)
        n2_other = move(n2_own, by_core)
        *before, keep, send = mlp_call(
            order, place, n2_other, n2_own, grad_other, grad_own, (up_l, down_l)
        )
        got = move(send, by_chip[0])
        weights = (up_near, up_far, down_near, down_far)
        mixed_send, mixed_own, back_send, back_own, *ff_r = mlp_call(
            order, place, n2_other, n2_own, grad_other, grad_own, weights, before
        )
        back_send, *ff_r = order.hold((back_send, *ff_r), (got,))
        ff_r = exchange(ff_r)
        grad_hidden, low_own, sums2 = norm2_back_call(
            order, hidden, back_own, move(back_send, by_core), grad_own, gain2
        )
        low_other = move(low_own, by_core)
        keep, send = half_sums_call(order, place, keep, got)
        got = move(send, by_chip[1])

        low = (low_own, low_other)
        grads_r, wo_r, logit_sum = backward_call(
            order, place, *low, out_r, heads_r, qkvt_r, lse_r, penalty
        )
        at_r = weights_first_call(order, place, n1, grads_r, wo_r)
        ff, ff_move = first_sums_call(order, (keep, got), ff_r)
        ff_got = move(ff_move, by_part)
        at_r = exchange(at_r)
        grads_l, wo_l, logit_sum = backward_call(
            order, place, *low, out_l, heads_l, qkvt_l, lse_l, penalty, logit_sum
        )
        logit_got = move(logit_sum, by_core)
        at_r, ff, *at = weights_second_call(
            order, place, n1, grads_l, wo_l, at_r, (ff, ff_got)
        )
        at_r = move(at_r, by_part)
        ff_got = move(ff, by_chip[2])
        at = exchange(at)
        own, send, late = norm1_grad_call(
            order,
            place,
            (logit_sum, logit_got),
            qk0,
            seg_pad,
            n1,
            grads_l,
            qkv_l,
            first,
            grads_r,
            qkv_r,
            gain1,
            shift1,
            sums2,
        )
        send, late = order.hold((send, late), (*at, at_r))
        received = move(send, by_core)
        late_got = move(late, by_part)
        ff = step0_call(order, (ff, ff_got))
        ff = exchange([add_more(ff)] * 4)
        both = step1_call(order, (late, late_got), (*at, at_r))
        size = at_r.shape[1]
        both_got = move(both, by_chip[2])
        results = results_call(
            order,
            mine,
            own,
            received,
            grad_hidden,
            gain1,
            hidden,
            mixed_own,
            move(mixed_send, by_core),
        )
        (results,) = order.hold((results,), (both_got,))
        results = move(results, by_role)
        both, ff = step2_call(order, place, size, both, both_got, ff)
        both = exchange([add_more(both)] * 4)
        ff_far = move(ff, by_core)
        up_grad, down_grad = finish_mlp_call(order, place, ff, ff_far)
        both, mixed, tokens_grad = step3_call(order, place, size, both, results)
        query_grad, key_grad, value_grad, out_grad, *norms = finish_attention_call(
            order, place, size, both, move(both, by_core)
        )
        return (
            mixed,
            tokens_grad,
            norms[0],
            norms[1],
            query_grad,
            key_grad,
            value_grad,
            out_grad,
            norms[2],
            norms[3],
            up_grad,
            down_grad,
        )

    return body


def solution(mesh):
    in_specs = (
        P(("dp", "tensor"), None),
        P("dp", None),
        P("dp", None),
        P(),
        P(),
        P(None, "tensor"),
        P(None, "tensor"),
        P(None, "tensor"),
        P("tensor", None),
        P(),
        P(),
        P(None, "tensor"),
        P("tensor", None),
        P(("dp", "tensor"), None),
    )
    out_specs = (
        P(("dp", "tensor"), None),
        P(("dp", "tensor"), None),
        P(),
        P(),
        P(None, "tensor"),
        P(None, "tensor"),
        P(None, "tensor"),
        P("tensor", None),
        P(),
        P(),
        P(None, "tensor"),
        P("tensor", None),
    )
    body = make_body(mesh.shape["dp"], mesh.shape["tensor"])
    return jax.shard_map(body, mesh=mesh, in_specs=in_specs, out_specs=out_specs, check_vma=False)
```

```python
import functools

import jax
import jax.numpy as jnp
from jax import lax
from jax.experimental import pallas as pl
from jax.experimental.pallas import tpu as pltpu
from jax.sharding import PartitionSpec as P

HEAD_DIM = 64
EPS = 1e-05
FAR = 1e30
FORWARD_BLOCK = 512
BF16 = jnp.bfloat16
F32 = jnp.float32
TN = (((0,), (0,)), ((), ()))
NT = (((1,), (1,)), ((), ()))
NN = (((1,), (0,)), ((), ()))
TT = (((0,), (1,)), ((), ()))
ERF_C = (
    1.5897294934128858e-07,
    -5.985900079472216e-06,
    8.971378204617447e-05,
    -0.0006257225011275588,
    -0.0001843806018428344,
    0.10276548023357895,
    1.1283797055884355,
)
ERF_X = tuple(c * 0.5 ** (6 - i) * 0.7071067811865476 for i, c in enumerate(ERF_C))


def dot(left, right, dims):
    return lax.dot_general(left, right, dims, preferred_element_type=F32)


def sds(shape, dtype):
    return jax.ShapeDtypeStruct(shape, dtype)


SMEM = pl.BlockSpec(memory_space=pltpu.SMEM)
VMEM = pl.BlockSpec(memory_space=pltpu.VMEM)
ANY = pl.BlockSpec(memory_space=pl.ANY)


WEIGHT = 20.0


class Order:
    def __init__(self):
        self.last = None

    def run(self, us, kernel, operands, out_shape, in_specs=None, after=(), **rest):
        after = tuple(after) + (() if self.last is None else (self.last,))
        count, extra = len(operands), len(after)
        in_specs = list(in_specs or [VMEM] * count) + [ANY] * extra

        def body(*refs):
            kernel(*refs[:count], *refs[count + extra :])

        out = pl.pallas_call(
            body,
            out_shape=out_shape,
            in_specs=in_specs,
            compiler_params=pltpu.CompilerParams(vmem_limit_bytes=58 << 20),
            cost_estimate=pl.CostEstimate(
                flops=int(us * WEIGHT * 1.15e9), bytes_accessed=0, transcendentals=0
            ),
            **rest,
        )(*operands, *after)
        self.last = out[-1] if isinstance(out, (list, tuple)) else out
        return out

    def hold(self, values, after, us=0):
        count = len(values)

        def kernel(*refs):
            pass

        held = pl.pallas_call(
            kernel,
            out_shape=[sds(value.shape, value.dtype) for value in values],
            in_specs=[ANY] * (count + len(after)),
            out_specs=[ANY] * count,
            input_output_aliases={i: i for i in range(count)},
            compiler_params=pltpu.CompilerParams(has_side_effects=True),
            cost_estimate=pl.CostEstimate(
                flops=int(us * WEIGHT * 1.15e9), bytes_accessed=0, transcendentals=0
            ),
        )(*values, *after)
        for value, same in zip(values, held):
            if self.last is value:
                self.last = same
        return held


def whole(shape):
    return pl.BlockSpec(shape, lambda *_: (0,) * len(shape))


def low_sum(*terms):
    total = terms[0].astype(F32)
    for term in terms[1:]:
        total = total + term.astype(F32)
    return total.astype(BF16)


def part_rows(index, size):
    return pl.ds(pl.multiple_of(index * size, size), size)


def split(place, bit, source, keep, send):
    half = keep.shape[1]
    keep[...] = source[:, part_rows(place[2 + bit], half), :]
    send[...] = source[:, part_rows(1 - place[2 + bit], half), :]


def quarter(place):
    return 2 * place[2] + place[3]


def scatter(place, source, outs):
    for partner, out in enumerate(outs):
        out[...] = source[:, part_rows(quarter(place) ^ partner, out.shape[1]), :]


def gather(place, pieces, out):
    for partner, piece in enumerate(pieces):
        out[:, part_rows(quarter(place) ^ partner, piece.shape[1]), :] = piece[...]


def normalize(values):
    center = values - jnp.mean(values, axis=-1, keepdims=True)
    inverse = lax.rsqrt(jnp.mean(center * center, axis=-1, keepdims=True) + EPS)
    return center * inverse, inverse


def norm_back(grad_normed, scaled, inverse, gain):
    grad_scaled = grad_normed * gain
    return inverse * (
        grad_scaled
        - jnp.mean(grad_scaled, axis=-1, keepdims=True)
        - scaled * jnp.mean(grad_scaled * scaled, axis=-1, keepdims=True)
    )


def gelu_pair(x):
    square = x * x
    near = jnp.minimum(square, 64.0)
    poly = ERF_X[0]
    for coefficient in ERF_X[1:]:
        poly = poly * near + coefficient
    phi = 0.5 * jnp.tanh(x * poly) + 0.5
    bell = jnp.exp(square * -0.5)
    return x * phi, phi + x * (bell * 0.3989422804014327)


def pack_first_kernel(place, w_query, w_key, w_value, qkv, qkv_send, first):
    width = qkv.shape[1] // 3
    half = qkv_send.shape[0]
    first[:, :HEAD_DIM] = w_query[:, :HEAD_DIM]
    first[:, HEAD_DIM:] = w_key[:, :HEAD_DIM]
    for core in range(2):

        @pl.when(place[0] == core)
        def _():
            narrow = slice(core * width, (core + 1) * width)
            for i, weight in enumerate((w_query, w_key, w_value)):
                qkv[:, i * width : (i + 1) * width] = weight[:, narrow]

    qkv_send[...] = qkv[pl.ds(pl.multiple_of(place[2] * half, half), half), :]


def pack_first_call(order, place, w_query, w_key, w_value):
    dim, width = w_query.shape[0], w_query.shape[1] // 2
    return order.run(
        4,
        pack_first_kernel,
        (place, w_query, w_key, w_value),
        [
            sds((dim, 3 * width), BF16),
            sds((dim // 2, 3 * width), BF16),
            sds((dim, 2 * HEAD_DIM), BF16),
        ],
        [SMEM] + [VMEM] * 3,
    )


def pack_last_kernel(place, w_out, w_up, w_down, grad, out, up, up_send, down, down_send, grad_out):
    width = out.shape[0]
    units = down.shape[0]
    half = units // 2
    grad_out[...] = grad[...]
    for core in range(2):

        @pl.when(place[0] == core)
        def _():
            wide = slice(core * units, (core + 1) * units)
            out[...] = w_out[core * width : (core + 1) * width, :]
            up[...] = w_up[:, wide]
            down[...] = w_down[wide, :]

    rows = pl.ds(pl.multiple_of(place[2] * half, half), half)
    up_send[...] = up[rows, :]
    down_send[...] = down[rows, :]


def pack_last_call(order, place, w_out, w_up, w_down, grad):
    width, dim = w_out.shape[0] // 2, w_out.shape[1]
    units = w_up.shape[1] // 2
    return order.run(
        5,
        pack_last_kernel,
        (place, w_out, w_up, w_down, grad),
        [
            sds((width, dim), BF16),
            sds((dim, units), BF16),
            sds((dim // 2, units), BF16),
            sds((units, dim), BF16),
            sds((units // 2, dim), BF16),
            sds(grad.shape, BF16),
        ],
        [SMEM] + [VMEM] * 4,
    )


def norm1_kernel(tokens, gain, shift, out):
    scaled, _ = normalize(tokens[...].astype(F32))
    out[...] = (scaled * gain[...] + shift[...]).astype(BF16)


def rows_spec(block, dim):
    return pl.BlockSpec((block, dim), lambda i: (i, 0))


def norm1_call(order, tokens, gain, shift):
    return order.run(2.5, norm1_kernel, (tokens, gain, shift), sds(tokens.shape, BF16))


def masks(seg_pad, cols, low, high):
    width = high - low
    seg_row = seg_pad[0:1, low:high]
    pad_row = seg_pad[1:2, low:high]
    row_key = jnp.where(pad_row > 0, seg_row, -2.0)
    col_seg = cols[:high, 0:1]
    col_pad = cols[:high, 1:2]
    col_key = jnp.where(col_pad > 0, col_seg, -1.0)
    key_at = lax.broadcasted_iota(jnp.int32, (high, width), 0)
    query_at = lax.broadcasted_iota(jnp.int32, (high, width), 1) + low
    allowed = ((col_key == seg_row) & (key_at <= query_at)) | (key_at == query_at)
    picked = (col_key == row_key) & (key_at < query_at)
    return allowed, picked


def penalty_kernel(
    block, place, n1_own, n1_other, first, first_moved, seg_pad, n1_out, penalty, qk0, first_out
):
    seq = n1_out.shape[0]
    half = seq // 2
    core = place[0]
    n1_out[pl.ds(pl.multiple_of(core * half, half), half), :] = n1_own[...]
    n1_out[pl.ds(pl.multiple_of((1 - core) * half, half), half), :] = n1_other[...]

    @pl.when(place[1] == 0)
    def _():
        first_out[...] = first[...]

    @pl.when(place[1] != 0)
    def _():
        first_out[...] = first_moved[...]

    qk = dot(first_out[...], n1_out[...], TT)
    q0 = (qk[:HEAD_DIM].astype(BF16) * 0.125).astype(BF16)
    k0 = qk[HEAD_DIM:].astype(BF16)
    qk0[:HEAD_DIM, :] = q0
    qk0[HEAD_DIM:, :] = k0
    seg_value = seg_pad[...]
    cols = seg_value.T
    earlier = lax.broadcasted_iota(jnp.int32, (block, block + 128), 0)
    later = lax.broadcasted_iota(jnp.int32, (block, block + 128), 1)
    sums = ((earlier < later) | (later >= block)).astype(F32).astype(BF16)
    carry = jnp.zeros((seq, 128), F32)
    for low in range(0, seq, block):
        high = low + block
        allowed, picked = masks(seg_value, cols, low, high)
        score = dot(k0[:, :high], q0[:, low:high], TN)
        small = jnp.exp(-jnp.abs(score))
        log1p = jnp.where(small < 1e-3, small - 0.5 * small * small, jnp.log(1.0 + small))
        select = jnp.where(picked, jnp.maximum(score, 0.0) + log1p, 0.0).astype(BF16)
        total = dot(select, sums, NN)
        before = jnp.concatenate([carry[:high]] * (block // 128), axis=1)
        penalty[:high, low:high] = jnp.where(allowed, total[:, :block] + before, FAR)
        if high % FORWARD_BLOCK:
            edge = high + FORWARD_BLOCK - high % FORWARD_BLOCK
            penalty[high:edge, low:high] = jnp.full((edge - high, block), FAR, F32)
        carry = jnp.concatenate([carry[:high] + total[:, block:], carry[high:]], axis=0)


def penalty_call(order, place, n1_own, n1_other, first, first_moved, seg_pad, after=()):
    half, dim = n1_own.shape
    seq = 2 * half
    return order.run(
        6.5,
        functools.partial(penalty_kernel, 256),
        (place, n1_own, n1_other, first, first_moved, seg_pad),
        [
            sds((seq, dim), BF16),
            sds((seq, seq), F32),
            sds((2 * HEAD_DIM, seq), BF16),
            sds(first.shape, BF16),
        ],
        [SMEM] + [VMEM] * 5,
        after,
    )


def forward_kernel(block, last, *refs):
    if last:
        place, n1, near, far, penalty, out_l, w_l, w_r, *refs = refs
        qkv, out, lse, weights, own, send, out_r = refs
    else:
        n1, weights, penalty, qkv, out, lse = refs
    head = pl.program_id(0)
    third = qkv.shape[0] // 3
    seq = qkv.shape[1]

    @pl.when(head == 0)
    def _():
        if last:
            join(place[2], weights, near, far)
        product = dot(weights[...], n1[...], TT).astype(BF16)
        qkv[:third, :] = (product[:third] * 0.125).astype(BF16)
        qkv[third:, :] = product[third:]

    at = pl.multiple_of(head * HEAD_DIM, HEAD_DIM)
    query = qkv[pl.ds(at, HEAD_DIM), :]
    key = qkv[pl.ds(third + at, HEAD_DIM), :]
    value = qkv[pl.ds(2 * third + at, HEAD_DIM), :]
    value = jnp.concatenate([value, jnp.ones((16, seq), BF16)], axis=0)
    for low in range(0, seq, block):
        high = low + block
        logits = dot(key[:, :high], query[:, low:high], TN) - penalty[:high, low:high]
        largest = jnp.max(logits, axis=0, keepdims=True)
        weight = jnp.exp(logits - largest).astype(BF16)
        result = dot(value[:, :high], weight, NN)
        total = result[HEAD_DIM : HEAD_DIM + 1, :]
        out[:, low:high] = (result[:HEAD_DIM] / total).astype(BF16)
        lse[:, low:high] = largest + jnp.log(total)
    if last:
        out_r[pl.ds(at, HEAD_DIM), :] = out[...]

        @pl.when(head == pl.num_programs(0) - 1)
        def _():
            project(place, out_l, out_r, w_l, w_r, own, send)


def join(bit, out, near, far):
    half = near.shape[0]
    out[pl.ds(pl.multiple_of(bit * half, half), half), :] = near[...]
    out[pl.ds(pl.multiple_of((1 - bit) * half, half), half), :] = far[...]


def forward_call(order, n1, weights, penalty, place=None, others=(), after=()):
    seq, dim = n1.shape
    last = place is not None
    width = weights[0].shape[1]
    heads = width // (3 * HEAD_DIM)
    operands = ((place,) if last else ()) + (n1,) + tuple(weights) + (penalty,) + tuple(others)
    in_specs = [SMEM] if last else []
    in_specs += [whole(x.shape) for x in operands if x is not place]
    out_specs = [
        whole((width, seq)),
        pl.BlockSpec((HEAD_DIM, seq), lambda h: (h, 0)),
        pl.BlockSpec((None, 1, seq), lambda h: (h, 0, 0)),
    ]
    out_shape = [
        sds((width, seq), BF16),
        sds((heads * HEAD_DIM, seq), BF16),
        sds((heads, 1, seq), F32),
    ]
    scratch = []
    if last:
        out_specs += [whole((dim, width)), whole((seq // 2, dim)), whole((seq // 2, dim))]
        out_shape += [sds((dim, width), BF16), sds((seq // 2, dim), F32), sds((seq // 2, dim), BF16)]
        scratch.append(pltpu.VMEM((heads * HEAD_DIM, seq), BF16))
    return order.run(
        10,
        functools.partial(forward_kernel, FORWARD_BLOCK, last),
        operands,
        out_shape,
        in_specs,
        after,
        grid=(heads,),
        out_specs=out_specs,
        scratch_shapes=scratch,
    )


def project(place, out_l, out_r, w_l, w_r, own, send):
    half = own.shape[0]
    core = place[0]
    mixed = jnp.concatenate([w_l[...], w_r[...]], axis=0)

    def part(which):
        heads = jnp.concatenate([out_l[:, part_rows(which, half)], out_r[:, part_rows(which, half)]], axis=0)
        return dot(heads, mixed, TN)

    send[...] = part(1 - core).astype(BF16)
    own[...] = part(core)


def norm2_kernel(tokens, own, received, gain, shift, hidden, out):
    total = tokens[...].astype(F32) + (own[...] + received[...].astype(F32))
    hidden[...] = total
    scaled, _ = normalize(total)
    out[...] = (scaled * gain[...] + shift[...]).astype(BF16)


def norm2_call(order, tokens, own, received, gain, shift, after=()):
    size, dim = tokens.shape
    rows = rows_spec(size // 2, dim)
    vector = whole((1, dim))
    return order.run(
        4,
        norm2_kernel,
        (tokens, own, received, gain, shift),
        [sds(tokens.shape, F32), sds(tokens.shape, BF16)],
        [rows] * 3 + [vector] * 2,
        after,
        grid=(2,),
        out_specs=[rows, rows],
    )


def mlp_kernel(first, *refs):
    place, n2_other, n2_own, g_other, g_own, *refs = refs
    if first:
        w_up, w_down, *refs = refs
        before = (None,) * 4
    else:
        up_near, up_far, down_near, down_far, *refs = refs
        before, refs = refs[:4], refs[4:]
    outs, refs = refs[:4], refs[4:]
    count = 2 if first else 4
    parts, refs = refs[:count], refs[count:]
    if not first:
        w_up, w_down, *refs = refs
        join(place[2], w_up, up_near, up_far)
        join(place[2], w_down, down_near, down_far)
    actives, grad_ups, w_grads = refs
    size = n2_own.shape[0]

    def put(out, rows, value, more):
        out[rows, :] = (value if more is None else value + more[rows, :].astype(F32)).astype(out.dtype)

    block = min(256, size)
    for at, n2, g in ((0, n2_other, g_other), (1, n2_own, g_own)):

        def work(step, _):
            rows = part_rows(step, block)
            here = part_rows(step + at * (size // block), block)
            active, slope = gelu_pair(dot(n2[rows, :], w_up[...], NN))
            active = active.astype(BF16)
            grad_up = (dot(g[rows, :], w_down[...], NT) * slope).astype(BF16)
            actives[here, :] = active
            grad_ups[here, :] = grad_up
            put(outs[2 + at], rows, dot(grad_up, w_up[...], NT), before[2 + at])
            put(outs[at], rows, dot(active, w_down[...], NN), before[at])
            return 0

        lax.fori_loop(0, size // block, work, 0)
    w_grads[0] = (
        dot(n2_other[...], grad_ups[:size, :], TN) + dot(n2_own[...], grad_ups[size:, :], TN)
    ).astype(BF16)
    w_grads[1] = (
        dot(actives[:size, :], g_other[...], TN) + dot(actives[size:, :], g_own[...], TN)
    ).astype(BF16)
    if first:
        split(place, 0, w_grads, *parts)
    else:
        scatter(place, w_grads, parts)


def mlp_call(order, place, n2_other, n2_own, g_other, g_own, weights, before=(), after=()):
    size, dim = n2_own.shape
    first = not before
    units = weights[0].shape[1]
    count = 2 if first else 4
    sent = sds((size, dim), BF16)
    kept = sent
    rows = pltpu.VMEM((2 * size, units), BF16)
    scratch = [rows, rows, pltpu.VMEM((2, units, dim), BF16)]
    if not first:
        scratch = [pltpu.VMEM((dim, units), BF16), pltpu.VMEM((units, dim), BF16)] + scratch
    operands = (n2_other, n2_own, g_other, g_own, *weights, *before)
    return order.run(
        14.6,
        functools.partial(mlp_kernel, first),
        (place, *operands),
        [sent, kept, sent, kept] + [sds((2, units // count, dim), BF16)] * count,
        [SMEM] + [VMEM] * len(operands),
        after,
        scratch_shapes=scratch,
    )


def norm2_back_kernel(hidden, own, received, grad, gain, grad_hidden, low, sums):
    normed_grad = own[...].astype(F32) + received[...].astype(F32)
    scaled, inverse = normalize(hidden[...])
    total = grad[...].astype(F32) + norm_back(normed_grad, scaled, inverse, gain[...])
    grad_hidden[...] = total
    low[...] = total.astype(BF16)
    add_sums(sums, normed_grad, scaled)


def add_sums(sums, normed_grad, scaled):
    @pl.when(pl.program_id(0) == 0)
    def _():
        sums[...] = jnp.zeros(sums.shape, F32)

    sums[0:1, :] += jnp.sum(normed_grad * scaled, axis=0, keepdims=True)
    sums[1:2, :] += jnp.sum(normed_grad, axis=0, keepdims=True)


def norm2_back_call(order, hidden, own, received, grad, gain, after=()):
    size, dim = hidden.shape
    rows = rows_spec(size // 2, dim)
    return order.run(
        5,
        norm2_back_kernel,
        (hidden, own, received, grad, gain),
        [sds(hidden.shape, F32), sds(hidden.shape, BF16), sds((8, dim), F32)],
        [rows] * 4 + [whole((1, dim))],
        after,
        grid=(2,),
        out_specs=[rows, rows, whole((8, dim))],
    )


def half_sums_kernel(place, near, far, keep, send):
    half = keep.shape[1]
    for out, which in ((keep, place[3]), (send, 1 - place[3])):
        rows = part_rows(which, half)
        out[...] = low_sum(near[:, rows, :], far[:, rows, :])


def half_sums_call(order, place, near, far):
    groups, rows, dim = near.shape
    return order.run(
        3,
        half_sums_kernel,
        (place, near, far),
        [sds((groups, rows // 2, dim), BF16)] * 2,
        [SMEM] + [VMEM] * 2,
    )


def backward_kernel(first, block, *refs):
    place, g_own, g_other, w_out, heads_out, qkv, lse, penalty, *refs = refs
    if not first:
        before, *refs = refs
    grads, w_grad, logit_sum, grad_full, key_sum, value_sum, *refs = refs
    third = qkv.shape[0] // 3
    seq = qkv.shape[1]
    half = seq // 2
    total = logit_sum if first else refs[0]
    core = place[0]
    grad_full[part_rows(core, half), :] = g_own[...]
    grad_full[part_rows(1 - core, half), :] = g_other[...]
    whole_grad = grad_full[...]
    grad_heads = dot(w_out[...], whole_grad, NT).astype(BF16)
    w_grad[...] = dot(heads_out[...], whole_grad, NN).astype(BF16)
    heads = third // HEAD_DIM
    for head in range(heads):
        rows = slice(head * HEAD_DIM, (head + 1) * HEAD_DIM)
        query = qkv[rows, :]
        key = qkv[third + head * HEAD_DIM : third + (head + 1) * HEAD_DIM, :]
        value = qkv[2 * third + head * HEAD_DIM : 2 * third + (head + 1) * HEAD_DIM, :]
        grad = grad_heads[rows]
        for low in range(0, seq, block):
            high = low + block
            cols = slice(low, high)
            score = dot(key[:, :high], query[:, cols], TN)
            probs = jnp.exp(score - penalty[:high, cols] - lse[head, :, cols])
            grad_probs = dot(value[:, :high], grad[:, cols], TN)
            row_dot = jnp.sum(probs * grad_probs, axis=0, keepdims=True)
            grad_logits = probs * (grad_probs - row_dot)
            if head:
                sum_now = total[:high, cols] + grad_logits
            elif first:
                sum_now = grad_logits
            else:
                sum_now = before[:high, cols] + grad_logits
            if first or head < heads - 1:
                total[:high, cols] = sum_now
            else:
                logit_sum[:high, cols] = sum_now.astype(BF16)
            low_logits = grad_logits.astype(BF16)
            low_probs = probs.astype(BF16)
            grads[rows, cols] = (dot(key[:, :high], low_logits, NN) * 0.125).astype(BF16)
            value_new = dot(grad[:, cols], low_probs, NT)
            key_new = dot(query[:, cols], low_logits, NT)
            if low:
                key_sum[head, :, :low] += key_new[:, :low]
                value_sum[head, :, :low] += value_new[:, :low]
            key_sum[head, :, cols] = key_new[:, low:]
            value_sum[head, :, cols] = value_new[:, low:]
        at = third + head * HEAD_DIM
        grads[at : at + HEAD_DIM, :] = key_sum[head].astype(BF16)
        at = at + third
        grads[at : at + HEAD_DIM, :] = value_sum[head].astype(BF16)


def backward_call(order, place, g_own, g_other, w_out, heads_out, qkv, lse, penalty, before=None):
    width, seq = qkv.shape
    heads = width // (3 * HEAD_DIM)
    first = before is None
    operands = (g_own, g_other, w_out, heads_out, qkv, lse, penalty)
    operands += () if first else (before,)
    sums = pltpu.VMEM((heads, HEAD_DIM, seq), F32)
    scratch = [pltpu.VMEM((seq, g_own.shape[1]), BF16), sums, sums]
    scratch += [] if first else [pltpu.VMEM((seq, seq), F32)]
    return order.run(
        16,
        functools.partial(backward_kernel, first, 256),
        (place, *operands),
        [
            sds((width, seq), BF16),
            sds(w_out.shape, BF16),
            sds((seq, seq), F32 if first else BF16),
        ],
        [SMEM] + [VMEM] * len(operands),
        scratch_shapes=scratch,
    )


def halves(value):
    high = value.astype(BF16)
    return high, (value - high.astype(F32)).astype(BF16)


def select_back(block, core, own, received, qk0, seg_pad, n1, out, w_grad, total_grad):
    seq = own.shape[0]
    q0 = qk0[:HEAD_DIM, :]
    k0 = qk0[HEAD_DIM:, :]
    seg_value = seg_pad[...]
    cols = seg_value.T
    later = lax.broadcasted_iota(jnp.int32, (block, block + 128), 0)
    earlier = lax.broadcasted_iota(jnp.int32, (block, block + 128), 1)
    sums = ((later > earlier) | (earlier >= block)).astype(F32).astype(BF16)
    carry = jnp.zeros((seq, 128), F32)
    total_grad[...] = jnp.zeros(total_grad.shape, F32)
    for low in range(seq - block, -1, -block):
        high = low + block
        logit_sum = own[:high, low:high].astype(F32) + received[:high, low:high].astype(F32)
        top, bottom = halves(logit_sum)
        total = dot(top, sums, NN) + dot(bottom, sums, NN)
        after = jnp.concatenate([carry[:high]] * (block // 128), axis=1)
        select_grad = -(total[:, :block] + after)
        carry = carry[:high] + total[:, block:]
        _, picked = masks(seg_value, cols, low, high)
        score = dot(k0[:, :high], q0[:, low:high], TN)
        through = jnp.where(picked, select_grad / (1.0 + jnp.exp(-score)), 0.0)
        top, bottom = halves(through)

        @pl.when(core == 0)
        def _():
            total_grad[:, low:high] = 0.125 * (
                dot(k0[:, :high], top, NN) + dot(k0[:, :high], bottom, NN)
            )

        @pl.when(core == 1)
        def _():
            total_grad[:, :high] += dot(q0[:, low:high], top, NT) + dot(
                q0[:, low:high], bottom, NT
            )

    out[...] = total_grad[...].astype(BF16)
    w_grad[...] = dot(out[...], n1[...], NN).astype(BF16)


def weights_first_kernel(place, n1, grads, w_out, *refs):
    parts, total = refs[:4], refs[4]
    width = grads.shape[0]
    total[0, :width, :] = dot(grads[...], n1[...], NN).astype(BF16)
    total[0, width:, :] = w_out[...]
    scatter(place, total, parts)


def weights_first_call(order, place, n1, grads, w_out):
    dim = n1.shape[1]
    rows = grads.shape[0] + w_out.shape[0]
    return order.run(
        4,
        weights_first_kernel,
        (place, n1, grads, w_out),
        [sds((1, rows // 4, dim), BF16)] * 4,
        [SMEM] + [VMEM] * 3,
        scratch_shapes=[pltpu.VMEM((1, rows, dim), BF16)],
    )


def weights_second_kernel(place, n1, grads, w_out, *refs):
    parts_r, ff_terms, refs = refs[:4], refs[4:6], refs[6:]
    move_r, ff, *refs = refs
    parts, total = refs[:4], refs[4]
    width = grads.shape[0]
    move_r[...] = low_sum(*(part[...] for part in parts_r))
    ff[...] = low_sum(*(term[...] for term in ff_terms))
    total[0, :width, :] = dot(grads[...], n1[...], NN).astype(BF16)
    total[0, width:, :] = w_out[...]
    scatter(place, total, parts)


def weights_second_call(order, place, n1, grads, w_out, parts_r, ff_terms):
    dim = n1.shape[1]
    rows = grads.shape[0] + w_out.shape[0]
    part = sds((1, rows // 4, dim), BF16)
    return order.run(
        6,
        weights_second_kernel,
        (place, n1, grads, w_out, *parts_r, *ff_terms),
        [part, sds(ff_terms[0].shape, BF16)] + [part] * 4,
        [SMEM] + [VMEM] * 9,
        scratch_shapes=[pltpu.VMEM((1, rows, dim), BF16)],
    )


def norm1_grad_kernel(block, place, logit_own, logit_got, qk0, seg_pad, n1, grads, weights, first, *refs):
    grads_r, weights_r, gain, shift, sums2, own, send, late, extra, extra_w, total_grad = refs
    select_back(
        block, place[0], logit_own, logit_got, qk0, seg_pad, n1, extra, extra_w, total_grad
    )
    half = own.shape[0]
    mine = jnp.where(place[0] == 0, first[:, :HEAD_DIM], first[:, HEAD_DIM:])
    total = dot(grads[...], weights[...], TT) + dot(grads_r[...], weights_r[...], TT)
    total = total + dot(extra[...], mine, TT)
    for core in range(2):

        @pl.when(place[0] == core)
        def _():
            own[...] = total[core * half : (core + 1) * half]
            send[...] = total[(1 - core) * half : (2 - core) * half].astype(BF16)

    scaled = (n1[...].astype(F32) - shift[...]) * (1.0 / gain[...])
    gain_sum = jnp.sum(total * scaled, axis=0, keepdims=True)
    shift_sum = jnp.sum(total, axis=0, keepdims=True)
    norms = jnp.concatenate([gain_sum, shift_sum, sums2[0:2, :], sums2[4:8, :]], axis=0)
    rows = extra_w.shape[0]
    late[:rows, :] = extra_w[...]
    high, low = halves(norms)
    late[rows : rows + 8, :] = high
    late[rows + 8 :, :] = low


def norm1_grad_call(order, place, logits, qk0, seg_pad, n1, grads, weights, first, *rest):
    seq, dim = n1.shape
    rows = HEAD_DIM
    return order.run(
        14,
        functools.partial(norm1_grad_kernel, 256),
        (place, *logits, qk0, seg_pad, n1, grads, weights, first, *rest),
        [
            sds((seq // 2, dim), F32),
            sds((seq // 2, dim), BF16),
            sds((rows + 16, dim), BF16),
        ],
        [SMEM] + [VMEM] * 13,
        scratch_shapes=[
            pltpu.VMEM((rows, seq), BF16),
            pltpu.VMEM((rows, dim), BF16),
            pltpu.VMEM((rows, seq), F32),
        ],
    )


def results_kernel(tokens, own, received, grad_hidden, gain, hidden, mixed_own, mixed_received, out):
    mixed = hidden[...] + (mixed_own[...].astype(F32) + mixed_received[...].astype(F32))
    out[0] = mixed.astype(BF16)
    normed_grad = own[...] + received[...].astype(F32)
    scaled, inverse = normalize(tokens[...].astype(F32))
    total = grad_hidden[...] + norm_back(normed_grad, scaled, inverse, gain[...])
    out[1] = total.astype(BF16)


def results_call(order, tokens, own, received, grad_hidden, gain, hidden, mixed_own, mixed_received):
    size, dim = tokens.shape
    rows = rows_spec(size // 2, dim)
    return order.run(
        5,
        results_kernel,
        (tokens, own, received, grad_hidden, gain, hidden, mixed_own, mixed_received),
        sds((2, size, dim), BF16),
        [rows] * 4 + [whole((1, dim))] + [rows] * 3,
        grid=(2,),
        out_specs=pl.BlockSpec((2, size // 2, dim), lambda i: (0, i, 0)),
    )


def add_late(terms, out):
    def pairs(values):
        while len(values) > 1:
            values = [values[i] + values[i + 1] for i in range(0, len(values), 2)]
        return values[0]

    rows = out.shape[0] - 16
    out[:rows, :] = pairs([term[:rows, :].astype(F32) for term in terms]).astype(BF16)
    norms = pairs(
        [term[rows : rows + 8, :].astype(F32) + term[rows + 8 :, :].astype(F32) for term in terms]
    )
    high, low = halves(norms)
    out[rows : rows + 8, :] = high
    out[rows + 8 :, :] = low


def first_sums_kernel(*refs):
    near, far, *refs = refs
    *parts, ff, ff_move = refs
    ff[...] = low_sum(near[...], far[...])
    ff_move[...] = low_sum(*(part[...] for part in parts))


def first_sums_call(order, terms, parts):
    shape = sds(parts[0].shape, BF16)
    return order.run(3, first_sums_kernel, (*terms, *parts), [shape, shape])


def step0_kernel(own, got, out):
    out[...] = low_sum(own[...], got[...])


def step0_call(order, terms):
    return order.run(2, step0_kernel, terms, sds(terms[0].shape, BF16))


def step1_kernel(late_own, late_got, *refs):
    *at_terms, both = refs
    size = at_terms[0].shape[1]
    both[:size, :] = low_sum(*(term[0] for term in at_terms))
    add_late((late_own, late_got), both.at[size:, :])


def step1_call(order, late_terms, at_terms):
    _, size, dim = at_terms[0].shape
    rows = size + late_terms[0].shape[0]
    return order.run(3, step1_kernel, (*late_terms, *at_terms), sds((rows, dim), BF16))


def step2_kernel(size, place, own, got, *refs):
    *parts, both, ff = refs
    both[:size, :] = low_sum(own[:size, :], got[:size, :])
    add_late((own.at[size:, :], got.at[size:, :]), both.at[size:, :])
    gather(place, parts, ff)


def step2_call(order, place, size, own, got, parts, after=()):
    groups, rows, dim = parts[0].shape
    return order.run(
        4.5,
        functools.partial(step2_kernel, size),
        (place, own, got, *parts),
        [sds(own.shape, BF16), sds((groups, 4 * rows, dim), BF16)],
        [SMEM] + [VMEM] * 6,
        after,
    )


def step3_kernel(size, place, *refs):
    parts, refs = refs[:4], refs[4:]
    (both,) = refs
    for partner, part in enumerate(parts):
        both[part_rows(quarter(place) ^ partner, size), :] = part[:size, :]
    add_late([part.at[size:, :] for part in parts], both.at[4 * size :, :])


def step3_call(order, place, size, parts):
    rows, dim = parts[0].shape
    return order.run(
        3.5,
        functools.partial(step3_kernel, size),
        (place, *parts),
        sds((rows + 3 * size, dim), BF16),
        [SMEM] + [VMEM] * 4,
    )


def copy_kernel(place, results, moved, mixed, tokens_grad):
    stays = place[0] == place[1]
    for source, wanted in ((results, stays), (moved, jnp.logical_not(stays))):

        @pl.when(wanted)
        def _():
            mixed[...] = source[0]
            tokens_grad[...] = source[1]


def copy_call(order, place, results, moved):
    return order.run(
        2,
        copy_kernel,
        (place, results, moved),
        [sds(results.shape[1:], BF16)] * 2,
        [SMEM] + [VMEM] * 2,
    )


def finish_attention_kernel(place, near, far, *outs):
    w_query, w_key, w_value, w_out, *norms = outs
    width = w_out.shape[0] // 2
    late = 4 * width
    rows = late + HEAD_DIM
    total = jnp.zeros((8, near.shape[1]), F32)
    for ref in (near, far):
        total = total + (ref[rows : rows + 8, :].astype(F32) + ref[rows + 8 :, :].astype(F32))
    for i, out in enumerate(norms):
        out[...] = total[i]
    here = (place[1] == 0).astype(F32)
    for core in range(2):

        @pl.when(place[0] == core)
        def _():
            low, high = (near, far) if core == 0 else (far, near)
            for i, out in enumerate((w_query, w_key, w_value)):
                piece = slice(i * width, (i + 1) * width)
                part = low[piece, :].astype(F32)
                if i < 2:
                    more = here * (low, high)[i][late:rows, :].astype(F32)
                    part = jnp.concatenate([part[:HEAD_DIM] + more, part[HEAD_DIM:]], axis=0)
                out[...] = jnp.concatenate([part, high[piece, :].astype(F32)], axis=0).T
            w_out[:width, :] = low[3 * width : late, :].astype(F32)
            w_out[width:, :] = high[3 * width : late, :].astype(F32)


def finish_attention_call(order, place, width, near, far):
    dim = near.shape[1]
    return order.run(
        4.5,
        finish_attention_kernel,
        (place, near, far),
        [sds((dim, 2 * width), F32)] * 3 + [sds((2 * width, dim), F32)] + [sds((dim,), F32)] * 4,
        [SMEM] + [VMEM] * 2,
    )


def finish_mlp_kernel(place, near, far, w_up, w_down):
    units = near.shape[1]
    for core in range(2):

        @pl.when(place[0] == core)
        def _():
            low, high = (near, far) if core == 0 else (far, near)
            w_up[:, :units] = low[0].astype(F32)
            w_up[:, units:] = high[0].astype(F32)
            w_down[:units, :] = low[1].astype(F32)
            w_down[units:, :] = high[1].astype(F32)


def finish_mlp_call(order, place, near, far):
    _, units, dim = near.shape
    return order.run(
        6.8,
        finish_mlp_kernel,
        (place, near, far),
        [sds((dim, 2 * units), F32), sds((2 * units, dim), F32)],
        [SMEM] + [VMEM] * 2,
    )


def make_body(devices, parts):
    axes = ("dp", "tensor")
    chips = devices // 2
    in_order = [1 << bit for bit in range(chips.bit_length() - 1)]
    turned = [in_order[1], in_order[0], *in_order[2:]]
    rounds = len(in_order)
    rounds_more = range(3, rounds)

    def pairs(move):
        found = []
        for device in range(devices):
            for part in range(parts):
                to_chip, to_core, to_part = move(device // 2, device % 2, part)
                source = device * parts + part
                found.append((source, (to_chip * 2 + to_core) * parts + to_part))
        return found

    def by_bit(bit):
        return pairs(
            lambda chip, core, part: (chip ^ (turned if core else in_order)[bit], core, part)
        )

    by_role = pairs(lambda chip, core, part: (chip, part, core))
    swapped = [pair for pair in by_role if pair[0] != pair[1]]
    by_core = pairs(lambda chip, core, part: (chip, 1 - core, part))
    by_part = pairs(lambda chip, core, part: (chip, core, 1 - part))
    from_first_part = [pair for pair in by_part if pair[0] % parts == 0]
    by_chip = [by_bit(bit) for bit in range(rounds)]

    def by_quarter(partner):
        def across(chip, core, part):
            for bit in range(2):
                if partner >> (1 - bit) & 1:
                    chip ^= (turned if core else in_order)[bit]
            return chip, core, part

        return pairs(across)

    def move(value, how):
        return lax.ppermute(value, axes, how)

    def add_more(value):
        for bit in rounds_more:
            other = move(value, by_chip[bit])
            value = (value.astype(F32) + other.astype(F32)).astype(value.dtype)
        return value

    def exchange(values):
        return [values[0]] + [move(values[i], by_quarter(i)) for i in range(1, 4)]

    def body(
        tokens,
        segment_ids,
        pad_mask,
        norm1_gain,
        norm1_shift,
        w_query,
        w_key,
        w_value,
        w_out,
        norm2_gain,
        norm2_shift,
        w_up,
        w_down,
        cotangent,
    ):
        order = Order()
        device = lax.axis_index("dp")
        part = lax.axis_index("tensor")
        core = device % 2
        chip = device // 2
        bits = [
            jnp.where(core == 1, (chip & turned[i]) != 0, (chip & in_order[i]) != 0)
            for i in range(rounds)
        ]
        place = jnp.stack([core, part] + bits).astype(jnp.int32)
        gain1, shift1, gain2, shift2 = (
            vector[None, :] for vector in (norm1_gain, norm1_shift, norm2_gain, norm2_shift)
        )

        mine = move(tokens, by_role)
        ints = jnp.concatenate([segment_ids, pad_mask], axis=0)
        ints = jnp.where(core == part, ints, move(ints, by_core)).astype(F32)
        seg_pad = jnp.concatenate([ints, jnp.zeros((6, ints.shape[1]), F32)], axis=0)

        qkv_l, qkv_s, first = pack_first_call(order, place, w_query, w_key, w_value)
        first_moved = move(first, from_first_part)
        qkv_near = move(qkv_s, by_part)
        n1_own = norm1_call(order, mine, gain1, shift1)
        n1_other = move(n1_own, by_core)
        out_l, up_l, up_s, down_l, down_s, grad = pack_last_call(
            order, place, w_out, w_up, w_down, cotangent
        )
        out_r = move(out_l, by_part)
        up_near = move(up_s, by_part)
        grad_moved = move(grad, swapped)
        down_near = move(down_s, by_part)
        n1, penalty, qk0, first = penalty_call(
            order, place, n1_own, n1_other, first, first_moved, seg_pad
        )
        (qkv_near,) = order.hold((qkv_near,), (penalty,))
        qkv_far = move(qkv_near, by_chip[0])
        qkvt_l, heads_l, lse_l = forward_call(order, n1, (qkv_l,), penalty)
        qkvt_r, heads_r, lse_r, qkv_r, own, send = forward_call(
            order,
            n1,
            (qkv_near, qkv_far),
            penalty,
            place,
            (heads_l, out_l, out_r),
            (up_near,),
        )
        (send,) = order.hold((send,), (down_near,))
        (mine,) = order.hold((mine,), (send,), 5)
        hidden, n2_own = norm2_call(order, mine, own, move(send, by_core), gain2, shift2)
        n2_other = move(n2_own, by_core)
        up_near, down_near = order.hold((up_near, down_near), (mine,))
        up_far = move(up_near, by_chip[0])
        down_far = move(down_near, by_chip[0])
        (grad_moved,) = order.hold((grad_moved,), (n2_own,))
        grad_own = jnp.where(core == part, grad, grad_moved)
        grad_other = move(grad_own, by_core)
        (up_l,) = order.hold((up_l,), (n2_own,), 5)
        *before, keep, send = mlp_call(
            order, place, n2_other, n2_own, grad_other, grad_own, (up_l, down_l)
        )
        got = move(send, by_chip[0])
        weights = (up_near, up_far, down_near, down_far)
        mixed_send, mixed_own, back_send, back_own, *ff_r = mlp_call(
            order, place, n2_other, n2_own, grad_other, grad_own, weights, before
        )
        back_send, *ff_r = order.hold((back_send, *ff_r), (got,))
        ff_r = exchange(ff_r)
        grad_hidden, low_own, sums2 = norm2_back_call(
            order, hidden, back_own, move(back_send, by_core), grad_own, gain2
        )
        low_other = move(low_own, by_core)
        keep, send = half_sums_call(order, place, keep, got)
        got = move(send, by_chip[1])

        low = (low_own, low_other)
        grads_r, wo_r, logit_sum = backward_call(
            order, place, *low, out_r, heads_r, qkvt_r, lse_r, penalty
        )
        at_r = weights_first_call(order, place, n1, grads_r, wo_r)
        ff, ff_move = first_sums_call(order, (keep, got), ff_r)
        ff_got = move(ff_move, by_part)
        at_r = exchange(at_r)
        grads_l, wo_l, logit_sum = backward_call(
            order, place, *low, out_l, heads_l, qkvt_l, lse_l, penalty, logit_sum
        )
        logit_got = move(logit_sum, by_core)
        at_r, ff, *at = weights_second_call(
            order, place, n1, grads_l, wo_l, at_r, (ff, ff_got)
        )
        at_r = move(at_r, by_part)
        ff_got = move(ff, by_chip[2])
        at = exchange(at)
        own, send, late = norm1_grad_call(
            order,
            place,
            (logit_sum, logit_got),
            qk0,
            seg_pad,
            n1,
            grads_l,
            qkv_l,
            first,
            grads_r,
            qkv_r,
            gain1,
            shift1,
            sums2,
        )
        send, late = order.hold((send, late), (*at, at_r))
        received = move(send, by_core)
        late_got = move(late, by_part)
        ff = step0_call(order, (ff, ff_got))
        ff = exchange([add_more(ff)] * 4)
        both = step1_call(order, (late, late_got), (*at, at_r))
        size = at_r.shape[1]
        both_got = move(both, by_chip[2])
        results = results_call(
            order,
            mine,
            own,
            received,
            grad_hidden,
            gain1,
            hidden,
            mixed_own,
            move(mixed_send, by_core),
        )
        (results,) = order.hold((results,), (both_got,))
        moved = move(results, swapped)
        both, ff = step2_call(order, place, size, both, both_got, ff)
        both = exchange([add_more(both)] * 4)
        ff_far = move(ff, by_core)
        up_grad, down_grad = finish_mlp_call(order, place, ff, ff_far)
        both = step3_call(order, place, size, both)
        both_far = move(both, by_core)
        mixed, tokens_grad = copy_call(order, place, results, moved)
        query_grad, key_grad, value_grad, out_grad, *norms = finish_attention_call(
            order, place, size, both, both_far
        )
        return (
            mixed,
            tokens_grad,
            norms[0],
            norms[1],
            query_grad,
            key_grad,
            value_grad,
            out_grad,
            norms[2],
            norms[3],
            up_grad,
            down_grad,
        )

    return body


def solution(mesh):
    in_specs = (
        P(("dp", "tensor"), None),
        P("dp", None),
        P("dp", None),
        P(),
        P(),
        P(None, "tensor"),
        P(None, "tensor"),
        P(None, "tensor"),
        P("tensor", None),
        P(),
        P(),
        P(None, "tensor"),
        P("tensor", None),
        P(("dp", "tensor"), None),
    )
    out_specs = (
        P(("dp", "tensor"), None),
        P(("dp", "tensor"), None),
        P(),
        P(),
        P(None, "tensor"),
        P(None, "tensor"),
        P(None, "tensor"),
        P("tensor", None),
        P(),
        P(),
        P(None, "tensor"),
        P("tensor", None),
    )
    body = make_body(mesh.shape["dp"], mesh.shape["tensor"])
    return jax.shard_map(body, mesh=mesh, in_specs=in_specs, out_specs=out_specs, check_vma=False)
```

```python
import functools

import jax
import jax.numpy as jnp
from jax import lax
from jax.experimental import pallas as pl
from jax.experimental.pallas import tpu as pltpu
from jax.sharding import PartitionSpec as P

HEAD_DIM = 64
EPS = 1e-05
FAR = 1e30
FORWARD_BLOCK = 512
BF16 = jnp.bfloat16
F32 = jnp.float32
TN = (((0,), (0,)), ((), ()))
NT = (((1,), (1,)), ((), ()))
NN = (((1,), (0,)), ((), ()))
TT = (((0,), (1,)), ((), ()))
ERF_C = (
    1.5897294934128858e-07,
    -5.985900079472216e-06,
    8.971378204617447e-05,
    -0.0006257225011275588,
    -0.0001843806018428344,
    0.10276548023357895,
    1.1283797055884355,
)
ERF_X = tuple(c * 0.5 ** (6 - i) * 0.7071067811865476 for i, c in enumerate(ERF_C))


def dot(left, right, dims):
    return lax.dot_general(left, right, dims, preferred_element_type=F32)


def sds(shape, dtype):
    return jax.ShapeDtypeStruct(shape, dtype)


SMEM = pl.BlockSpec(memory_space=pltpu.SMEM)
VMEM = pl.BlockSpec(memory_space=pltpu.VMEM)
ANY = pl.BlockSpec(memory_space=pl.ANY)


WEIGHT = 20.0


class Order:
    def __init__(self):
        self.last = None

    def run(self, us, kernel, operands, out_shape, in_specs=None, after=(), **rest):
        after = tuple(after) + (() if self.last is None else (self.last,))
        count, extra = len(operands), len(after)
        in_specs = list(in_specs or [VMEM] * count) + [ANY] * extra

        def body(*refs):
            kernel(*refs[:count], *refs[count + extra :])

        out = pl.pallas_call(
            body,
            out_shape=out_shape,
            in_specs=in_specs,
            compiler_params=pltpu.CompilerParams(vmem_limit_bytes=58 << 20),
            cost_estimate=pl.CostEstimate(
                flops=int(us * WEIGHT * 1.15e9), bytes_accessed=0, transcendentals=0
            ),
            **rest,
        )(*operands, *after)
        self.last = out[-1] if isinstance(out, (list, tuple)) else out
        return out

    def hold(self, values, after, us=0):
        count = len(values)

        def kernel(*refs):
            pass

        held = pl.pallas_call(
            kernel,
            out_shape=[sds(value.shape, value.dtype) for value in values],
            in_specs=[ANY] * (count + len(after)),
            out_specs=[ANY] * count,
            input_output_aliases={i: i for i in range(count)},
            compiler_params=pltpu.CompilerParams(has_side_effects=True),
            cost_estimate=pl.CostEstimate(
                flops=int(us * WEIGHT * 1.15e9), bytes_accessed=0, transcendentals=0
            ),
        )(*values, *after)
        for value, same in zip(values, held):
            if self.last is value:
                self.last = same
        return held


def whole(shape):
    return pl.BlockSpec(shape, lambda *_: (0,) * len(shape))


def low_sum(*terms):
    total = terms[0].astype(F32)
    for term in terms[1:]:
        total = total + term.astype(F32)
    return total.astype(BF16)


def part_rows(index, size):
    return pl.ds(pl.multiple_of(index * size, size), size)


def split(place, bit, source, keep, send):
    half = keep.shape[1]
    keep[...] = source[:, part_rows(place[2 + bit], half), :]
    send[...] = source[:, part_rows(1 - place[2 + bit], half), :]


def quarter(place):
    return 2 * place[2] + place[3]


def scatter(place, source, outs):
    for partner, out in enumerate(outs):
        out[...] = source[:, part_rows(quarter(place) ^ partner, out.shape[1]), :]


def gather(place, pieces, out):
    for partner, piece in enumerate(pieces):
        out[:, part_rows(quarter(place) ^ partner, piece.shape[1]), :] = piece[...]


def normalize(values):
    center = values - jnp.mean(values, axis=-1, keepdims=True)
    inverse = lax.rsqrt(jnp.mean(center * center, axis=-1, keepdims=True) + EPS)
    return center * inverse, inverse


def norm_back(grad_normed, scaled, inverse, gain):
    grad_scaled = grad_normed * gain
    return inverse * (
        grad_scaled
        - jnp.mean(grad_scaled, axis=-1, keepdims=True)
        - scaled * jnp.mean(grad_scaled * scaled, axis=-1, keepdims=True)
    )


def gelu_pair(x):
    square = x * x
    near = jnp.minimum(square, 64.0)
    poly = ERF_X[0]
    for coefficient in ERF_X[1:]:
        poly = poly * near + coefficient
    phi = 0.5 * jnp.tanh(x * poly) + 0.5
    bell = jnp.exp(square * -0.5)
    return x * phi, phi + x * (bell * 0.3989422804014327)


def pack_first_kernel(place, w_query, w_key, w_value, qkv, qkv_send, first):
    width = qkv.shape[1] // 3
    half = qkv_send.shape[0]
    first[:, :HEAD_DIM] = w_query[:, :HEAD_DIM]
    first[:, HEAD_DIM:] = w_key[:, :HEAD_DIM]
    for core in range(2):

        @pl.when(place[0] == core)
        def _():
            narrow = slice(core * width, (core + 1) * width)
            for i, weight in enumerate((w_query, w_key, w_value)):
                qkv[:, i * width : (i + 1) * width] = weight[:, narrow]

    qkv_send[...] = qkv[pl.ds(pl.multiple_of(place[2] * half, half), half), :]


def pack_first_call(order, place, w_query, w_key, w_value):
    dim, width = w_query.shape[0], w_query.shape[1] // 2
    return order.run(
        4,
        pack_first_kernel,
        (place, w_query, w_key, w_value),
        [
            sds((dim, 3 * width), BF16),
            sds((dim // 2, 3 * width), BF16),
            sds((dim, 2 * HEAD_DIM), BF16),
        ],
        [SMEM] + [VMEM] * 3,
    )


def pack_last_kernel(place, w_out, w_up, w_down, grad, out, up, up_send, down, down_send, grad_out):
    width = out.shape[0]
    units = down.shape[0]
    half = units // 2
    grad_out[...] = grad[...]
    for core in range(2):

        @pl.when(place[0] == core)
        def _():
            wide = slice(core * units, (core + 1) * units)
            out[...] = w_out[core * width : (core + 1) * width, :]
            up[...] = w_up[:, wide]
            down[...] = w_down[wide, :]

    rows = pl.ds(pl.multiple_of(place[2] * half, half), half)
    up_send[...] = up[rows, :]
    down_send[...] = down[rows, :]


def pack_last_call(order, place, w_out, w_up, w_down, grad):
    width, dim = w_out.shape[0] // 2, w_out.shape[1]
    units = w_up.shape[1] // 2
    return order.run(
        5,
        pack_last_kernel,
        (place, w_out, w_up, w_down, grad),
        [
            sds((width, dim), BF16),
            sds((dim, units), BF16),
            sds((dim // 2, units), BF16),
            sds((units, dim), BF16),
            sds((units // 2, dim), BF16),
            sds(grad.shape, BF16),
        ],
        [SMEM] + [VMEM] * 4,
    )


def norm1_kernel(place, tokens, moved, gain, shift, mine, out):
    rows = jnp.where(place[0] == place[1], tokens[...], moved[...])
    mine[...] = rows
    scaled, _ = normalize(rows.astype(F32))
    out[...] = (scaled * gain[...] + shift[...]).astype(BF16)


def rows_spec(block, dim):
    return pl.BlockSpec((block, dim), lambda i: (i, 0))


def norm1_call(order, place, tokens, moved, gain, shift):
    shape = sds(tokens.shape, BF16)
    return order.run(
        2.5,
        norm1_kernel,
        (place, tokens, moved, gain, shift),
        [shape, shape],
        [SMEM] + [VMEM] * 4,
    )


def masks(seg_pad, cols, low, high):
    width = high - low
    seg_row = seg_pad[0:1, low:high]
    pad_row = seg_pad[1:2, low:high]
    row_key = jnp.where(pad_row > 0, seg_row, -2.0)
    col_seg = cols[:high, 0:1]
    col_pad = cols[:high, 1:2]
    col_key = jnp.where(col_pad > 0, col_seg, -1.0)
    key_at = lax.broadcasted_iota(jnp.int32, (high, width), 0)
    query_at = lax.broadcasted_iota(jnp.int32, (high, width), 1) + low
    allowed = ((col_key == seg_row) & (key_at <= query_at)) | (key_at == query_at)
    picked = (col_key == row_key) & (key_at < query_at)
    return allowed, picked


def penalty_kernel(
    block, place, n1_own, n1_other, first, first_moved, seg_pad, n1_out, penalty, qk0, first_out
):
    seq = n1_out.shape[0]
    half = seq // 2
    core = place[0]
    n1_out[pl.ds(pl.multiple_of(core * half, half), half), :] = n1_own[...]
    n1_out[pl.ds(pl.multiple_of((1 - core) * half, half), half), :] = n1_other[...]

    @pl.when(place[1] == 0)
    def _():
        first_out[...] = first[...]

    @pl.when(place[1] != 0)
    def _():
        first_out[...] = first_moved[...]

    qk = dot(first_out[...], n1_out[...], TT)
    q0 = (qk[:HEAD_DIM].astype(BF16) * 0.125).astype(BF16)
    k0 = qk[HEAD_DIM:].astype(BF16)
    qk0[:HEAD_DIM, :] = q0
    qk0[HEAD_DIM:, :] = k0
    seg_value = seg_pad[...]
    cols = seg_value.T
    earlier = lax.broadcasted_iota(jnp.int32, (block, block + 128), 0)
    later = lax.broadcasted_iota(jnp.int32, (block, block + 128), 1)
    sums = ((earlier < later) | (later >= block)).astype(F32).astype(BF16)
    carry = jnp.zeros((seq, 128), F32)
    for low in range(0, seq, block):
        high = low + block
        allowed, picked = masks(seg_value, cols, low, high)
        score = dot(k0[:, :high], q0[:, low:high], TN)
        small = jnp.exp(-jnp.abs(score))
        log1p = jnp.where(small < 1e-3, small - 0.5 * small * small, jnp.log(1.0 + small))
        select = jnp.where(picked, jnp.maximum(score, 0.0) + log1p, 0.0).astype(BF16)
        total = dot(select, sums, NN)
        before = jnp.concatenate([carry[:high]] * (block // 128), axis=1)
        penalty[:high, low:high] = jnp.where(allowed, total[:, :block] + before, FAR)
        if high % FORWARD_BLOCK:
            edge = high + FORWARD_BLOCK - high % FORWARD_BLOCK
            penalty[high:edge, low:high] = jnp.full((edge - high, block), FAR, F32)
        carry = jnp.concatenate([carry[:high] + total[:, block:], carry[high:]], axis=0)


def penalty_call(order, place, n1_own, n1_other, first, first_moved, seg_pad, after=()):
    half, dim = n1_own.shape
    seq = 2 * half
    return order.run(
        6.5,
        functools.partial(penalty_kernel, 256),
        (place, n1_own, n1_other, first, first_moved, seg_pad),
        [
            sds((seq, dim), BF16),
            sds((seq, seq), F32),
            sds((2 * HEAD_DIM, seq), BF16),
            sds(first.shape, BF16),
        ],
        [SMEM] + [VMEM] * 5,
        after,
    )


def forward_kernel(block, last, *refs):
    if last:
        place, n1, near, far, penalty, out_l, w_l, w_r, *refs = refs
        qkv, out, lse, weights, own, send, out_r = refs
    else:
        n1, weights, penalty, qkv, out, lse = refs
    head = pl.program_id(0)
    third = qkv.shape[0] // 3
    seq = qkv.shape[1]

    @pl.when(head == 0)
    def _():
        if last:
            join(place[2], weights, near, far)
        product = dot(weights[...], n1[...], TT).astype(BF16)
        qkv[:third, :] = (product[:third] * 0.125).astype(BF16)
        qkv[third:, :] = product[third:]

    at = pl.multiple_of(head * HEAD_DIM, HEAD_DIM)
    query = qkv[pl.ds(at, HEAD_DIM), :]
    key = qkv[pl.ds(third + at, HEAD_DIM), :]
    value = qkv[pl.ds(2 * third + at, HEAD_DIM), :]
    value = jnp.concatenate([value, jnp.ones((16, seq), BF16)], axis=0)
    for low in range(0, seq, block):
        high = low + block
        logits = dot(key[:, :high], query[:, low:high], TN) - penalty[:high, low:high]
        largest = jnp.max(logits, axis=0, keepdims=True)
        weight = jnp.exp(logits - largest).astype(BF16)
        result = dot(value[:, :high], weight, NN)
        total = result[HEAD_DIM : HEAD_DIM + 1, :]
        out[:, low:high] = (result[:HEAD_DIM] / total).astype(BF16)
        lse[:, low:high] = largest + jnp.log(total)
    if last:
        out_r[pl.ds(at, HEAD_DIM), :] = out[...]

        @pl.when(head == pl.num_programs(0) - 1)
        def _():
            project(place, out_l, out_r, w_l, w_r, own, send)


def join(bit, out, near, far):
    half = near.shape[0]
    out[pl.ds(pl.multiple_of(bit * half, half), half), :] = near[...]
    out[pl.ds(pl.multiple_of((1 - bit) * half, half), half), :] = far[...]


def forward_call(order, n1, weights, penalty, place=None, others=(), after=()):
    seq, dim = n1.shape
    last = place is not None
    width = weights[0].shape[1]
    heads = width // (3 * HEAD_DIM)
    operands = ((place,) if last else ()) + (n1,) + tuple(weights) + (penalty,) + tuple(others)
    in_specs = [SMEM] if last else []
    in_specs += [whole(x.shape) for x in operands if x is not place]
    out_specs = [
        whole((width, seq)),
        pl.BlockSpec((HEAD_DIM, seq), lambda h: (h, 0)),
        pl.BlockSpec((None, 1, seq), lambda h: (h, 0, 0)),
    ]
    out_shape = [
        sds((width, seq), BF16),
        sds((heads * HEAD_DIM, seq), BF16),
        sds((heads, 1, seq), F32),
    ]
    scratch = []
    if last:
        out_specs += [whole((dim, width)), whole((seq // 2, dim)), whole((seq // 2, dim))]
        out_shape += [sds((dim, width), BF16), sds((seq // 2, dim), F32), sds((seq // 2, dim), BF16)]
        scratch.append(pltpu.VMEM((heads * HEAD_DIM, seq), BF16))
    return order.run(
        10,
        functools.partial(forward_kernel, FORWARD_BLOCK, last),
        operands,
        out_shape,
        in_specs,
        after,
        grid=(heads,),
        out_specs=out_specs,
        scratch_shapes=scratch,
    )


def project(place, out_l, out_r, w_l, w_r, own, send):
    half = own.shape[0]
    core = place[0]
    mixed = jnp.concatenate([w_l[...], w_r[...]], axis=0)

    def part(which):
        heads = jnp.concatenate([out_l[:, part_rows(which, half)], out_r[:, part_rows(which, half)]], axis=0)
        return dot(heads, mixed, TN)

    send[...] = part(1 - core).astype(BF16)
    own[...] = part(core)


def norm2_kernel(tokens, own, received, gain, shift, hidden, out):
    total = tokens[...].astype(F32) + (own[...] + received[...].astype(F32))
    hidden[...] = total
    scaled, _ = normalize(total)
    out[...] = (scaled * gain[...] + shift[...]).astype(BF16)


def norm2_call(order, tokens, own, received, gain, shift, after=()):
    size, dim = tokens.shape
    rows = rows_spec(size // 2, dim)
    vector = whole((1, dim))
    return order.run(
        4,
        norm2_kernel,
        (tokens, own, received, gain, shift),
        [sds(tokens.shape, F32), sds(tokens.shape, BF16)],
        [rows] * 3 + [vector] * 2,
        after,
        grid=(2,),
        out_specs=[rows, rows],
    )


def mlp_kernel(first, *refs):
    place, n2_other, n2_own, g_other, g_own, *refs = refs
    if first:
        w_up, w_down, *refs = refs
        before = (None,) * 4
    else:
        up_near, up_far, down_near, down_far, *refs = refs
        before, refs = refs[:4], refs[4:]
    outs, refs = refs[:4], refs[4:]
    count = 2 if first else 4
    parts, refs = refs[:count], refs[count:]
    if not first:
        w_up, w_down, *refs = refs
        join(place[2], w_up, up_near, up_far)
        join(place[2], w_down, down_near, down_far)
    actives, grad_ups, w_grads = refs
    size = n2_own.shape[0]

    def put(out, rows, value, more):
        out[rows, :] = (value if more is None else value + more[rows, :].astype(F32)).astype(out.dtype)

    block = min(256, size)
    for at, n2, g in ((0, n2_other, g_other), (1, n2_own, g_own)):

        def work(step, _):
            rows = part_rows(step, block)
            here = part_rows(step + at * (size // block), block)
            active, slope = gelu_pair(dot(n2[rows, :], w_up[...], NN))
            active = active.astype(BF16)
            grad_up = (dot(g[rows, :], w_down[...], NT) * slope).astype(BF16)
            actives[here, :] = active
            grad_ups[here, :] = grad_up
            put(outs[2 + at], rows, dot(grad_up, w_up[...], NT), before[2 + at])
            put(outs[at], rows, dot(active, w_down[...], NN), before[at])
            return 0

        lax.fori_loop(0, size // block, work, 0)
    w_grads[0] = (
        dot(n2_other[...], grad_ups[:size, :], TN) + dot(n2_own[...], grad_ups[size:, :], TN)
    ).astype(BF16)
    w_grads[1] = (
        dot(actives[:size, :], g_other[...], TN) + dot(actives[size:, :], g_own[...], TN)
    ).astype(BF16)
    if first:
        split(place, 0, w_grads, *parts)
    else:
        scatter(place, w_grads, parts)


def mlp_call(order, place, n2_other, n2_own, g_other, g_own, weights, before=(), after=()):
    size, dim = n2_own.shape
    first = not before
    units = weights[0].shape[1]
    count = 2 if first else 4
    sent = sds((size, dim), BF16)
    kept = sent
    rows = pltpu.VMEM((2 * size, units), BF16)
    scratch = [rows, rows, pltpu.VMEM((2, units, dim), BF16)]
    if not first:
        scratch = [pltpu.VMEM((dim, units), BF16), pltpu.VMEM((units, dim), BF16)] + scratch
    operands = (n2_other, n2_own, g_other, g_own, *weights, *before)
    return order.run(
        14.6,
        functools.partial(mlp_kernel, first),
        (place, *operands),
        [sent, kept, sent, kept] + [sds((2, units // count, dim), BF16)] * count,
        [SMEM] + [VMEM] * len(operands),
        after,
        scratch_shapes=scratch,
    )


def norm2_back_kernel(hidden, own, received, grad, gain, grad_hidden, low, sums):
    normed_grad = own[...].astype(F32) + received[...].astype(F32)
    scaled, inverse = normalize(hidden[...])
    total = grad[...].astype(F32) + norm_back(normed_grad, scaled, inverse, gain[...])
    grad_hidden[...] = total
    low[...] = total.astype(BF16)
    add_sums(sums, normed_grad, scaled)


def add_sums(sums, normed_grad, scaled):
    @pl.when(pl.program_id(0) == 0)
    def _():
        sums[...] = jnp.zeros(sums.shape, F32)

    sums[0:1, :] += jnp.sum(normed_grad * scaled, axis=0, keepdims=True)
    sums[1:2, :] += jnp.sum(normed_grad, axis=0, keepdims=True)


def norm2_back_call(order, hidden, own, received, grad, gain, after=()):
    size, dim = hidden.shape
    rows = rows_spec(size // 2, dim)
    return order.run(
        5,
        norm2_back_kernel,
        (hidden, own, received, grad, gain),
        [sds(hidden.shape, F32), sds(hidden.shape, BF16), sds((8, dim), F32)],
        [rows] * 4 + [whole((1, dim))],
        after,
        grid=(2,),
        out_specs=[rows, rows, whole((8, dim))],
    )


def half_sums_kernel(place, near, far, keep, send):
    half = keep.shape[1]
    for out, which in ((keep, place[3]), (send, 1 - place[3])):
        rows = part_rows(which, half)
        out[...] = low_sum(near[:, rows, :], far[:, rows, :])


def half_sums_call(order, place, near, far):
    groups, rows, dim = near.shape
    return order.run(
        3,
        half_sums_kernel,
        (place, near, far),
        [sds((groups, rows // 2, dim), BF16)] * 2,
        [SMEM] + [VMEM] * 2,
    )


def backward_kernel(first, block, *refs):
    place, g_own, g_other, w_out, heads_out, qkv, lse, penalty, *refs = refs
    if not first:
        before, *refs = refs
    grads, w_grad, logit_sum, grad_full, key_sum, value_sum, *refs = refs
    third = qkv.shape[0] // 3
    seq = qkv.shape[1]
    half = seq // 2
    total = logit_sum if first else refs[0]
    core = place[0]
    grad_full[part_rows(core, half), :] = g_own[...]
    grad_full[part_rows(1 - core, half), :] = g_other[...]
    whole_grad = grad_full[...]
    grad_heads = dot(w_out[...], whole_grad, NT).astype(BF16)
    w_grad[...] = dot(heads_out[...], whole_grad, NN).astype(BF16)
    heads = third // HEAD_DIM
    for head in range(heads):
        rows = slice(head * HEAD_DIM, (head + 1) * HEAD_DIM)
        query = qkv[rows, :]
        key = qkv[third + head * HEAD_DIM : third + (head + 1) * HEAD_DIM, :]
        value = qkv[2 * third + head * HEAD_DIM : 2 * third + (head + 1) * HEAD_DIM, :]
        grad = grad_heads[rows]
        for low in range(0, seq, block):
            high = low + block
            cols = slice(low, high)
            score = dot(key[:, :high], query[:, cols], TN)
            probs = jnp.exp(score - penalty[:high, cols] - lse[head, :, cols])
            grad_probs = dot(value[:, :high], grad[:, cols], TN)
            row_dot = jnp.sum(probs * grad_probs, axis=0, keepdims=True)
            grad_logits = probs * (grad_probs - row_dot)
            if head:
                sum_now = total[:high, cols] + grad_logits
            elif first:
                sum_now = grad_logits
            else:
                sum_now = before[:high, cols] + grad_logits
            if first or head < heads - 1:
                total[:high, cols] = sum_now
            else:
                logit_sum[:high, cols] = sum_now.astype(BF16)
            low_logits = grad_logits.astype(BF16)
            low_probs = probs.astype(BF16)
            grads[rows, cols] = (dot(key[:, :high], low_logits, NN) * 0.125).astype(BF16)
            value_new = dot(grad[:, cols], low_probs, NT)
            key_new = dot(query[:, cols], low_logits, NT)
            if low:
                key_sum[head, :, :low] += key_new[:, :low]
                value_sum[head, :, :low] += value_new[:, :low]
            key_sum[head, :, cols] = key_new[:, low:]
            value_sum[head, :, cols] = value_new[:, low:]
        at = third + head * HEAD_DIM
        grads[at : at + HEAD_DIM, :] = key_sum[head].astype(BF16)
        at = at + third
        grads[at : at + HEAD_DIM, :] = value_sum[head].astype(BF16)


def backward_call(order, place, g_own, g_other, w_out, heads_out, qkv, lse, penalty, before=None):
    width, seq = qkv.shape
    heads = width // (3 * HEAD_DIM)
    first = before is None
    operands = (g_own, g_other, w_out, heads_out, qkv, lse, penalty)
    operands += () if first else (before,)
    sums = pltpu.VMEM((heads, HEAD_DIM, seq), F32)
    scratch = [pltpu.VMEM((seq, g_own.shape[1]), BF16), sums, sums]
    scratch += [] if first else [pltpu.VMEM((seq, seq), F32)]
    return order.run(
        16,
        functools.partial(backward_kernel, first, 256),
        (place, *operands),
        [
            sds((width, seq), BF16),
            sds(w_out.shape, BF16),
            sds((seq, seq), F32 if first else BF16),
        ],
        [SMEM] + [VMEM] * len(operands),
        scratch_shapes=scratch,
    )


def halves(value):
    high = value.astype(BF16)
    return high, (value - high.astype(F32)).astype(BF16)


def select_back(block, core, own, received, qk0, seg_pad, n1, out, w_grad, total_grad):
    seq = own.shape[0]
    q0 = qk0[:HEAD_DIM, :]
    k0 = qk0[HEAD_DIM:, :]
    seg_value = seg_pad[...]
    cols = seg_value.T
    later = lax.broadcasted_iota(jnp.int32, (block, block + 128), 0)
    earlier = lax.broadcasted_iota(jnp.int32, (block, block + 128), 1)
    sums = ((later > earlier) | (earlier >= block)).astype(F32).astype(BF16)
    carry = jnp.zeros((seq, 128), F32)
    total_grad[...] = jnp.zeros(total_grad.shape, F32)
    for low in range(seq - block, -1, -block):
        high = low + block
        logit_sum = own[:high, low:high].astype(F32) + received[:high, low:high].astype(F32)
        top, bottom = halves(logit_sum)
        total = dot(top, sums, NN) + dot(bottom, sums, NN)
        after = jnp.concatenate([carry[:high]] * (block // 128), axis=1)
        select_grad = -(total[:, :block] + after)
        carry = carry[:high] + total[:, block:]
        _, picked = masks(seg_value, cols, low, high)
        score = dot(k0[:, :high], q0[:, low:high], TN)
        through = jnp.where(picked, select_grad / (1.0 + jnp.exp(-score)), 0.0)
        top, bottom = halves(through)

        @pl.when(core == 0)
        def _():
            total_grad[:, low:high] = 0.125 * (
                dot(k0[:, :high], top, NN) + dot(k0[:, :high], bottom, NN)
            )

        @pl.when(core == 1)
        def _():
            total_grad[:, :high] += dot(q0[:, low:high], top, NT) + dot(
                q0[:, low:high], bottom, NT
            )

    out[...] = total_grad[...].astype(BF16)
    w_grad[...] = dot(out[...], n1[...], NN).astype(BF16)


def weights_first_kernel(place, n1, grads, w_out, *refs):
    parts, total = refs[:4], refs[4]
    width = grads.shape[0]
    total[0, :width, :] = dot(grads[...], n1[...], NN).astype(BF16)
    total[0, width:, :] = w_out[...]
    scatter(place, total, parts)


def weights_first_call(order, place, n1, grads, w_out):
    dim = n1.shape[1]
    rows = grads.shape[0] + w_out.shape[0]
    return order.run(
        4,
        weights_first_kernel,
        (place, n1, grads, w_out),
        [sds((1, rows // 4, dim), BF16)] * 4,
        [SMEM] + [VMEM] * 3,
        scratch_shapes=[pltpu.VMEM((1, rows, dim), BF16)],
    )


def weights_second_kernel(place, n1, grads, w_out, *refs):
    parts_r, ff_terms, refs = refs[:4], refs[4:6], refs[6:]
    move_r, ff, *refs = refs
    parts, total = refs[:4], refs[4]
    width = grads.shape[0]
    move_r[...] = low_sum(*(part[...] for part in parts_r))
    ff[...] = low_sum(*(term[...] for term in ff_terms))
    total[0, :width, :] = dot(grads[...], n1[...], NN).astype(BF16)
    total[0, width:, :] = w_out[...]
    scatter(place, total, parts)


def weights_second_call(order, place, n1, grads, w_out, parts_r, ff_terms):
    dim = n1.shape[1]
    rows = grads.shape[0] + w_out.shape[0]
    part = sds((1, rows // 4, dim), BF16)
    return order.run(
        6,
        weights_second_kernel,
        (place, n1, grads, w_out, *parts_r, *ff_terms),
        [part, sds(ff_terms[0].shape, BF16)] + [part] * 4,
        [SMEM] + [VMEM] * 9,
        scratch_shapes=[pltpu.VMEM((1, rows, dim), BF16)],
    )


def norm1_grad_kernel(block, place, logit_own, logit_got, qk0, seg_pad, n1, grads, weights, first, *refs):
    grads_r, weights_r, gain, shift, sums2, own, send, late, extra, extra_w, total_grad = refs
    select_back(
        block, place[0], logit_own, logit_got, qk0, seg_pad, n1, extra, extra_w, total_grad
    )
    half = own.shape[0]
    mine = jnp.where(place[0] == 0, first[:, :HEAD_DIM], first[:, HEAD_DIM:])
    total = dot(grads[...], weights[...], TT) + dot(grads_r[...], weights_r[...], TT)
    total = total + dot(extra[...], mine, TT)
    for core in range(2):

        @pl.when(place[0] == core)
        def _():
            own[...] = total[core * half : (core + 1) * half]
            send[...] = total[(1 - core) * half : (2 - core) * half].astype(BF16)

    scaled = (n1[...].astype(F32) - shift[...]) * (1.0 / gain[...])
    gain_sum = jnp.sum(total * scaled, axis=0, keepdims=True)
    shift_sum = jnp.sum(total, axis=0, keepdims=True)
    norms = jnp.concatenate([gain_sum, shift_sum, sums2[0:2, :], sums2[4:8, :]], axis=0)
    rows = extra_w.shape[0]
    late[:rows, :] = extra_w[...]
    late[rows:, :] = pack_norms(norms)


def norm1_grad_call(order, place, logits, qk0, seg_pad, n1, grads, weights, first, *rest):
    seq, dim = n1.shape
    rows = HEAD_DIM
    return order.run(
        14,
        functools.partial(norm1_grad_kernel, 256),
        (place, *logits, qk0, seg_pad, n1, grads, weights, first, *rest),
        [
            sds((seq // 2, dim), F32),
            sds((seq // 2, dim), BF16),
            sds((rows + 16, dim), BF16),
        ],
        [SMEM] + [VMEM] * 13,
        scratch_shapes=[
            pltpu.VMEM((rows, seq), BF16),
            pltpu.VMEM((rows, dim), BF16),
            pltpu.VMEM((rows, seq), F32),
        ],
    )


def results_kernel(tokens, own, received, grad_hidden, gain, hidden, mixed_own, mixed_received, out):
    mixed = hidden[...] + (mixed_own[...].astype(F32) + mixed_received[...].astype(F32))
    out[0] = mixed.astype(BF16)
    normed_grad = own[...] + received[...].astype(F32)
    scaled, inverse = normalize(tokens[...].astype(F32))
    total = grad_hidden[...] + norm_back(normed_grad, scaled, inverse, gain[...])
    out[1] = total.astype(BF16)


def results_call(order, tokens, own, received, grad_hidden, gain, hidden, mixed_own, mixed_received):
    size, dim = tokens.shape
    rows = rows_spec(size // 2, dim)
    return order.run(
        5,
        results_kernel,
        (tokens, own, received, grad_hidden, gain, hidden, mixed_own, mixed_received),
        sds((2, size, dim), BF16),
        [rows] * 4 + [whole((1, dim))] + [rows] * 3,
        grid=(2,),
        out_specs=pl.BlockSpec((2, size // 2, dim), lambda i: (0, i, 0)),
    )


def pack_norms(norms):
    high = norms.astype(BF16).astype(F32)
    return jnp.concatenate([high, norms - high], axis=0).astype(BF16)


def unpack_norms(ref, rows):
    both = ref[rows:, :].astype(F32)
    return both[:8] + both[8:]


def add_late(terms, out):
    def pairs(values):
        while len(values) > 1:
            values = [values[i] + values[i + 1] for i in range(0, len(values), 2)]
        return values[0]

    rows = out.shape[0] - 16
    out[:rows, :] = pairs([term[:rows, :].astype(F32) for term in terms]).astype(BF16)
    out[rows:, :] = pack_norms(pairs([unpack_norms(term, rows) for term in terms]))


def first_sums_kernel(*refs):
    near, far, *refs = refs
    *parts, ff, ff_move = refs
    ff[...] = low_sum(near[...], far[...])
    ff_move[...] = low_sum(*(part[...] for part in parts))


def first_sums_call(order, terms, parts):
    shape = sds(parts[0].shape, BF16)
    return order.run(3, first_sums_kernel, (*terms, *parts), [shape, shape])


def step0_kernel(own, got, out):
    out[...] = low_sum(own[...], got[...])


def step0_call(order, terms):
    return order.run(2, step0_kernel, terms, sds(terms[0].shape, BF16))


def step1_kernel(late_own, late_got, *refs):
    *at_terms, both = refs
    size = at_terms[0].shape[1]
    both[:size, :] = low_sum(*(term[0] for term in at_terms))
    add_late((late_own, late_got), both.at[size:, :])


def step1_call(order, late_terms, at_terms):
    _, size, dim = at_terms[0].shape
    rows = size + late_terms[0].shape[0]
    return order.run(3, step1_kernel, (*late_terms, *at_terms), sds((rows, dim), BF16))


def step2_kernel(size, place, own, got, *refs):
    *parts, both, ff = refs
    both[:size, :] = low_sum(own[:size, :], got[:size, :])
    add_late((own.at[size:, :], got.at[size:, :]), both.at[size:, :])
    gather(place, parts, ff)


def step2_call(order, place, size, own, got, parts, after=()):
    groups, rows, dim = parts[0].shape
    return order.run(
        4.5,
        functools.partial(step2_kernel, size),
        (place, own, got, *parts),
        [sds(own.shape, BF16), sds((groups, 4 * rows, dim), BF16)],
        [SMEM] + [VMEM] * 6,
        after,
    )


def step3_kernel(size, place, *refs):
    parts, refs = refs[:4], refs[4:]
    (both,) = refs
    for partner, part in enumerate(parts):
        both[part_rows(quarter(place) ^ partner, size), :] = part[:size, :]
    add_late([part.at[size:, :] for part in parts], both.at[4 * size :, :])


def step3_call(order, place, size, parts):
    rows, dim = parts[0].shape
    return order.run(
        3.5,
        functools.partial(step3_kernel, size),
        (place, *parts),
        sds((rows + 3 * size, dim), BF16),
        [SMEM] + [VMEM] * 4,
    )


def copy_kernel(place, results, moved, mixed, tokens_grad):
    stays = place[0] == place[1]
    for source, wanted in ((results, stays), (moved, jnp.logical_not(stays))):

        @pl.when(wanted)
        def _():
            mixed[...] = source[0]
            tokens_grad[...] = source[1]


def copy_call(order, place, results, moved):
    return order.run(
        2,
        copy_kernel,
        (place, results, moved),
        [sds(results.shape[1:], BF16)] * 2,
        [SMEM] + [VMEM] * 2,
    )


def finish_attention_kernel(place, near, far, *outs):
    w_query, w_key, w_value, w_out, *norms = outs
    width = w_out.shape[0] // 2
    late = 4 * width
    rows = late + HEAD_DIM
    total = unpack_norms(near, rows) + unpack_norms(far, rows)
    for i, out in enumerate(norms):
        out[...] = total[i]
    here = (place[1] == 0).astype(F32)
    for core in range(2):

        @pl.when(place[0] == core)
        def _():
            low, high = (near, far) if core == 0 else (far, near)
            for i, out in enumerate((w_query, w_key, w_value)):
                piece = slice(i * width, (i + 1) * width)
                part = low[piece, :].astype(F32)
                if i < 2:
                    more = here * (low, high)[i][late:rows, :].astype(F32)
                    part = jnp.concatenate([part[:HEAD_DIM] + more, part[HEAD_DIM:]], axis=0)
                out[...] = jnp.concatenate([part, high[piece, :].astype(F32)], axis=0).T
            w_out[:width, :] = low[3 * width : late, :].astype(F32)
            w_out[width:, :] = high[3 * width : late, :].astype(F32)


def finish_attention_call(order, place, width, near, far):
    dim = near.shape[1]
    return order.run(
        4.5,
        finish_attention_kernel,
        (place, near, far),
        [sds((dim, 2 * width), F32)] * 3 + [sds((2 * width, dim), F32)] + [sds((dim,), F32)] * 4,
        [SMEM] + [VMEM] * 2,
    )


def finish_mlp_kernel(place, near, far, w_up, w_down):
    units = near.shape[1]
    for core in range(2):

        @pl.when(place[0] == core)
        def _():
            low, high = (near, far) if core == 0 else (far, near)
            w_up[:, :units] = low[0].astype(F32)
            w_up[:, units:] = high[0].astype(F32)
            w_down[:units, :] = low[1].astype(F32)
            w_down[units:, :] = high[1].astype(F32)


def finish_mlp_call(order, place, near, far):
    _, units, dim = near.shape
    return order.run(
        6.8,
        finish_mlp_kernel,
        (place, near, far),
        [sds((dim, 2 * units), F32), sds((2 * units, dim), F32)],
        [SMEM] + [VMEM] * 2,
    )


def make_body(devices, parts):
    axes = ("dp", "tensor")
    chips = devices // 2
    in_order = [1 << bit for bit in range(chips.bit_length() - 1)]
    turned = [in_order[1], in_order[0], *in_order[2:]]
    rounds = len(in_order)
    rounds_more = range(3, rounds)

    def pairs(move):
        found = []
        for device in range(devices):
            for part in range(parts):
                to_chip, to_core, to_part = move(device // 2, device % 2, part)
                source = device * parts + part
                found.append((source, (to_chip * 2 + to_core) * parts + to_part))
        return found

    def by_bit(bit):
        return pairs(
            lambda chip, core, part: (chip ^ (turned if core else in_order)[bit], core, part)
        )

    swapped = [
        pair
        for pair in pairs(lambda chip, core, part: (chip, part, core))
        if pair[0] != pair[1]
    ]
    by_core = pairs(lambda chip, core, part: (chip, 1 - core, part))
    by_part = pairs(lambda chip, core, part: (chip, core, 1 - part))
    from_first_part = [pair for pair in by_part if pair[0] % parts == 0]
    by_chip = [by_bit(bit) for bit in range(rounds)]

    def by_quarter(partner):
        def across(chip, core, part):
            for bit in range(2):
                if partner >> (1 - bit) & 1:
                    chip ^= (turned if core else in_order)[bit]
            return chip, core, part

        return pairs(across)

    def move(value, how):
        return lax.ppermute(value, axes, how)

    def add_more(value):
        for bit in rounds_more:
            other = move(value, by_chip[bit])
            value = (value.astype(F32) + other.astype(F32)).astype(value.dtype)
        return value

    def exchange(values):
        return [values[0]] + [move(values[i], by_quarter(i)) for i in range(1, 4)]

    def body(
        tokens,
        segment_ids,
        pad_mask,
        norm1_gain,
        norm1_shift,
        w_query,
        w_key,
        w_value,
        w_out,
        norm2_gain,
        norm2_shift,
        w_up,
        w_down,
        cotangent,
    ):
        order = Order()
        device = lax.axis_index("dp")
        part = lax.axis_index("tensor")
        core = device % 2
        chip = device // 2
        bits = [
            jnp.where(core == 1, (chip & turned[i]) != 0, (chip & in_order[i]) != 0)
            for i in range(rounds)
        ]
        place = jnp.stack([core, part] + bits).astype(jnp.int32)
        gain1, shift1, gain2, shift2 = (
            vector[None, :] for vector in (norm1_gain, norm1_shift, norm2_gain, norm2_shift)
        )

        moved = move(tokens, swapped)
        ints = jnp.concatenate([segment_ids, pad_mask], axis=0)
        ints = jnp.where(core == part, ints, move(ints, by_core)).astype(F32)
        seg_pad = jnp.concatenate([ints, jnp.zeros((6, ints.shape[1]), F32)], axis=0)

        qkv_l, qkv_s, first = pack_first_call(order, place, w_query, w_key, w_value)
        first_moved = move(first, from_first_part)
        qkv_near = move(qkv_s, by_part)
        mine, n1_own = norm1_call(order, place, tokens, moved, gain1, shift1)
        n1_other = move(n1_own, by_core)
        out_l, up_l, up_s, down_l, down_s, grad = pack_last_call(
            order, place, w_out, w_up, w_down, cotangent
        )
        out_r = move(out_l, by_part)
        up_near = move(up_s, by_part)
        grad_moved = move(grad, swapped)
        down_near = move(down_s, by_part)
        n1, penalty, qk0, first = penalty_call(
            order, place, n1_own, n1_other, first, first_moved, seg_pad
        )
        (qkv_near,) = order.hold((qkv_near,), (penalty,))
        qkv_far = move(qkv_near, by_chip[0])
        qkvt_l, heads_l, lse_l = forward_call(order, n1, (qkv_l,), penalty)
        qkvt_r, heads_r, lse_r, qkv_r, own, send = forward_call(
            order,
            n1,
            (qkv_near, qkv_far),
            penalty,
            place,
            (heads_l, out_l, out_r),
            (up_near,),
        )
        (send,) = order.hold((send,), (down_near,))
        (mine,) = order.hold((mine,), (send,), 5)
        hidden, n2_own = norm2_call(order, mine, own, move(send, by_core), gain2, shift2)
        n2_other = move(n2_own, by_core)
        up_near, down_near = order.hold((up_near, down_near), (mine,))
        up_far = move(up_near, by_chip[0])
        down_far = move(down_near, by_chip[0])
        (grad_moved,) = order.hold((grad_moved,), (n2_own,))
        grad_own = jnp.where(core == part, grad, grad_moved)
        grad_other = move(grad_own, by_core)
        (up_l,) = order.hold((up_l,), (n2_own,), 5)
        *before, keep, send = mlp_call(
            order, place, n2_other, n2_own, grad_other, grad_own, (up_l, down_l)
        )
        got = move(send, by_chip[0])
        weights = (up_near, up_far, down_near, down_far)
        mixed_send, mixed_own, back_send, back_own, *ff_r = mlp_call(
            order, place, n2_other, n2_own, grad_other, grad_own, weights, before
        )
        back_send, *ff_r = order.hold((back_send, *ff_r), (got,))
        ff_r = exchange(ff_r)
        grad_hidden, low_own, sums2 = norm2_back_call(
            order, hidden, back_own, move(back_send, by_core), grad_own, gain2
        )
        low_other = move(low_own, by_core)
        keep, send = half_sums_call(order, place, keep, got)
        got = move(send, by_chip[1])

        low = (low_own, low_other)
        grads_r, wo_r, logit_sum = backward_call(
            order, place, *low, out_r, heads_r, qkvt_r, lse_r, penalty
        )
        at_r = weights_first_call(order, place, n1, grads_r, wo_r)
        ff, ff_move = first_sums_call(order, (keep, got), ff_r)
        ff_got = move(ff_move, by_part)
        at_r = exchange(at_r)
        grads_l, wo_l, logit_sum = backward_call(
            order, place, *low, out_l, heads_l, qkvt_l, lse_l, penalty, logit_sum
        )
        logit_got = move(logit_sum, by_core)
        at_r, ff, *at = weights_second_call(
            order, place, n1, grads_l, wo_l, at_r, (ff, ff_got)
        )
        at_r = move(at_r, by_part)
        ff_got = move(ff, by_chip[2])
        at = exchange(at)
        own, send, late = norm1_grad_call(
            order,
            place,
            (logit_sum, logit_got),
            qk0,
            seg_pad,
            n1,
            grads_l,
            qkv_l,
            first,
            grads_r,
            qkv_r,
            gain1,
            shift1,
            sums2,
        )
        send, late = order.hold((send, late), (*at, at_r))
        received = move(send, by_core)
        late_got = move(late, by_part)
        ff = step0_call(order, (ff, ff_got))
        ff = exchange([add_more(ff)] * 4)
        both = step1_call(order, (late, late_got), (*at, at_r))
        size = at_r.shape[1]
        both_got = move(both, by_chip[2])
        results = results_call(
            order,
            mine,
            own,
            received,
            grad_hidden,
            gain1,
            hidden,
            mixed_own,
            move(mixed_send, by_core),
        )
        (results,) = order.hold((results,), (both_got,))
        moved = move(results, swapped)
        both, ff = step2_call(order, place, size, both, both_got, ff)
        both = exchange([add_more(both)] * 4)
        ff_far = move(ff, by_core)
        up_grad, down_grad = finish_mlp_call(order, place, ff, ff_far)
        both = step3_call(order, place, size, both)
        both_far = move(both, by_core)
        mixed, tokens_grad = copy_call(order, place, results, moved)
        query_grad, key_grad, value_grad, out_grad, *norms = finish_attention_call(
            order, place, size, both, both_far
        )
        return (
            mixed,
            tokens_grad,
            norms[0],
            norms[1],
            query_grad,
            key_grad,
            value_grad,
            out_grad,
            norms[2],
            norms[3],
            up_grad,
            down_grad,
        )

    return body


def solution(mesh):
    in_specs = (
        P(("dp", "tensor"), None),
        P("dp", None),
        P("dp", None),
        P(),
        P(),
        P(None, "tensor"),
        P(None, "tensor"),
        P(None, "tensor"),
        P("tensor", None),
        P(),
        P(),
        P(None, "tensor"),
        P("tensor", None),
        P(("dp", "tensor"), None),
    )
    out_specs = (
        P(("dp", "tensor"), None),
        P(("dp", "tensor"), None),
        P(),
        P(),
        P(None, "tensor"),
        P(None, "tensor"),
        P(None, "tensor"),
        P("tensor", None),
        P(),
        P(),
        P(None, "tensor"),
        P("tensor", None),
    )
    body = make_body(mesh.shape["dp"], mesh.shape["tensor"])
    return jax.shard_map(body, mesh=mesh, in_specs=in_specs, out_specs=out_specs, check_vma=False)
```

```python
import functools

import jax
import jax.numpy as jnp
from jax import lax
from jax.experimental import pallas as pl
from jax.experimental.pallas import tpu as pltpu
from jax.sharding import PartitionSpec as P

HEAD_DIM = 64
EPS = 1e-05
FAR = 1e30
FORWARD_BLOCK = 512
BF16 = jnp.bfloat16
F32 = jnp.float32
TN = (((0,), (0,)), ((), ()))
NT = (((1,), (1,)), ((), ()))
NN = (((1,), (0,)), ((), ()))
TT = (((0,), (1,)), ((), ()))
ERF_C = (
    1.5897294934128858e-07,
    -5.985900079472216e-06,
    8.971378204617447e-05,
    -0.0006257225011275588,
    -0.0001843806018428344,
    0.10276548023357895,
    1.1283797055884355,
)
ERF_X = tuple(c * 0.5 ** (6 - i) * 0.7071067811865476 for i, c in enumerate(ERF_C))


def dot(left, right, dims):
    return lax.dot_general(left, right, dims, preferred_element_type=F32)


def sds(shape, dtype):
    return jax.ShapeDtypeStruct(shape, dtype)


SMEM = pl.BlockSpec(memory_space=pltpu.SMEM)
VMEM = pl.BlockSpec(memory_space=pltpu.VMEM)
ANY = pl.BlockSpec(memory_space=pl.ANY)


WEIGHT = 20.0


class Order:
    def __init__(self):
        self.last = None

    def run(self, us, kernel, operands, out_shape, in_specs=None, after=(), **rest):
        after = tuple(after) + (() if self.last is None else (self.last,))
        count, extra = len(operands), len(after)
        in_specs = list(in_specs or [VMEM] * count) + [ANY] * extra

        def body(*refs):
            kernel(*refs[:count], *refs[count + extra :])

        out = pl.pallas_call(
            body,
            out_shape=out_shape,
            in_specs=in_specs,
            compiler_params=pltpu.CompilerParams(vmem_limit_bytes=58 << 20),
            cost_estimate=pl.CostEstimate(
                flops=int(us * WEIGHT * 1.15e9), bytes_accessed=0, transcendentals=0
            ),
            **rest,
        )(*operands, *after)
        self.last = out[-1] if isinstance(out, (list, tuple)) else out
        return out

    def hold(self, values, after, us=0):
        count = len(values)

        def kernel(*refs):
            pass

        held = pl.pallas_call(
            kernel,
            out_shape=[sds(value.shape, value.dtype) for value in values],
            in_specs=[ANY] * (count + len(after)),
            out_specs=[ANY] * count,
            input_output_aliases={i: i for i in range(count)},
            compiler_params=pltpu.CompilerParams(has_side_effects=True),
            cost_estimate=pl.CostEstimate(
                flops=int(us * WEIGHT * 1.15e9), bytes_accessed=0, transcendentals=0
            ),
        )(*values, *after)
        for value, same in zip(values, held):
            if self.last is value:
                self.last = same
        return held


def whole(shape):
    return pl.BlockSpec(shape, lambda *_: (0,) * len(shape))


def low_sum(*terms):
    total = terms[0].astype(F32)
    for term in terms[1:]:
        total = total + term.astype(F32)
    return total.astype(BF16)


def part_rows(index, size):
    return pl.ds(pl.multiple_of(index * size, size), size)


def split(place, bit, source, keep, send):
    half = keep.shape[1]
    keep[...] = source[:, part_rows(place[2 + bit], half), :]
    send[...] = source[:, part_rows(1 - place[2 + bit], half), :]


def quarter(place):
    return 2 * place[2] + place[3]


def scatter(place, source, outs):
    for partner, out in enumerate(outs):
        out[...] = source[:, part_rows(quarter(place) ^ partner, out.shape[1]), :]


def gather(place, pieces, out):
    for partner, piece in enumerate(pieces):
        out[:, part_rows(quarter(place) ^ partner, piece.shape[1]), :] = piece[...]


def normalize(values):
    center = values - jnp.mean(values, axis=-1, keepdims=True)
    inverse = lax.rsqrt(jnp.mean(center * center, axis=-1, keepdims=True) + EPS)
    return center * inverse, inverse


def norm_back(grad_normed, scaled, inverse, gain):
    grad_scaled = grad_normed * gain
    return inverse * (
        grad_scaled
        - jnp.mean(grad_scaled, axis=-1, keepdims=True)
        - scaled * jnp.mean(grad_scaled * scaled, axis=-1, keepdims=True)
    )


def gelu_pair(x):
    square = x * x
    near = jnp.minimum(square, 64.0)
    poly = ERF_X[0]
    for coefficient in ERF_X[1:]:
        poly = poly * near + coefficient
    phi = 0.5 * jnp.tanh(x * poly) + 0.5
    bell = jnp.exp(square * -0.5)
    return x * phi, phi + x * (bell * 0.3989422804014327)


def pack_first_kernel(place, w_query, w_key, w_value, qkv, qkv_send, first):
    width = qkv.shape[1] // 3
    half = qkv_send.shape[0]
    first[:, :HEAD_DIM] = w_query[:, :HEAD_DIM]
    first[:, HEAD_DIM:] = w_key[:, :HEAD_DIM]
    for core in range(2):

        @pl.when(place[0] == core)
        def _():
            narrow = slice(core * width, (core + 1) * width)
            for i, weight in enumerate((w_query, w_key, w_value)):
                qkv[:, i * width : (i + 1) * width] = weight[:, narrow]

    qkv_send[...] = qkv[pl.ds(pl.multiple_of(place[2] * half, half), half), :]


def pack_first_call(order, place, w_query, w_key, w_value):
    dim, width = w_query.shape[0], w_query.shape[1] // 2
    return order.run(
        4,
        pack_first_kernel,
        (place, w_query, w_key, w_value),
        [
            sds((dim, 3 * width), BF16),
            sds((dim // 2, 3 * width), BF16),
            sds((dim, 2 * HEAD_DIM), BF16),
        ],
        [SMEM] + [VMEM] * 3,
    )


def pack_last_kernel(place, w_out, w_up, w_down, grad, out, up, up_send, down, down_send, grad_out):
    width = out.shape[0]
    units = down.shape[0]
    half = units // 2
    grad_out[...] = grad[...]
    for core in range(2):

        @pl.when(place[0] == core)
        def _():
            wide = slice(core * units, (core + 1) * units)
            out[...] = w_out[core * width : (core + 1) * width, :]
            up[...] = w_up[:, wide]
            down[...] = w_down[wide, :]

    rows = pl.ds(pl.multiple_of(place[2] * half, half), half)
    up_send[...] = up[rows, :]
    down_send[...] = down[rows, :]


def pack_last_call(order, place, w_out, w_up, w_down, grad):
    width, dim = w_out.shape[0] // 2, w_out.shape[1]
    units = w_up.shape[1] // 2
    return order.run(
        5,
        pack_last_kernel,
        (place, w_out, w_up, w_down, grad),
        [
            sds((width, dim), BF16),
            sds((dim, units), BF16),
            sds((dim // 2, units), BF16),
            sds((units, dim), BF16),
            sds((units // 2, dim), BF16),
            sds(grad.shape, BF16),
        ],
        [SMEM] + [VMEM] * 4,
    )


def norm1_kernel(place, tokens, moved, gain, shift, mine, out):
    rows = jnp.where(place[0] == place[1], tokens[...], moved[...])
    mine[...] = rows
    scaled, _ = normalize(rows.astype(F32))
    out[...] = (scaled * gain[...] + shift[...]).astype(BF16)


def rows_spec(block, dim):
    return pl.BlockSpec((block, dim), lambda i: (i, 0))


def norm1_call(order, place, tokens, moved, gain, shift):
    shape = sds(tokens.shape, BF16)
    return order.run(
        2.5,
        norm1_kernel,
        (place, tokens, moved, gain, shift),
        [shape, shape],
        [SMEM] + [VMEM] * 4,
    )


def masks(seg_pad, cols, low, high):
    width = high - low
    seg_row = seg_pad[0:1, low:high]
    pad_row = seg_pad[1:2, low:high]
    row_key = jnp.where(pad_row > 0, seg_row, -2.0)
    col_seg = cols[:high, 0:1]
    col_pad = cols[:high, 1:2]
    col_key = jnp.where(col_pad > 0, col_seg, -1.0)
    key_at = lax.broadcasted_iota(jnp.int32, (high, width), 0)
    query_at = lax.broadcasted_iota(jnp.int32, (high, width), 1) + low
    allowed = ((col_key == seg_row) & (key_at <= query_at)) | (key_at == query_at)
    picked = (col_key == row_key) & (key_at < query_at)
    return allowed, picked


def penalty_kernel(
    block, place, n1_own, n1_other, first, first_moved, seg_pad, n1_out, penalty, qk0, first_out
):
    seq = n1_out.shape[0]
    half = seq // 2
    core = place[0]
    n1_out[pl.ds(pl.multiple_of(core * half, half), half), :] = n1_own[...]
    n1_out[pl.ds(pl.multiple_of((1 - core) * half, half), half), :] = n1_other[...]

    @pl.when(place[1] == 0)
    def _():
        first_out[...] = first[...]

    @pl.when(place[1] != 0)
    def _():
        first_out[...] = first_moved[...]

    qk = dot(first_out[...], n1_out[...], TT)
    q0 = (qk[:HEAD_DIM].astype(BF16) * 0.125).astype(BF16)
    k0 = qk[HEAD_DIM:].astype(BF16)
    qk0[:HEAD_DIM, :] = q0
    qk0[HEAD_DIM:, :] = k0
    seg_value = seg_pad[...]
    cols = seg_value.T
    earlier = lax.broadcasted_iota(jnp.int32, (block, block + 128), 0)
    later = lax.broadcasted_iota(jnp.int32, (block, block + 128), 1)
    sums = ((earlier < later) | (later >= block)).astype(F32).astype(BF16)
    carry = jnp.zeros((seq, 128), F32)
    for low in range(0, seq, block):
        high = low + block
        allowed, picked = masks(seg_value, cols, low, high)
        score = dot(k0[:, :high], q0[:, low:high], TN)
        small = jnp.exp(-jnp.abs(score))
        log1p = jnp.where(small < 1e-3, small - 0.5 * small * small, jnp.log(1.0 + small))
        select = jnp.where(picked, jnp.maximum(score, 0.0) + log1p, 0.0).astype(BF16)
        total = dot(select, sums, NN)
        before = jnp.concatenate([carry[:high]] * (block // 128), axis=1)
        penalty[:high, low:high] = jnp.where(allowed, total[:, :block] + before, FAR)
        if high % FORWARD_BLOCK:
            edge = high + FORWARD_BLOCK - high % FORWARD_BLOCK
            penalty[high:edge, low:high] = jnp.full((edge - high, block), FAR, F32)
        carry = jnp.concatenate([carry[:high] + total[:, block:], carry[high:]], axis=0)


def penalty_call(order, place, n1_own, n1_other, first, first_moved, seg_pad, after=()):
    half, dim = n1_own.shape
    seq = 2 * half
    return order.run(
        6.5,
        functools.partial(penalty_kernel, 256),
        (place, n1_own, n1_other, first, first_moved, seg_pad),
        [
            sds((seq, dim), BF16),
            sds((seq, seq), F32),
            sds((2 * HEAD_DIM, seq), BF16),
            sds(first.shape, BF16),
        ],
        [SMEM] + [VMEM] * 5,
        after,
    )


def forward_kernel(block, last, *refs):
    if last:
        place, n1, near, far, penalty, out_l, w_l, w_r, *refs = refs
        qkv, out, lse, weights, own, send, out_r = refs
    else:
        n1, weights, penalty, qkv, out, lse = refs
    head = pl.program_id(0)
    third = qkv.shape[0] // 3
    seq = qkv.shape[1]

    @pl.when(head == 0)
    def _():
        if last:
            join(place[2], weights, near, far)
        product = dot(weights[...], n1[...], TT).astype(BF16)
        qkv[:third, :] = (product[:third] * 0.125).astype(BF16)
        qkv[third:, :] = product[third:]

    at = pl.multiple_of(head * HEAD_DIM, HEAD_DIM)
    query = qkv[pl.ds(at, HEAD_DIM), :]
    key = qkv[pl.ds(third + at, HEAD_DIM), :]
    value = qkv[pl.ds(2 * third + at, HEAD_DIM), :]
    value = jnp.concatenate([value, jnp.ones((16, seq), BF16)], axis=0)
    for low in range(0, seq, block):
        high = low + block
        logits = dot(key[:, :high], query[:, low:high], TN) - penalty[:high, low:high]
        largest = jnp.max(logits, axis=0, keepdims=True)
        weight = jnp.exp(logits - largest).astype(BF16)
        result = dot(value[:, :high], weight, NN)
        total = result[HEAD_DIM : HEAD_DIM + 1, :]
        out[:, low:high] = (result[:HEAD_DIM] / total).astype(BF16)
        lse[:, low:high] = largest + jnp.log(total)
    if last:
        out_r[pl.ds(at, HEAD_DIM), :] = out[...]

        @pl.when(head == pl.num_programs(0) - 1)
        def _():
            project(place, out_l, out_r, w_l, w_r, own, send)


def join(bit, out, near, far):
    half = near.shape[0]
    out[pl.ds(pl.multiple_of(bit * half, half), half), :] = near[...]
    out[pl.ds(pl.multiple_of((1 - bit) * half, half), half), :] = far[...]


def forward_call(order, n1, weights, penalty, place=None, others=(), after=()):
    seq, dim = n1.shape
    last = place is not None
    width = weights[0].shape[1]
    heads = width // (3 * HEAD_DIM)
    operands = ((place,) if last else ()) + (n1,) + tuple(weights) + (penalty,) + tuple(others)
    in_specs = [SMEM] if last else []
    in_specs += [whole(x.shape) for x in operands if x is not place]
    out_specs = [
        whole((width, seq)),
        pl.BlockSpec((HEAD_DIM, seq), lambda h: (h, 0)),
        pl.BlockSpec((None, 1, seq), lambda h: (h, 0, 0)),
    ]
    out_shape = [
        sds((width, seq), BF16),
        sds((heads * HEAD_DIM, seq), BF16),
        sds((heads, 1, seq), F32),
    ]
    scratch = []
    if last:
        out_specs += [whole((dim, width)), whole((seq // 2, dim)), whole((seq // 2, dim))]
        out_shape += [sds((dim, width), BF16), sds((seq // 2, dim), F32), sds((seq // 2, dim), BF16)]
        scratch.append(pltpu.VMEM((heads * HEAD_DIM, seq), BF16))
    return order.run(
        10,
        functools.partial(forward_kernel, FORWARD_BLOCK, last),
        operands,
        out_shape,
        in_specs,
        after,
        grid=(heads,),
        out_specs=out_specs,
        scratch_shapes=scratch,
    )


def project(place, out_l, out_r, w_l, w_r, own, send):
    half = own.shape[0]
    core = place[0]
    mixed = jnp.concatenate([w_l[...], w_r[...]], axis=0)

    def part(which):
        heads = jnp.concatenate([out_l[:, part_rows(which, half)], out_r[:, part_rows(which, half)]], axis=0)
        return dot(heads, mixed, TN)

    send[...] = part(1 - core).astype(BF16)
    own[...] = part(core)


def norm2_kernel(tokens, own, received, gain, shift, hidden, out):
    total = tokens[...].astype(F32) + (own[...] + received[...].astype(F32))
    hidden[...] = total
    scaled, _ = normalize(total)
    out[...] = (scaled * gain[...] + shift[...]).astype(BF16)


def norm2_call(order, tokens, own, received, gain, shift, after=()):
    size, dim = tokens.shape
    rows = rows_spec(size // 2, dim)
    vector = whole((1, dim))
    return order.run(
        4,
        norm2_kernel,
        (tokens, own, received, gain, shift),
        [sds(tokens.shape, F32), sds(tokens.shape, BF16)],
        [rows] * 3 + [vector] * 2,
        after,
        grid=(2,),
        out_specs=[rows, rows],
    )


def mlp_kernel(first, *refs):
    place, n2_other, n2_own, g_other, g_own, *refs = refs
    if first:
        w_up, w_down, *refs = refs
        before = (None,) * 4
    else:
        up_near, up_far, down_near, down_far, *refs = refs
        before, refs = refs[:4], refs[4:]
    outs, refs = refs[:4], refs[4:]
    count = 2 if first else 4
    parts, refs = refs[:count], refs[count:]
    if not first:
        w_up, w_down, *refs = refs
        join(place[2], w_up, up_near, up_far)
        join(place[2], w_down, down_near, down_far)
    actives, grad_ups, w_grads = refs
    size = n2_own.shape[0]

    def put(out, rows, value, more):
        out[rows, :] = (value if more is None else value + more[rows, :].astype(F32)).astype(out.dtype)

    block = min(512, size)
    for at, n2, g in ((0, n2_other, g_other), (1, n2_own, g_own)):

        def work(step, _):
            rows = part_rows(step, block)
            here = part_rows(step + at * (size // block), block)
            active, slope = gelu_pair(dot(n2[rows, :], w_up[...], NN))
            active = active.astype(BF16)
            grad_up = (dot(g[rows, :], w_down[...], NT) * slope).astype(BF16)
            actives[here, :] = active
            grad_ups[here, :] = grad_up
            put(outs[2 + at], rows, dot(grad_up, w_up[...], NT), before[2 + at])
            put(outs[at], rows, dot(active, w_down[...], NN), before[at])
            return 0

        lax.fori_loop(0, size // block, work, 0)
    w_grads[0] = (
        dot(n2_other[...], grad_ups[:size, :], TN) + dot(n2_own[...], grad_ups[size:, :], TN)
    ).astype(BF16)
    w_grads[1] = (
        dot(actives[:size, :], g_other[...], TN) + dot(actives[size:, :], g_own[...], TN)
    ).astype(BF16)
    if first:
        split(place, 0, w_grads, *parts)
    else:
        scatter(place, w_grads, parts)


def mlp_call(order, place, n2_other, n2_own, g_other, g_own, weights, before=(), after=()):
    size, dim = n2_own.shape
    first = not before
    units = weights[0].shape[1]
    count = 2 if first else 4
    sent = sds((size, dim), BF16)
    kept = sent
    rows = pltpu.VMEM((2 * size, units), BF16)
    scratch = [rows, rows, pltpu.VMEM((2, units, dim), BF16)]
    if not first:
        scratch = [pltpu.VMEM((dim, units), BF16), pltpu.VMEM((units, dim), BF16)] + scratch
    operands = (n2_other, n2_own, g_other, g_own, *weights, *before)
    return order.run(
        14.6,
        functools.partial(mlp_kernel, first),
        (place, *operands),
        [sent, kept, sent, kept] + [sds((2, units // count, dim), BF16)] * count,
        [SMEM] + [VMEM] * len(operands),
        after,
        scratch_shapes=scratch,
    )


def norm2_back_kernel(hidden, own, received, grad, gain, grad_hidden, low, sums):
    normed_grad = own[...].astype(F32) + received[...].astype(F32)
    scaled, inverse = normalize(hidden[...])
    total = grad[...].astype(F32) + norm_back(normed_grad, scaled, inverse, gain[...])
    grad_hidden[...] = total
    low[...] = total.astype(BF16)
    add_sums(sums, normed_grad, scaled)


def add_sums(sums, normed_grad, scaled):
    @pl.when(pl.program_id(0) == 0)
    def _():
        sums[...] = jnp.zeros(sums.shape, F32)

    sums[0:1, :] += jnp.sum(normed_grad * scaled, axis=0, keepdims=True)
    sums[1:2, :] += jnp.sum(normed_grad, axis=0, keepdims=True)


def norm2_back_call(order, hidden, own, received, grad, gain, after=()):
    size, dim = hidden.shape
    rows = rows_spec(size // 2, dim)
    return order.run(
        5,
        norm2_back_kernel,
        (hidden, own, received, grad, gain),
        [sds(hidden.shape, F32), sds(hidden.shape, BF16), sds((8, dim), F32)],
        [rows] * 4 + [whole((1, dim))],
        after,
        grid=(2,),
        out_specs=[rows, rows, whole((8, dim))],
    )


def half_sums_kernel(place, near, far, keep, send):
    half = keep.shape[1]
    for out, which in ((keep, place[3]), (send, 1 - place[3])):
        rows = part_rows(which, half)
        out[...] = low_sum(near[:, rows, :], far[:, rows, :])


def half_sums_call(order, place, near, far):
    groups, rows, dim = near.shape
    return order.run(
        3,
        half_sums_kernel,
        (place, near, far),
        [sds((groups, rows // 2, dim), BF16)] * 2,
        [SMEM] + [VMEM] * 2,
    )


def backward_kernel(first, block, *refs):
    place, g_own, g_other, w_out, heads_out, qkv, lse, penalty, *refs = refs
    if not first:
        before, *refs = refs
    grads, w_grad, logit_sum, grad_full, key_sum, value_sum, *refs = refs
    third = qkv.shape[0] // 3
    seq = qkv.shape[1]
    half = seq // 2
    total = logit_sum if first else refs[0]
    core = place[0]
    grad_full[part_rows(core, half), :] = g_own[...]
    grad_full[part_rows(1 - core, half), :] = g_other[...]
    whole_grad = grad_full[...]
    grad_heads = dot(w_out[...], whole_grad, NT).astype(BF16)
    w_grad[...] = dot(heads_out[...], whole_grad, NN).astype(BF16)
    heads = third // HEAD_DIM
    for head in range(heads):
        rows = slice(head * HEAD_DIM, (head + 1) * HEAD_DIM)
        query = qkv[rows, :]
        key = qkv[third + head * HEAD_DIM : third + (head + 1) * HEAD_DIM, :]
        value = qkv[2 * third + head * HEAD_DIM : 2 * third + (head + 1) * HEAD_DIM, :]
        grad = grad_heads[rows]
        for low in range(0, seq, block):
            high = low + block
            cols = slice(low, high)
            score = dot(key[:, :high], query[:, cols], TN)
            probs = jnp.exp(score - penalty[:high, cols] - lse[head, :, cols])
            grad_probs = dot(value[:, :high], grad[:, cols], TN)
            row_dot = jnp.sum(probs * grad_probs, axis=0, keepdims=True)
            grad_logits = probs * (grad_probs - row_dot)
            if head:
                sum_now = total[:high, cols] + grad_logits
            elif first:
                sum_now = grad_logits
            else:
                sum_now = before[:high, cols] + grad_logits
            if first or head < heads - 1:
                total[:high, cols] = sum_now
            else:
                logit_sum[:high, cols] = sum_now.astype(BF16)
            low_logits = grad_logits.astype(BF16)
            low_probs = probs.astype(BF16)
            grads[rows, cols] = (dot(key[:, :high], low_logits, NN) * 0.125).astype(BF16)
            value_new = dot(grad[:, cols], low_probs, NT)
            key_new = dot(query[:, cols], low_logits, NT)
            if low:
                key_sum[head, :, :low] += key_new[:, :low]
                value_sum[head, :, :low] += value_new[:, :low]
            key_sum[head, :, cols] = key_new[:, low:]
            value_sum[head, :, cols] = value_new[:, low:]
        at = third + head * HEAD_DIM
        grads[at : at + HEAD_DIM, :] = key_sum[head].astype(BF16)
        at = at + third
        grads[at : at + HEAD_DIM, :] = value_sum[head].astype(BF16)


def backward_call(order, place, g_own, g_other, w_out, heads_out, qkv, lse, penalty, before=None):
    width, seq = qkv.shape
    heads = width // (3 * HEAD_DIM)
    first = before is None
    operands = (g_own, g_other, w_out, heads_out, qkv, lse, penalty)
    operands += () if first else (before,)
    sums = pltpu.VMEM((heads, HEAD_DIM, seq), F32)
    scratch = [pltpu.VMEM((seq, g_own.shape[1]), BF16), sums, sums]
    scratch += [] if first else [pltpu.VMEM((seq, seq), F32)]
    return order.run(
        16,
        functools.partial(backward_kernel, first, 256),
        (place, *operands),
        [
            sds((width, seq), BF16),
            sds(w_out.shape, BF16),
            sds((seq, seq), F32 if first else BF16),
        ],
        [SMEM] + [VMEM] * len(operands),
        scratch_shapes=scratch,
    )


def halves(value):
    high = value.astype(BF16)
    return high, (value - high.astype(F32)).astype(BF16)


def select_back(block, core, own, received, qk0, seg_pad, n1, out, w_grad, total_grad):
    seq = own.shape[0]
    q0 = qk0[:HEAD_DIM, :]
    k0 = qk0[HEAD_DIM:, :]
    seg_value = seg_pad[...]
    cols = seg_value.T
    later = lax.broadcasted_iota(jnp.int32, (block, block + 128), 0)
    earlier = lax.broadcasted_iota(jnp.int32, (block, block + 128), 1)
    sums = ((later > earlier) | (earlier >= block)).astype(F32).astype(BF16)
    carry = jnp.zeros((seq, 128), F32)
    total_grad[...] = jnp.zeros(total_grad.shape, F32)
    for low in range(seq - block, -1, -block):
        high = low + block
        logit_sum = own[:high, low:high].astype(F32) + received[:high, low:high].astype(F32)
        top, bottom = halves(logit_sum)
        total = dot(top, sums, NN) + dot(bottom, sums, NN)
        after = jnp.concatenate([carry[:high]] * (block // 128), axis=1)
        select_grad = -(total[:, :block] + after)
        carry = carry[:high] + total[:, block:]
        _, picked = masks(seg_value, cols, low, high)
        score = dot(k0[:, :high], q0[:, low:high], TN)
        through = jnp.where(picked, select_grad / (1.0 + jnp.exp(-score)), 0.0)
        top, bottom = halves(through)

        @pl.when(core == 0)
        def _():
            total_grad[:, low:high] = 0.125 * (
                dot(k0[:, :high], top, NN) + dot(k0[:, :high], bottom, NN)
            )

        @pl.when(core == 1)
        def _():
            total_grad[:, :high] += dot(q0[:, low:high], top, NT) + dot(
                q0[:, low:high], bottom, NT
            )

    out[...] = total_grad[...].astype(BF16)
    w_grad[...] = dot(out[...], n1[...], NN).astype(BF16)


def weights_first_kernel(place, n1, grads, w_out, *refs):
    parts, total = refs[:4], refs[4]
    width = grads.shape[0]
    total[0, :width, :] = dot(grads[...], n1[...], NN).astype(BF16)
    total[0, width:, :] = w_out[...]
    scatter(place, total, parts)


def weights_first_call(order, place, n1, grads, w_out):
    dim = n1.shape[1]
    rows = grads.shape[0] + w_out.shape[0]
    return order.run(
        4,
        weights_first_kernel,
        (place, n1, grads, w_out),
        [sds((1, rows // 4, dim), BF16)] * 4,
        [SMEM] + [VMEM] * 3,
        scratch_shapes=[pltpu.VMEM((1, rows, dim), BF16)],
    )


def weights_second_kernel(place, n1, grads, w_out, *refs):
    parts_r, ff_terms, refs = refs[:4], refs[4:6], refs[6:]
    move_r, ff, *refs = refs
    parts, total = refs[:4], refs[4]
    width = grads.shape[0]
    move_r[...] = low_sum(*(part[...] for part in parts_r))
    ff[...] = low_sum(*(term[...] for term in ff_terms))
    total[0, :width, :] = dot(grads[...], n1[...], NN).astype(BF16)
    total[0, width:, :] = w_out[...]
    scatter(place, total, parts)


def weights_second_call(order, place, n1, grads, w_out, parts_r, ff_terms):
    dim = n1.shape[1]
    rows = grads.shape[0] + w_out.shape[0]
    part = sds((1, rows // 4, dim), BF16)
    return order.run(
        6,
        weights_second_kernel,
        (place, n1, grads, w_out, *parts_r, *ff_terms),
        [part, sds(ff_terms[0].shape, BF16)] + [part] * 4,
        [SMEM] + [VMEM] * 9,
        scratch_shapes=[pltpu.VMEM((1, rows, dim), BF16)],
    )


def norm1_grad_kernel(block, place, logit_own, logit_got, qk0, seg_pad, n1, grads, weights, first, *refs):
    grads_r, weights_r, gain, shift, sums2, own, send, late, extra, extra_w, total_grad = refs
    select_back(
        block, place[0], logit_own, logit_got, qk0, seg_pad, n1, extra, extra_w, total_grad
    )
    half = own.shape[0]
    mine = jnp.where(place[0] == 0, first[:, :HEAD_DIM], first[:, HEAD_DIM:])
    total = dot(grads[...], weights[...], TT) + dot(grads_r[...], weights_r[...], TT)
    total = total + dot(extra[...], mine, TT)
    for core in range(2):

        @pl.when(place[0] == core)
        def _():
            own[...] = total[core * half : (core + 1) * half]
            send[...] = total[(1 - core) * half : (2 - core) * half].astype(BF16)

    scaled = (n1[...].astype(F32) - shift[...]) * (1.0 / gain[...])
    gain_sum = jnp.sum(total * scaled, axis=0, keepdims=True)
    shift_sum = jnp.sum(total, axis=0, keepdims=True)
    norms = jnp.concatenate([gain_sum, shift_sum, sums2[0:2, :], sums2[4:8, :]], axis=0)
    rows = extra_w.shape[0]
    late[:rows, :] = extra_w[...]
    late[rows:, :] = pack_norms(norms)


def norm1_grad_call(order, place, logits, qk0, seg_pad, n1, grads, weights, first, *rest):
    seq, dim = n1.shape
    rows = HEAD_DIM
    return order.run(
        14,
        functools.partial(norm1_grad_kernel, 256),
        (place, *logits, qk0, seg_pad, n1, grads, weights, first, *rest),
        [
            sds((seq // 2, dim), F32),
            sds((seq // 2, dim), BF16),
            sds((rows + 16, dim), BF16),
        ],
        [SMEM] + [VMEM] * 13,
        scratch_shapes=[
            pltpu.VMEM((rows, seq), BF16),
            pltpu.VMEM((rows, dim), BF16),
            pltpu.VMEM((rows, seq), F32),
        ],
    )


def results_kernel(tokens, own, received, grad_hidden, gain, hidden, mixed_own, mixed_received, out):
    mixed = hidden[...] + (mixed_own[...].astype(F32) + mixed_received[...].astype(F32))
    out[0] = mixed.astype(BF16)
    normed_grad = own[...] + received[...].astype(F32)
    scaled, inverse = normalize(tokens[...].astype(F32))
    total = grad_hidden[...] + norm_back(normed_grad, scaled, inverse, gain[...])
    out[1] = total.astype(BF16)


def results_call(order, tokens, own, received, grad_hidden, gain, hidden, mixed_own, mixed_received):
    size, dim = tokens.shape
    rows = rows_spec(size // 2, dim)
    return order.run(
        5,
        results_kernel,
        (tokens, own, received, grad_hidden, gain, hidden, mixed_own, mixed_received),
        sds((2, size, dim), BF16),
        [rows] * 4 + [whole((1, dim))] + [rows] * 3,
        grid=(2,),
        out_specs=pl.BlockSpec((2, size // 2, dim), lambda i: (0, i, 0)),
    )


def pack_norms(norms):
    high = norms.astype(BF16).astype(F32)
    return jnp.concatenate([high, norms - high], axis=0).astype(BF16)


def unpack_norms(ref, rows):
    both = ref[rows:, :].astype(F32)
    return both[:8] + both[8:]


def add_late(terms, out):
    def pairs(values):
        while len(values) > 1:
            values = [values[i] + values[i + 1] for i in range(0, len(values), 2)]
        return values[0]

    rows = out.shape[0] - 16
    out[:rows, :] = pairs([term[:rows, :].astype(F32) for term in terms]).astype(BF16)
    out[rows:, :] = pack_norms(pairs([unpack_norms(term, rows) for term in terms]))


def first_sums_kernel(*refs):
    near, far, *refs = refs
    *parts, ff, ff_move = refs
    ff[...] = low_sum(near[...], far[...])
    ff_move[...] = low_sum(*(part[...] for part in parts))


def first_sums_call(order, terms, parts):
    shape = sds(parts[0].shape, BF16)
    return order.run(3, first_sums_kernel, (*terms, *parts), [shape, shape])


def step0_kernel(own, got, out):
    out[...] = low_sum(own[...], got[...])


def step0_call(order, terms):
    return order.run(2, step0_kernel, terms, sds(terms[0].shape, BF16))


def step1_kernel(late_own, late_got, *refs):
    *at_terms, both = refs
    size = at_terms[0].shape[1]
    both[:size, :] = low_sum(*(term[0] for term in at_terms))
    add_late((late_own, late_got), both.at[size:, :])


def step1_call(order, late_terms, at_terms):
    _, size, dim = at_terms[0].shape
    rows = size + late_terms[0].shape[0]
    return order.run(3, step1_kernel, (*late_terms, *at_terms), sds((rows, dim), BF16))


def step2_kernel(size, place, own, got, *refs):
    *parts, both, ff = refs
    both[:size, :] = low_sum(own[:size, :], got[:size, :])
    add_late((own.at[size:, :], got.at[size:, :]), both.at[size:, :])
    gather(place, parts, ff)


def step2_call(order, place, size, own, got, parts, after=()):
    groups, rows, dim = parts[0].shape
    return order.run(
        4.5,
        functools.partial(step2_kernel, size),
        (place, own, got, *parts),
        [sds(own.shape, BF16), sds((groups, 4 * rows, dim), BF16)],
        [SMEM] + [VMEM] * 6,
        after,
    )


def step3_kernel(size, place, *refs):
    parts, refs = refs[:4], refs[4:]
    (both,) = refs
    for partner, part in enumerate(parts):
        both[part_rows(quarter(place) ^ partner, size), :] = part[:size, :]
    add_late([part.at[size:, :] for part in parts], both.at[4 * size :, :])


def step3_call(order, place, size, parts):
    rows, dim = parts[0].shape
    return order.run(
        3.5,
        functools.partial(step3_kernel, size),
        (place, *parts),
        sds((rows + 3 * size, dim), BF16),
        [SMEM] + [VMEM] * 4,
    )


def copy_kernel(place, results, moved, mixed, tokens_grad):
    stays = place[0] == place[1]
    for source, wanted in ((results, stays), (moved, jnp.logical_not(stays))):

        @pl.when(wanted)
        def _():
            mixed[...] = source[0]
            tokens_grad[...] = source[1]


def copy_call(order, place, results, moved):
    return order.run(
        2,
        copy_kernel,
        (place, results, moved),
        [sds(results.shape[1:], BF16)] * 2,
        [SMEM] + [VMEM] * 2,
    )


def finish_attention_kernel(place, near, far, *outs):
    w_query, w_key, w_value, w_out, *norms = outs
    width = w_out.shape[0] // 2
    late = 4 * width
    rows = late + HEAD_DIM
    total = unpack_norms(near, rows) + unpack_norms(far, rows)
    for i, out in enumerate(norms):
        out[...] = total[i]
    here = (place[1] == 0).astype(F32)
    for core in range(2):

        @pl.when(place[0] == core)
        def _():
            low, high = (near, far) if core == 0 else (far, near)
            for i, out in enumerate((w_query, w_key, w_value)):
                piece = slice(i * width, (i + 1) * width)
                part = low[piece, :].astype(F32)
                if i < 2:
                    more = here * (low, high)[i][late:rows, :].astype(F32)
                    part = jnp.concatenate([part[:HEAD_DIM] + more, part[HEAD_DIM:]], axis=0)
                out[...] = jnp.concatenate([part, high[piece, :].astype(F32)], axis=0).T
            w_out[:width, :] = low[3 * width : late, :].astype(F32)
            w_out[width:, :] = high[3 * width : late, :].astype(F32)


def finish_attention_call(order, place, width, near, far):
    dim = near.shape[1]
    return order.run(
        4.5,
        finish_attention_kernel,
        (place, near, far),
        [sds((dim, 2 * width), F32)] * 3 + [sds((2 * width, dim), F32)] + [sds((dim,), F32)] * 4,
        [SMEM] + [VMEM] * 2,
    )


def finish_mlp_kernel(place, near, far, w_up, w_down):
    units = near.shape[1]
    for core in range(2):

        @pl.when(place[0] == core)
        def _():
            low, high = (near, far) if core == 0 else (far, near)
            w_up[:, :units] = low[0].astype(F32)
            w_up[:, units:] = high[0].astype(F32)
            w_down[:units, :] = low[1].astype(F32)
            w_down[units:, :] = high[1].astype(F32)


def finish_mlp_call(order, place, near, far):
    _, units, dim = near.shape
    return order.run(
        6.8,
        finish_mlp_kernel,
        (place, near, far),
        [sds((dim, 2 * units), F32), sds((2 * units, dim), F32)],
        [SMEM] + [VMEM] * 2,
    )


def make_body(devices, parts):
    axes = ("dp", "tensor")
    chips = devices // 2
    in_order = [1 << bit for bit in range(chips.bit_length() - 1)]
    turned = [in_order[1], in_order[0], *in_order[2:]]
    rounds = len(in_order)
    rounds_more = range(3, rounds)

    def pairs(move):
        found = []
        for device in range(devices):
            for part in range(parts):
                to_chip, to_core, to_part = move(device // 2, device % 2, part)
                source = device * parts + part
                found.append((source, (to_chip * 2 + to_core) * parts + to_part))
        return found

    def by_bit(bit):
        return pairs(
            lambda chip, core, part: (chip ^ (turned if core else in_order)[bit], core, part)
        )

    swapped = [
        pair
        for pair in pairs(lambda chip, core, part: (chip, part, core))
        if pair[0] != pair[1]
    ]
    by_core = pairs(lambda chip, core, part: (chip, 1 - core, part))
    by_part = pairs(lambda chip, core, part: (chip, core, 1 - part))
    from_first_part = [pair for pair in by_part if pair[0] % parts == 0]
    by_chip = [by_bit(bit) for bit in range(rounds)]

    def by_quarter(partner):
        def across(chip, core, part):
            for bit in range(2):
                if partner >> (1 - bit) & 1:
                    chip ^= (turned if core else in_order)[bit]
            return chip, core, part

        return pairs(across)

    def move(value, how):
        return lax.ppermute(value, axes, how)

    def add_more(value):
        for bit in rounds_more:
            other = move(value, by_chip[bit])
            value = (value.astype(F32) + other.astype(F32)).astype(value.dtype)
        return value

    def exchange(values):
        return [values[0]] + [move(values[i], by_quarter(i)) for i in range(1, 4)]

    def body(
        tokens,
        segment_ids,
        pad_mask,
        norm1_gain,
        norm1_shift,
        w_query,
        w_key,
        w_value,
        w_out,
        norm2_gain,
        norm2_shift,
        w_up,
        w_down,
        cotangent,
    ):
        order = Order()
        device = lax.axis_index("dp")
        part = lax.axis_index("tensor")
        core = device % 2
        chip = device // 2
        bits = [
            jnp.where(core == 1, (chip & turned[i]) != 0, (chip & in_order[i]) != 0)
            for i in range(rounds)
        ]
        place = jnp.stack([core, part] + bits).astype(jnp.int32)
        gain1, shift1, gain2, shift2 = (
            vector[None, :] for vector in (norm1_gain, norm1_shift, norm2_gain, norm2_shift)
        )

        moved = move(tokens, swapped)
        ints = jnp.concatenate([segment_ids, pad_mask], axis=0)
        ints = jnp.where(core == part, ints, move(ints, by_core)).astype(F32)
        seg_pad = jnp.concatenate([ints, jnp.zeros((6, ints.shape[1]), F32)], axis=0)

        qkv_l, qkv_s, first = pack_first_call(order, place, w_query, w_key, w_value)
        first_moved = move(first, from_first_part)
        qkv_near = move(qkv_s, by_part)
        mine, n1_own = norm1_call(order, place, tokens, moved, gain1, shift1)
        n1_other = move(n1_own, by_core)
        out_l, up_l, up_s, down_l, down_s, grad = pack_last_call(
            order, place, w_out, w_up, w_down, cotangent
        )
        out_r = move(out_l, by_part)
        up_near = move(up_s, by_part)
        grad_moved = move(grad, swapped)
        down_near = move(down_s, by_part)
        n1, penalty, qk0, first = penalty_call(
            order, place, n1_own, n1_other, first, first_moved, seg_pad
        )
        (qkv_near,) = order.hold((qkv_near,), (penalty,))
        qkv_far = move(qkv_near, by_chip[0])
        qkvt_l, heads_l, lse_l = forward_call(order, n1, (qkv_l,), penalty)
        qkvt_r, heads_r, lse_r, qkv_r, own, send = forward_call(
            order,
            n1,
            (qkv_near, qkv_far),
            penalty,
            place,
            (heads_l, out_l, out_r),
            (up_near,),
        )
        (send,) = order.hold((send,), (down_near,))
        (mine,) = order.hold((mine,), (send,), 5)
        hidden, n2_own = norm2_call(order, mine, own, move(send, by_core), gain2, shift2)
        n2_other = move(n2_own, by_core)
        up_near, down_near = order.hold((up_near, down_near), (mine,))
        up_far = move(up_near, by_chip[0])
        down_far = move(down_near, by_chip[0])
        (grad_moved,) = order.hold((grad_moved,), (n2_own,))
        grad_own = jnp.where(core == part, grad, grad_moved)
        grad_other = move(grad_own, by_core)
        (up_l,) = order.hold((up_l,), (n2_own,), 5)
        *before, keep, send = mlp_call(
            order, place, n2_other, n2_own, grad_other, grad_own, (up_l, down_l)
        )
        got = move(send, by_chip[0])
        weights = (up_near, up_far, down_near, down_far)
        mixed_send, mixed_own, back_send, back_own, *ff_r = mlp_call(
            order, place, n2_other, n2_own, grad_other, grad_own, weights, before
        )
        back_send, *ff_r = order.hold((back_send, *ff_r), (got,))
        ff_r = exchange(ff_r)
        grad_hidden, low_own, sums2 = norm2_back_call(
            order, hidden, back_own, move(back_send, by_core), grad_own, gain2
        )
        low_other = move(low_own, by_core)
        keep, send = half_sums_call(order, place, keep, got)
        got = move(send, by_chip[1])

        low = (low_own, low_other)
        grads_r, wo_r, logit_sum = backward_call(
            order, place, *low, out_r, heads_r, qkvt_r, lse_r, penalty
        )
        at_r = weights_first_call(order, place, n1, grads_r, wo_r)
        ff, ff_move = first_sums_call(order, (keep, got), ff_r)
        ff_got = move(ff_move, by_part)
        at_r = exchange(at_r)
        grads_l, wo_l, logit_sum = backward_call(
            order, place, *low, out_l, heads_l, qkvt_l, lse_l, penalty, logit_sum
        )
        logit_got = move(logit_sum, by_core)
        at_r, ff, *at = weights_second_call(
            order, place, n1, grads_l, wo_l, at_r, (ff, ff_got)
        )
        at_r = move(at_r, by_part)
        ff_got = move(ff, by_chip[2])
        at = exchange(at)
        own, send, late = norm1_grad_call(
            order,
            place,
            (logit_sum, logit_got),
            qk0,
            seg_pad,
            n1,
            grads_l,
            qkv_l,
            first,
            grads_r,
            qkv_r,
            gain1,
            shift1,
            sums2,
        )
        send, late = order.hold((send, late), (*at, at_r))
        received = move(send, by_core)
        late_got = move(late, by_part)
        ff = step0_call(order, (ff, ff_got))
        ff = exchange([add_more(ff)] * 4)
        both = step1_call(order, (late, late_got), (*at, at_r))
        size = at_r.shape[1]
        both_got = move(both, by_chip[2])
        results = results_call(
            order,
            mine,
            own,
            received,
            grad_hidden,
            gain1,
            hidden,
            mixed_own,
            move(mixed_send, by_core),
        )
        (results,) = order.hold((results,), (both_got,))
        moved = move(results, swapped)
        both, ff = step2_call(order, place, size, both, both_got, ff)
        both = exchange([add_more(both)] * 4)
        ff_far = move(ff, by_core)
        up_grad, down_grad = finish_mlp_call(order, place, ff, ff_far)
        both = step3_call(order, place, size, both)
        both_far = move(both, by_core)
        mixed, tokens_grad = copy_call(order, place, results, moved)
        query_grad, key_grad, value_grad, out_grad, *norms = finish_attention_call(
            order, place, size, both, both_far
        )
        return (
            mixed,
            tokens_grad,
            norms[0],
            norms[1],
            query_grad,
            key_grad,
            value_grad,
            out_grad,
            norms[2],
            norms[3],
            up_grad,
            down_grad,
        )

    return body


def solution(mesh):
    in_specs = (
        P(("dp", "tensor"), None),
        P("dp", None),
        P("dp", None),
        P(),
        P(),
        P(None, "tensor"),
        P(None, "tensor"),
        P(None, "tensor"),
        P("tensor", None),
        P(),
        P(),
        P(None, "tensor"),
        P("tensor", None),
        P(("dp", "tensor"), None),
    )
    out_specs = (
        P(("dp", "tensor"), None),
        P(("dp", "tensor"), None),
        P(),
        P(),
        P(None, "tensor"),
        P(None, "tensor"),
        P(None, "tensor"),
        P("tensor", None),
        P(),
        P(),
        P(None, "tensor"),
        P("tensor", None),
    )
    body = make_body(mesh.shape["dp"], mesh.shape["tensor"])
    return jax.shard_map(body, mesh=mesh, in_specs=in_specs, out_specs=out_specs, check_vma=False)
```
